128 devices in a mesh: pool: 2 (over y_lo), tp: 4 (over x), dp: 16 (over y_hi, z, core).
Axes of the slice: x: 4, y: 4 (y_hi: 2, y_lo: 2; y = y_hi * 2 + y_lo), z: 4, core: 2. Of those that a mesh axis runs over, the one named last changes fastest.
Arguments:
- x_in: bfloat16 [2, 4096, 16384], P('pool', 'dp', 'tp'), may hold values from -6 to 6
- bc_in: bfloat16 [2, 4096, 2, 2048], P('pool', 'dp', None, 'tp'), may hold values from -1.5 to 1.5
- dt_raw: bfloat16 [2, 4096, 256], P('pool', 'dp', 'tp'), may hold values from -5 to 9
- conv_w_x: bfloat16 [4, 16384], P(None, 'tp'), may hold values from -3 to 3
- conv_b_x: float32 [16384], P('tp'), may hold values from -3 to 3
- conv_w_bc: bfloat16 [4, 2, 2048], P(None, None, 'tp'), may hold values from -3 to 3
- conv_b_bc: float32 [2, 2048], P(None, 'tp'), may hold values from -0.6 to 0.6
- dt_bias: float32 [256], P('tp'), may hold values from -1 to 1
- a_log: float32 [256], P('tp'), may hold values from -12 to 0
- d_skip: float32 [256], P('tp'), may hold values from 0.5 to 1.5
- lengths: int32 [2, 3], P('pool'), may hold values from 1 to 2048, 4096 in all within a row
- decode_prompt: int32 [2, 16, 4], P('pool', 'dp'), may hold values from 0 to 2
- dec_x: bfloat16 [2, 16, 4, 4, 16384], P('pool', 'dp', None, None, 'tp'), may hold values from -6 to 6
- dec_bc: bfloat16 [2, 16, 4, 4, 2, 2048], P('pool', 'dp', None, None, None, 'tp'), may hold values from -1.5 to 1.5
- dec_dt: bfloat16 [2, 16, 4, 4, 256], P('pool', 'dp', None, None, 'tp'), may hold values from -4 to 4
Outputs:
- prefill_out: bfloat16 [2, 4096, 16384], P('pool', 'dp', 'tp')
- decode_out: bfloat16 [2, 16, 4, 4, 16384], P('pool', 'dp', None, None, 'tp')
The draws below stay inside these ranges and needn't reach their ends.
Inputs may be any that keep to these rules, and one draw needn't show every extreme that they name: `lengths`: the 3 prompts of a half fill its stream of 4096 tokens exactly; the longest has exactly 2048 tokens. `decode_prompt`: A prompt number of the other half; a prompt may be continued by several rows or by none.
All inputs are finite; a program needn't handle non-finite values.
Results may differ from the reference program's by a relative error of at most 0.0051.
Values may be sent and summed in bfloat16 or wider, within the bound.
No kernel may reach another device: no remote copies, remote signals or barrier semaphores. Data moves between devices by JAX's collectives and lax.ppermute only.
A program may use at most 256 MiB of HBM per device.

```python
import math
import jax
import jax.numpy as jnp
import numpy as np
from jax import lax

D_INNER = 16384
HEADS = 256
HEAD_DIM = 64
GROUPS = 8
STATE = 256
CONV = 4
BLOCK_TOKENS = 128
PROMPTS = 3
ROWS_DEC = 4
STEPS = 4
PACKED_TOKENS = 4096
MOST = 2048
N_DP = 16


def head_rates(key, slow_share):
    shared_key = jax.random.fold_in(key, 101)
    key_pick, key_slow, key_middle, key_quick = jax.random.split(shared_key, 4)
    pick_values = jax.random.uniform(key_pick, (HEADS,), jnp.float32)
    slow_values = math.log(0.3 / PACKED_TOKENS) + jax.random.uniform(key_slow, (HEADS,), jnp.float32) * math.log(3.0)
    middle_values = jax.random.uniform(key_middle, (HEADS,), jnp.float32, math.log(0.9 / PACKED_TOKENS), math.log(0.7))
    quick_values = jax.random.uniform(key_quick, (HEADS,), jnp.float32, math.log(0.7), 0.0)
    rapid_heads = pick_values > 0.94
    values = jnp.where(pick_values < slow_share, slow_values, jnp.where(rapid_heads, quick_values, middle_values))
    return (values, rapid_heads)


def draw_dt_raw(key, part):
    slow_share = 0.5
    unused_values, rapid_heads = head_rates(key, slow_share)
    key = jax.random.fold_in(key, 11)
    key_floor_level, key_peak, key_lift, block_key_seed, key_shift_amount, key_surge = jax.random.split(key, 6)
    complete_shape = (2, PACKED_TOKENS, HEADS)
    baseline_values = jnp.clip(jax.random.normal(key_floor_level, complete_shape, jnp.float32) * 0.8 - 1.0, -5.0, 3.0)
    spike_rows = jax.random.uniform(key_peak, (2, PACKED_TOKENS, 1), jnp.float32) < 4.0 / PACKED_TOKENS
    raised_values = jax.random.uniform(key_lift, complete_shape, jnp.float32, 3.0, 6.0)
    peaked_values = jnp.where(spike_rows, baseline_values + raised_values, baseline_values)
    block_pick = jax.random.randint(block_key_seed, (2, 1, 1), 0, PACKED_TOKENS // BLOCK_TOKENS)
    offset_pick = jax.random.randint(key_shift_amount, (2, 1, 1), 0, max(BLOCK_TOKENS // 8, 1))
    leading_row = block_pick * BLOCK_TOKENS + BLOCK_TOKENS // 2 + offset_pick
    index_of_row = jnp.arange(PACKED_TOKENS, dtype=jnp.int32)[None, :, None]
    inside_surge = (index_of_row >= leading_row) & (index_of_row < leading_row + BLOCK_TOKENS * 3 // 8) & rapid_heads[None, None, :]
    surge_values = jax.random.uniform(key_surge, complete_shape, jnp.float32, 4.5, 5.5)
    return jnp.where(inside_surge, surge_values, peaked_values).astype(jnp.bfloat16)


def draw_a_log(key, part):
    slow_share = 0.5
    values, unused_heads = head_rates(key, slow_share)
    return values.astype(jnp.float32)


def touch_ends(array, key, smallest, largest):
    shape = array.shape
    spot = [jax.random.randint(jax.random.fold_in(key, axis), (), 0, shape[axis]) for axis in range(len(shape))]
    array = array.at[tuple(spot)].set(smallest)
    longest = shape.index(max(shape))
    spot[longest] = (spot[longest] + 1) % shape[longest]
    return array.at[tuple(spot)].set(largest)


def shard_levels(stream_key, shape, shards, low, high):
    loudness = 1.0
    for position, shards_of in shards:
        steps = jax.random.uniform(jax.random.fold_in(jax.random.fold_in(stream_key, 6), position), (shards_of,), jnp.float32, low / len(shards), high / len(shards))
        loudness = loudness * jnp.repeat(jnp.exp(steps), shape[position] // shards_of).reshape((-1,) + (1,) * (len(shape) - 1 - position))
    return loudness


def length_profile(amount, total, most, lean):
    portions = [(1 << 20) // math.isqrt(standing ** lean) + 1 for standing in range(2, amount + 1)]
    spare, counts = total - most - (amount - 1), [1] * (amount - 1)
    while spare > 0:
        movable = [i for i in range(amount - 1) if counts[i] < most]
        whole, left = sum([portions[i] for i in movable]), spare
        for i in movable:
            more = min(most - counts[i], max(1, left * portions[i] // whole), spare)
            counts[i] = counts[i] + more
            spare = spare - more
    return np.array([most] + counts)


def ragged(rng, count, total, bound, lean):
    if count == 2:
        one = jax.random.randint(rng, (), max(1, total - bound), min(bound, total - 1) + 1)
        return jnp.stack([one, total - one])
    sizes = jnp.asarray(length_profile(count, total, bound, lean), jnp.int32)
    pairs = (count - 1) // 2
    giver, sink = sizes[1:1 + 2 * pairs:2], sizes[2:2 + 2 * pairs:2]
    room = jnp.minimum(giver - 1, bound - sink)
    passed = jax.random.randint(jax.random.fold_in(rng, 1), (pairs,), 0, 1 << 20) % (room + 1)
    sizes = sizes.at[1:1 + 2 * pairs:2].set(giver - passed).at[2:2 + 2 * pairs:2].set(sink + passed)
    return sizes[jax.random.permutation(jax.random.fold_in(rng, 2), count)]


def noise(own_key, dims, width, limit, shards=(), held_as=jnp.bfloat16):
    drawn = width * jax.random.normal(own_key, dims, jnp.float32)
    if shards:
        drawn = drawn * shard_levels(own_key, dims, shards, -0.22, 0.18)
    return jnp.clip(drawn, -limit, limit).astype(held_as)


def setup_inputs(seed: int = 0) -> dict:
    splits = jax.random.split(jax.random.key(seed), 16)
    return {
        "x_in": noise(splits[0], (2, PACKED_TOKENS, D_INNER), 1.0, 6.0, ((0, 2), (1, 16), (2, 4))),
        "bc_in": noise(splits[1], (2, PACKED_TOKENS, 2, GROUPS * STATE), 0.25, 1.5, ((0, 2), (1, 16), (3, 4))),
        "dt_raw": draw_dt_raw(jax.random.fold_in(splits[15], 71), 0),
        "conv_w_x": noise(splits[3], (CONV, D_INNER), CONV ** -0.5, 3.0, ((1, 4),)),
        "conv_b_x": noise(splits[4], (D_INNER,), 0.5, 3.0, ((0, 4),), jnp.float32),
        "conv_w_bc": noise(splits[5], (CONV, 2, GROUPS * STATE), CONV ** -0.5, 3.0, ((2, 4),)),
        "conv_b_bc": noise(splits[6], (2, GROUPS * STATE), 0.1, 0.6, ((1, 4),), jnp.float32),
        "dt_bias": jnp.clip(jax.random.uniform(splits[7], (HEADS,), jnp.float32, -1.0, 1.0) * shard_levels(splits[7], (HEADS,), ((0, 4),), -0.4, 0.0), -1.0, 1.0),
        "a_log": draw_a_log(jax.random.fold_in(splits[15], 71), 0),
        "d_skip": jnp.clip(0.5 + 1.0 * jax.random.uniform(splits[9], (HEADS,), jnp.float32) ** shard_levels(splits[9], (HEADS,), ((0, 4),), -0.2, 0.2), 0.5, 1.5),
        "lengths": jax.vmap(lambda own: ragged(own, PROMPTS, PACKED_TOKENS, MOST, 2))(jax.random.split(splits[10], 2)).reshape((2, PROMPTS)).astype(jnp.int32),
        "decode_prompt": touch_ends(jax.random.randint(splits[11], (2, N_DP, ROWS_DEC), 0, PROMPTS), jax.random.fold_in(splits[11], 1), 0, PROMPTS - 1).astype(jnp.int32),
        "dec_x": noise(splits[12], (2, N_DP, STEPS, ROWS_DEC, D_INNER), 1.0, 6.0, ((0, 2), (1, 16), (4, 4))),
        "dec_bc": noise(splits[13], (2, N_DP, STEPS, ROWS_DEC, 2, GROUPS * STATE), 0.25, 1.5, ((0, 2), (1, 16), (5, 4))),
        "dec_dt": noise(splits[14], (2, N_DP, STEPS, ROWS_DEC, HEADS), 1.0, 4.0, ((0, 2), (1, 16), (4, 4))),
    }


HIGHEST_PRECISION = lax.Precision.HIGHEST


def prompt_segments(lengths, positions):
    bounds = jnp.cumsum(lengths).astype(jnp.int32)
    segment = jnp.sum((positions[:, None] >= bounds[None, :]).astype(jnp.int32), axis=1).astype(jnp.int32)
    return jnp.where(positions < 0, -1, segment).astype(jnp.int32)


def conv_window(extended, segment, weight, offset):
    row_count = extended.shape[0] - (CONV - 1)
    own_segment = segment[CONV - 1:]
    running = jnp.broadcast_to(offset.astype(jnp.float32)[None, :], (row_count, extended.shape[1]))
    for tap_index in range(CONV):
        same_prompt = (segment[tap_index:tap_index + row_count] == own_segment)[:, None]
        term_value = weight[tap_index].astype(jnp.float32)[None, :] * extended[tap_index:tap_index + row_count].astype(jnp.float32)
        running = running + jnp.where(same_prompt, term_value, 0.0)
    return jax.nn.silu(running).astype(jnp.bfloat16)


def span_outputs(mixed_rows, b_rows, c_rows, log_decay, step_size, segment, previous, carry_state, skip_gain):
    span_len = mixed_rows.shape[0]
    cumulative = jnp.cumsum(log_decay, axis=0)
    positions = jnp.arange(span_len)
    causal = (positions[:, None] >= positions[None, :]) & (segment[:, None] == segment[None, :])
    across = jnp.moveaxis(cumulative, 0, -1)
    spread = across[:, :, :, None] - across[:, :, None, :]
    decay_mask = jnp.where(causal, jnp.exp(jnp.where(causal, spread, 0.0)), 0.0)
    scores = jnp.einsum('tgn,sgn->gts', c_rows.astype(jnp.float32), b_rows.astype(jnp.float32))
    weights = (scores[:, None] * decay_mask * jnp.moveaxis(step_size, 0, -1)[:, :, None, :]).astype(jnp.bfloat16)
    inner_part = jnp.einsum('gkts,sgkp->tgkp', weights.astype(jnp.float32), mixed_rows.astype(jnp.float32))
    carried = jnp.einsum('tgn,gkpn->tgkp', c_rows.astype(jnp.float32), carry_state, precision=HIGHEST_PRECISION)
    first_rows = (segment == previous)[:, None, None, None]
    outer_part = jnp.where(first_rows, jnp.exp(cumulative)[:, :, :, None] * carried, 0.0)
    return (inner_part + outer_part + skip_gain[None, :, :, None] * mixed_rows.astype(jnp.float32)).astype(jnp.bfloat16)


def end_state(carry_state, mixed_rows, b_rows, log_decay, step_size, segment, previous, target):
    span_len = mixed_rows.shape[0]
    cumulative = jnp.cumsum(log_decay, axis=0)
    positions = jnp.arange(span_len)
    final_sum = lax.dynamic_index_in_dim(cumulative, target, 0, keepdims=False)
    own_segment = lax.dynamic_index_in_dim(segment, target, 0, keepdims=False)
    chosen = ((positions <= target) & (segment == own_segment))[:, None, None]
    row_weight = jnp.where(chosen, jnp.exp(jnp.where(chosen, final_sum[None] - cumulative, 0.0)), 0.0) * step_size
    scaled = (mixed_rows.astype(jnp.float32) * row_weight[:, :, :, None]).astype(jnp.bfloat16)
    fresh_part = jnp.einsum('sgkp,sgn->gkpn', scaled.astype(jnp.float32), b_rows.astype(jnp.float32))
    keep_factor = jnp.where(own_segment == previous, jnp.exp(final_sum), 0.0)
    return keep_factor[:, :, None, None] * carry_state + fresh_part


def decode_conv(window_rows, weight, offset):
    running = jnp.broadcast_to(offset.astype(jnp.float32)[None, :], (window_rows.shape[0], window_rows.shape[2]))
    for tap_index in range(CONV):
        running = running + weight[tap_index].astype(jnp.float32)[None, :] * window_rows[:, tap_index].astype(jnp.float32)
    return jax.nn.silu(running).astype(jnp.bfloat16)


def decode_rows(carry_state, cache_x, cache_bc, new_x, new_bc, raw_step, conv_w_x, conv_b_x, weight_bc, offset_bc, dt_bias, group_rates, group_skip):
    row_total = carry_state.shape[0]
    group_count = carry_state.shape[1]
    per_group = carry_state.shape[2]
    results = []
    for step_index in range(STEPS):
        window_x = jnp.concatenate([cache_x, new_x[step_index][:, None]], axis=1)
        window_bc = jnp.concatenate([cache_bc, new_bc[step_index][:, None]], axis=1)
        mixed_rows = decode_conv(window_x, conv_w_x, conv_b_x)
        both_rows = decode_conv(window_bc, weight_bc, offset_bc).reshape(row_total, 2, group_count, STATE)
        step_size = jax.nn.softplus(raw_step[step_index].astype(jnp.float32) + dt_bias[None, :]).reshape(row_total, group_count, per_group)
        values = mixed_rows.reshape(row_total, group_count, per_group, HEAD_DIM).astype(jnp.float32)
        b_rows = both_rows[:, 0].astype(jnp.float32)
        c_rows = both_rows[:, 1].astype(jnp.float32)
        carry_state = jnp.exp(step_size * group_rates[None])[:, :, :, None, None] * carry_state + (step_size[:, :, :, None] * values)[:, :, :, :, None] * b_rows[:, :, None, None, :]
        readout = jnp.einsum('rgn,rgkpn->rgkp', c_rows, carry_state, precision=HIGHEST_PRECISION)
        results.append((readout + group_skip[None, :, :, None] * values).astype(jnp.bfloat16).reshape(row_total, -1))
        cache_x = window_x[:, 1:]
        cache_bc = window_bc[:, 1:]
    return jnp.stack(results)


def prefill_half(tokens, bc_rows, raw_step, lengths, conv_w_x, conv_b_x, weight_bc, offset_bc, dt_bias, group_rates, group_skip):
    per_group = HEADS // GROUPS
    width_bc = 2 * GROUPS * STATE
    rim_rows = CONV - 1
    segment_ext = prompt_segments(lengths, jnp.arange(-rim_rows, PACKED_TOKENS).astype(jnp.int32))
    padded_x = jnp.pad(tokens, ((rim_rows, 0), (0, 0)))
    padded_bc = jnp.pad(bc_rows.reshape(PACKED_TOKENS, width_bc), ((rim_rows, 0), (0, 0)))
    last_tokens = (jnp.cumsum(lengths) - 1).astype(jnp.int32)

    def span_inputs(span_index):
        begin_row = (span_index * BLOCK_TOKENS).astype(jnp.int32)
        seg_slice = lax.dynamic_slice_in_dim(segment_ext, begin_row, BLOCK_TOKENS + rim_rows, 0)
        mixed_rows = conv_window(lax.dynamic_slice_in_dim(padded_x, begin_row, BLOCK_TOKENS + rim_rows, 0), seg_slice, conv_w_x, conv_b_x)
        both_rows = conv_window(lax.dynamic_slice_in_dim(padded_bc, begin_row, BLOCK_TOKENS + rim_rows, 0), seg_slice, weight_bc, offset_bc).reshape(BLOCK_TOKENS, 2, GROUPS, STATE)
        step_size = jax.nn.softplus(lax.dynamic_slice_in_dim(raw_step, begin_row, BLOCK_TOKENS, 0).astype(jnp.float32) + dt_bias[None, :]).reshape(BLOCK_TOKENS, GROUPS, per_group)
        return (mixed_rows.reshape(BLOCK_TOKENS, GROUPS, per_group, HEAD_DIM), both_rows[:, 0], both_rows[:, 1], step_size * group_rates[None], step_size, seg_slice[rim_rows:], seg_slice[rim_rows - 1])

    def advance(carry, span_index):
        carry_state, start_states = carry
        mixed_rows, b_rows, c_rows, log_decay, step_size, segment, previous = span_inputs(span_index)
        output = span_outputs(mixed_rows, b_rows, c_rows, log_decay, step_size, segment, previous, carry_state, group_skip)
        here_mask = (last_tokens // BLOCK_TOKENS == span_index)[:, None, None, None, None]
        start_states = jnp.where(here_mask, carry_state[None], start_states)
        carry_state = end_state(carry_state, mixed_rows, b_rows, log_decay, step_size, segment, previous, BLOCK_TOKENS - 1)
        return (carry_state, start_states), output

    zero_state = jnp.zeros((GROUPS, per_group, HEAD_DIM, STATE), jnp.float32)
    zero_starts = jnp.zeros((PROMPTS, GROUPS, per_group, HEAD_DIM, STATE), jnp.float32)
    (unused_state, start_states), outputs = lax.scan(advance, (zero_state, zero_starts), jnp.arange(PACKED_TOKENS // BLOCK_TOKENS).astype(jnp.int32))
    finals, caches_x, caches_bc = [], [], []
    for prompt in range(PROMPTS):
        last_row = last_tokens[prompt]
        mixed_rows, b_rows, c_rows, log_decay, step_size, segment, previous = span_inputs(last_row // BLOCK_TOKENS)
        finals.append(end_state(start_states[prompt], mixed_rows, b_rows, log_decay, step_size, segment, previous, last_row % BLOCK_TOKENS))
        own_segment = lax.dynamic_index_in_dim(segment_ext, last_row + rim_rows, 0, keepdims=False)
        keep_rows = (lax.dynamic_slice_in_dim(segment_ext, last_row + 1, rim_rows, 0) == own_segment)[:, None]
        caches_x.append(jnp.where(keep_rows, lax.dynamic_slice_in_dim(padded_x, last_row + 1, rim_rows, 0), 0.0).astype(jnp.bfloat16))
        caches_bc.append(jnp.where(keep_rows, lax.dynamic_slice_in_dim(padded_bc, last_row + 1, rim_rows, 0), 0.0).astype(jnp.bfloat16))
    return outputs.reshape(PACKED_TOKENS, D_INNER), jnp.stack(finals), jnp.stack(caches_x), jnp.stack(caches_bc)


def reference(x_in, bc_in, dt_raw, conv_w_x, conv_b_x, conv_w_bc, conv_b_bc, dt_bias, a_log, d_skip, lengths, decode_prompt, dec_x, dec_bc, dec_dt):
    per_group = HEADS // GROUPS
    width_bc = 2 * GROUPS * STATE
    group_rates = (-jnp.exp(a_log)).reshape(GROUPS, per_group)
    group_skip = d_skip.reshape(GROUPS, per_group)
    weight_bc = conv_w_bc.reshape(CONV, width_bc)
    offset_bc = conv_b_bc.reshape(width_bc)
    halves = [prefill_half(x_in[half_index], bc_in[half_index], dt_raw[half_index], lengths[half_index], conv_w_x, conv_b_x, weight_bc, offset_bc, dt_bias, group_rates, group_skip) for half_index in range(2)]
    prefill_out = jnp.stack([halves[0][0], halves[1][0]])
    decoded = []
    for half_index in range(2):
        source = halves[1 - half_index]

        def one_device(device_inputs):
            chosen, new_x, new_bc, raw_step = device_inputs
            return decode_rows(source[1][chosen], source[2][chosen], source[3][chosen], new_x, new_bc.reshape(STEPS, ROWS_DEC, width_bc), raw_step, conv_w_x, conv_b_x, weight_bc, offset_bc, dt_bias, group_rates, group_skip)

        decoded.append(lax.map(one_device, (decode_prompt[half_index], dec_x[half_index], dec_bc[half_index], dec_dt[half_index])))
    return prefill_out, jnp.stack(decoded)
```

```python
import functools

import jax
import jax.numpy as jnp
from jax import lax
from jax.experimental import pallas as pl
from jax.experimental.pallas import tpu as pltpu
from jax.sharding import PartitionSpec as P

HEAD_DIM = 64
STATE = 256
CONV = 4
BLOCK = 128
PROMPTS = 3
STEPS = 4
ROWS = 4
CORES = 2
RING = 4
LANES = 128
REP = 32
CHIP_TOKENS = 512
BLOCKS = CHIP_TOKENS // BLOCK
GROUP_CH = 2048
CHUNK = GROUP_CH // RING
WIDE = GROUP_CH + 1024
LOG2E = 1.4426950408889634
F32 = jnp.float32
BF16 = jnp.bfloat16
VMEM = 56 * 1024 * 1024


def split3(value):
    high = value.astype(BF16).astype(F32)
    rest = value - high
    middle = rest.astype(BF16).astype(F32)
    return high, middle, rest - middle


def pack3(value):
    high, middle, low = split3(value)
    lane = lax.broadcasted_iota(jnp.int32, value.shape, 1)
    return jnp.where(lane < REP, high, jnp.where(lane < 2 * REP, middle, low)).astype(BF16)


def spread_matrix(chunk):
    lane = lax.broadcasted_iota(jnp.int32, (LANES, CHUNK), 0)
    head = lax.broadcasted_iota(jnp.int32, (LANES, CHUNK), 1) // HEAD_DIM + chunk * (CHUNK // HEAD_DIM)
    hit = ((lane & (REP - 1)) == head) & (lane < 3 * REP)
    return jnp.where(hit, 1.0, 0.0).astype(BF16)


def mm(a, b):
    return jnp.dot(a, b, preferred_element_type=F32)


def silu(value):
    half = 0.5 * value
    return half + half * jnp.tanh(half)


def softplus(value):
    return jnp.maximum(value, 0.0) + jnp.log1p(jnp.exp(-jnp.abs(value)))


def seg_vec(s_ref, pos):
    anchor, lo0, lo1 = s_ref[3], s_ref[4], s_ref[5]
    seg = (pos >= lo0).astype(jnp.int32) + (pos >= lo1).astype(jnp.int32)
    return jnp.where(pos < -anchor, -1, seg)


def seg_at(s_ref, pos):
    anchor, lo0, lo1 = s_ref[3], s_ref[4], s_ref[5]
    seg = jnp.where(pos >= lo0, 1, 0) + jnp.where(pos >= lo1, 1, 0)
    return jnp.where(pos + anchor < 0, -1, seg)


def rows_of(parts, count, width):
    row = lax.broadcasted_iota(jnp.int32, (count, width), 0)
    out = jnp.zeros((count, width), F32)
    for index, part in enumerate(parts):
        out = jnp.where(row == index, part, out)
    return out


def conv_rows(src, start, weight, offset, mask):
    lanes = offset.shape[1]
    running = jnp.broadcast_to(offset, (BLOCK, lanes))
    for tap in range(CONV):
        term = weight[tap : tap + 1] * src[pl.ds(5 + tap + start, BLOCK), :]
        if tap < CONV - 1:
            keep = mask[tap, pl.ds(start, BLOCK), :]
            term = term * jnp.concatenate([keep] * (lanes // LANES), axis=1)
        running = running + term
    return silu(running)


def cache_rows(s_ref, src, out):
    out[...] = jnp.zeros_like(out)
    for prompt in range(PROMPTS):
        last = (s_ref[4] - 1, s_ref[5] - 1, RING * CORES * CHIP_TOKENS - 1 - s_ref[3])[prompt]

        @pl.when((last >= 0) & (last < CHIP_TOKENS))
        def _():
            for tap in range(CONV - 1):
                row = last - (CONV - 2) + tap
                same = jnp.where(seg_at(s_ref, row) == seg_at(s_ref, last), 1.0, 0.0)
                value = src[pl.ds(row + 8, 1), :]
                out[pl.ds(prompt * 3 + tap, 1), :] = jnp.where(same > 0.5, value, 0.0)


def cut_of(s_ref):
    first, second = s_ref[4] - 1, s_ref[5] - 1
    limit = CHIP_TOKENS - 1
    one = jnp.where((second >= 0) & (second < limit), second, -1)
    return jnp.where((first >= 0) & (first < limit), first, one)


def kernel_a(
    s_ref, x_own, x_rec, halo_x, wx, bx, g_own, g_rec, halo_g, wg, bg, vecs,
    l0, l1, l2, l3, xc_out, bcc_out, dtc_out, wc3_out, cx_out, cg_out,
    xs, gs, mask, wp3, keep3, bt, cache,
):
    m = pl.program_id(0)
    core = s_ref[0]
    chunk = s_ref[1] ^ m
    first = core == 0
    half = CHIP_TOKENS // 2

    @pl.when(m == 0)
    def _():
        pos = lax.broadcasted_iota(jnp.int32, (CHIP_TOKENS, LANES), 0)
        own_seg = seg_vec(s_ref, pos)
        for tap in range(CONV - 1):
            mask[tap] = jnp.where(seg_vec(s_ref, pos - 3 + tap) == own_seg, 1.0, 0.0)
        gs[0:8] = halo_g[:, 0:512].astype(F32)
        gs[8 : 8 + half] = jnp.where(first, g_own[:, 0:512], g_rec[:, 0:512]).astype(F32)
        gs[8 + half :] = jnp.where(first, g_rec[:, 0:512], g_own[:, 0:512]).astype(F32)
        weight = wg[...].astype(F32)
        for j in range(BLOCKS):
            both = conv_rows(gs, j * BLOCK, weight, bg[...], mask).astype(BF16)
            bcc_out[pl.ds(j * BLOCK, BLOCK), :] = both
            bt[j] = both[:, 0:STATE].astype(F32).T.astype(BF16)
        cache_rows(s_ref, gs, cache)
        cg_out[...] = cache[...].astype(BF16)
        raw_a = jnp.where(first, g_own[:, 512:640], g_rec[:, 512:640]).astype(F32)
        raw_b = jnp.where(first, g_rec[:, 512:640], g_own[:, 512:640]).astype(F32)
        dt = softplus(jnp.concatenate([raw_a, raw_b], axis=0) + vecs[0:1])
        decay = dt * vecs[1:2]
        row = lax.broadcasted_iota(jnp.int32, (BLOCK, BLOCK), 0)
        col = lax.broadcasted_iota(jnp.int32, (BLOCK, BLOCK), 1)
        lower = jnp.where(row >= col, 1.0, 0.0).astype(BF16)
        dtc_out[0:CHIP_TOKENS] = dt
        total = jnp.zeros((1, LANES), F32)
        before = seg_at(s_ref, -1)
        keeps = []
        for j in range(BLOCKS):
            rows = slice(j * BLOCK, (j + 1) * BLOCK)
            high, middle, low = split3(decay[rows])
            cum = mm(lower, high.astype(BF16)) + mm(lower, middle.astype(BF16)) + mm(lower, low.astype(BF16))
            dtc_out[CHIP_TOKENS + j * BLOCK : CHIP_TOKENS + (j + 1) * BLOCK] = cum
            end = cum[BLOCK - 1 :]
            end_seg = seg_at(s_ref, (j + 1) * BLOCK - 1)
            weight_p = jnp.where(own_seg[rows] == end_seg, jnp.exp2(end - cum) * dt[rows], 0.0)
            wp3[pl.ds(j * BLOCK, BLOCK), :] = pack3(weight_p)
            reach = jnp.where(own_seg[rows] == before, jnp.exp2(total + cum), 0.0)
            wc3_out[pl.ds(j * BLOCK, BLOCK), :] = pack3(reach)
            keeps.append(jnp.where(seg_at(s_ref, j * BLOCK - 1) == end_seg, jnp.exp2(end), 0.0))
            total = total + end
        keeps.append(jnp.where(before == seg_at(s_ref, CHIP_TOKENS - 1), jnp.exp2(total), 0.0))
        keep3[...] = pack3(rows_of(keeps, 16, LANES))

    xs[0:8] = halo_x[...].astype(F32)
    xs[8 : 8 + half] = jnp.where(first, x_own[...], x_rec[...]).astype(F32)
    xs[8 + half :] = jnp.where(first, x_rec[...], x_own[...]).astype(F32)
    weight = wx[...].astype(F32)
    spread = spread_matrix(chunk)
    keep = mm(keep3[...], spread)
    state = None
    for j in range(BLOCKS):
        xc = conv_rows(xs, j * BLOCK, weight, bx[...], mask).astype(BF16)
        xc_out[pl.ds(j * BLOCK, BLOCK), :] = xc
        scaled = (xc.astype(F32) * mm(wp3[pl.ds(j * BLOCK, BLOCK), :], spread)).astype(BF16)
        fresh = mm(bt[j], scaled)
        state = fresh if j == 0 else keep[j : j + 1] * state + fresh
    cache_rows(s_ref, xs, cache)
    cx_out[...] = cache[...].astype(BF16)
    tail = rows_of(split3(keep[BLOCKS : BLOCKS + 1]), 16, CHUNK).astype(BF16)
    for index, out in enumerate((l0, l1, l2, l3)):

        @pl.when(m == index)
        def _():
            out[0:STATE] = state.astype(BF16)
            out[STATE:] = tail


def run_a(scalars, x_in, recv, halo, wx, bx, g_own, wg, bg, vecs):
    def fixed(shape):
        return pl.BlockSpec(shape, lambda m, s: (0,) * len(shape))

    def chunked(rows, per_core=0):
        return pl.BlockSpec((rows, CHUNK), lambda m, s: (0, s[0] * per_core + (s[1] ^ m)))

    half = CHIP_TOKENS // 2
    side = pl.BlockSpec((half, 1024), lambda m, s: (0, 2))
    return pl.pallas_call(
        kernel_a,
        grid_spec=pltpu.PrefetchScalarGridSpec(
            num_scalar_prefetch=1,
            grid=(RING,),
            in_specs=[
                chunked(half, RING), chunked(half), chunked(8), chunked(CONV, RING), chunked(1, RING),
                fixed((half, 1024)), side, pl.BlockSpec((8, 1024), lambda m, s: (0, 2)),
                fixed((CONV, 512)), fixed((1, 512)), fixed((8, LANES)),
            ],
            out_specs=[fixed((STATE + 16, CHUNK))] * RING + [
                chunked(CHIP_TOKENS), fixed((CHIP_TOKENS, 512)), fixed((2 * CHIP_TOKENS, LANES)),
                fixed((CHIP_TOKENS, LANES)), chunked(16), fixed((16, 512)),
            ],
            scratch_shapes=[
                pltpu.VMEM((CHIP_TOKENS + 8, CHUNK), F32),
                pltpu.VMEM((CHIP_TOKENS + 8, 512), F32),
                pltpu.VMEM((CONV - 1, CHIP_TOKENS, LANES), F32),
                pltpu.VMEM((CHIP_TOKENS, LANES), BF16),
                pltpu.VMEM((16, LANES), BF16),
                pltpu.VMEM((BLOCKS, STATE, BLOCK), BF16),
                pltpu.VMEM((16, CHUNK), F32),
            ],
        ),
        out_shape=[jax.ShapeDtypeStruct((STATE + 16, CHUNK), BF16)] * RING + [
            jax.ShapeDtypeStruct((CHIP_TOKENS, GROUP_CH), BF16),
            jax.ShapeDtypeStruct((CHIP_TOKENS, 512), BF16),
            jax.ShapeDtypeStruct((2 * CHIP_TOKENS, LANES), F32),
            jax.ShapeDtypeStruct((CHIP_TOKENS, LANES), BF16),
            jax.ShapeDtypeStruct((16, GROUP_CH), BF16),
            jax.ShapeDtypeStruct((16, 512), BF16),
        ],
        compiler_params=pltpu.CompilerParams(vmem_limit_bytes=VMEM),
        cost_estimate=pl.CostEstimate(flops=6 * 10**9, bytes_accessed=8 * 10**6, transcendentals=10**6),
        name="conv_and_states",
    )(scalars, x_in, recv, halo, wx, bx, g_own, recv, halo, wg, bg, vecs)


def kernel_b(
    s_ref, xc_ref, bcc, dtc, skip, cx, cg,
    f0, f1, f2, f3, local_out,
    wp3, wb3, keep3, bt, gm, cum_t, dt_t, wf3,
):
    m = pl.program_id(0)
    chunk = s_ref[1] ^ m
    cut = cut_of(s_ref)
    cut_block = cut // BLOCK

    @pl.when(m == 0)
    def _():
        pos = lax.broadcasted_iota(jnp.int32, (BLOCK, LANES), 0)
        row = lax.broadcasted_iota(jnp.int32, (BLOCK, BLOCK), 0)
        col = lax.broadcasted_iota(jnp.int32, (BLOCK, BLOCK), 1)
        total = jnp.zeros((1, LANES), F32)
        before = seg_at(s_ref, -1)
        keeps = []
        cut_keep = jnp.zeros((1, LANES), F32)
        cut_reach = jnp.zeros((1, LANES), F32)
        cut_row = dtc[pl.ds(CHIP_TOKENS + jnp.maximum(cut, 0), 1), :]
        cut_seg = seg_at(s_ref, cut)
        wf3[...] = jnp.zeros_like(wf3)
        for j in range(BLOCKS):
            dt = dtc[j * BLOCK : (j + 1) * BLOCK]
            cum = dtc[CHIP_TOKENS + j * BLOCK : CHIP_TOKENS + (j + 1) * BLOCK]
            end = cum[BLOCK - 1 :]
            seg = seg_vec(s_ref, pos + j * BLOCK)
            end_seg = seg_at(s_ref, (j + 1) * BLOCK - 1)
            prev_seg = seg_at(s_ref, j * BLOCK - 1)
            wp3[pl.ds(j * BLOCK, BLOCK), :] = pack3(jnp.where(seg == end_seg, jnp.exp2(end - cum) * dt, 0.0))
            wb3[pl.ds(j * BLOCK, BLOCK), :] = pack3(jnp.where(seg == prev_seg, jnp.exp2(cum), 0.0))
            keeps.append(jnp.where(prev_seg == end_seg, jnp.exp2(end), 0.0))
            b_rows = bcc[pl.ds(j * BLOCK, BLOCK), 0:STATE]
            c_rows = bcc[pl.ds(j * BLOCK, BLOCK), STATE : 2 * STATE]
            b_t = b_rows.astype(F32).T.astype(BF16)
            bt[j] = b_t
            scores = mm(c_rows, b_t)
            same = seg_vec(s_ref, row + j * BLOCK) == seg_vec(s_ref, col + j * BLOCK)
            gm[j] = jnp.where((row >= col) & same, scores, 0.0)
            cum_t[j] = cum.T
            dt_t[j] = dt.T
            here = cut_block == j
            cut_keep = jnp.where(here & (cut_seg == prev_seg), jnp.exp2(cut_row), cut_keep)
            cut_reach = jnp.where(here & (cut_seg == before), jnp.exp2(total + cut_row), cut_reach)

            @pl.when((cut >= 0) & here)
            def _():
                chosen = (seg == cut_seg) & (pos + j * BLOCK <= cut)
                wf3[...] = pack3(jnp.where(chosen, jnp.exp2(jnp.minimum(cut_row - cum, 0.0)) * dt, 0.0))

            total = total + end
        keep3[...] = pack3(rows_of(keeps + [cut_keep, cut_reach], 16, LANES))

    spread = spread_matrix(chunk)
    keep = mm(keep3[...], spread)
    half_lane = lax.broadcasted_iota(jnp.int32, (BLOCK, LANES), 1) < HEAD_DIM
    outs = (f0, f1, f2, f3)
    for index, out in enumerate(outs):

        @pl.when(m == index)
        def _():
            out[0:STATE] = jnp.zeros((STATE, CHUNK), BF16)
            out[STATE : STATE + 16] = rows_of(split3(keep[BLOCKS + 1 : BLOCKS + 2]), 16, CHUNK).astype(BF16)
            out[STATE + 16 : STATE + 32] = cx[...]
            out[STATE + 32 : STATE + 48] = cg[...]

    state = None
    pairs = CHUNK // LANES
    for j in range(BLOCKS):
        rows = slice(j * BLOCK, (j + 1) * BLOCK)
        xc = xc_ref[rows]
        xf = xc.astype(F32)
        base = skip[...] * xf
        if j > 0:
            high = state.astype(BF16)
            low = (state - high.astype(F32)).astype(BF16)
            c_rows = bcc[rows, STATE : 2 * STATE]
            base = base + mm(wb3[rows], spread) * (mm(c_rows, high) + mm(c_rows, low))

        def cut_state(state, xf):
            scaled = (xf * mm(wf3[...], spread)).astype(BF16)
            fresh = mm(bt[j], scaled)
            if j > 0:
                fresh = keep[BLOCKS : BLOCKS + 1] * state + fresh
            for index, out in enumerate(outs):

                @pl.when(m == index)
                def _():
                    out[0:STATE] = fresh.astype(BF16)

        @pl.when((cut >= 0) & (cut_block == j))
        def _():
            cut_state(state, xf)

        if j < BLOCKS - 1:
            scaled = (xf * mm(wp3[rows], spread)).astype(BF16)
            fresh = mm(bt[j], scaled)
            state = fresh if j == 0 else keep[j : j + 1] * state + fresh
        cum = dtc[CHIP_TOKENS + j * BLOCK : CHIP_TOKENS + (j + 1) * BLOCK]
        heads = chunk * (CHUNK // HEAD_DIM)
        turned = pltpu.roll(cum, LANES - heads, 1)
        cum_rows = cum_t[j, pl.ds(pl.multiple_of(heads, 8), 8), :]
        dt_rows = dt_t[j, pl.ds(pl.multiple_of(heads, 8), 8), :]
        score = gm[j]
        for pair in range(pairs):
            weights = []
            for head in (2 * pair, 2 * pair + 1):
                gap = jnp.minimum(turned[:, head : head + 1] - cum_rows[head : head + 1], 0.0)
                weights.append((jnp.exp2(gap) * (score * dt_rows[head : head + 1])).astype(BF16))
            lanes = slice(pair * LANES, (pair + 1) * LANES)
            two = xc[:, lanes]
            zero = jnp.zeros_like(two)
            stacked = jnp.concatenate([jnp.where(half_lane, two, zero), jnp.where(half_lane, zero, two)], axis=0)
            inner = mm(jnp.concatenate(weights, axis=1), stacked)
            local_out[rows, lanes] = inner + base[:, lanes]


def run_b(scalars, xc, bcc, dtc, skip, cx, cg):
    def fixed(shape):
        return pl.BlockSpec(shape, lambda m, s: (0,) * len(shape))

    def chunked(rows, per_core=0):
        return pl.BlockSpec((rows, CHUNK), lambda m, s: (0, s[0] * per_core + (s[1] ^ m)))

    return pl.pallas_call(
        kernel_b,
        grid_spec=pltpu.PrefetchScalarGridSpec(
            num_scalar_prefetch=1,
            grid=(RING,),
            in_specs=[
                chunked(CHIP_TOKENS), fixed((CHIP_TOKENS, 512)), fixed((2 * CHIP_TOKENS, LANES)),
                chunked(1, RING), chunked(16), fixed((16, 512)),
            ],
            out_specs=[fixed((STATE + 48, CHUNK))] * RING + [chunked(CHIP_TOKENS)],
            scratch_shapes=[
                pltpu.VMEM((CHIP_TOKENS, LANES), BF16),
                pltpu.VMEM((CHIP_TOKENS, LANES), BF16),
                pltpu.VMEM((16, LANES), BF16),
                pltpu.VMEM((BLOCKS, STATE, BLOCK), BF16),
                pltpu.VMEM((BLOCKS, BLOCK, BLOCK), F32),
                pltpu.VMEM((BLOCKS, LANES, BLOCK), F32),
                pltpu.VMEM((BLOCKS, LANES, BLOCK), F32),
                pltpu.VMEM((BLOCK, LANES), BF16),
            ],
        ),
        out_shape=[jax.ShapeDtypeStruct((STATE + 48, CHUNK), BF16)] * RING
        + [jax.ShapeDtypeStruct((CHIP_TOKENS, GROUP_CH), F32)],
        compiler_params=pltpu.CompilerParams(vmem_limit_bytes=VMEM),
        cost_estimate=pl.CostEstimate(flops=12 * 10**9, bytes_accessed=8 * 10**6, transcendentals=2 * 10**6),
        name="output_within_chip",
    )(scalars, xc, bcc, dtc, skip, cx, cg)


def pick(refs, which, rows):
    out = refs[0][rows]
    for index in range(1, len(refs)):
        out = jnp.where(which == index, refs[index][rows], out)
    return out.astype(F32)


def decay_rows(tile):
    return tile[0:1] + tile[1:2] + tile[2:3]


def kernel_total(s_ref, l0, l1, l2, l3, total_out):
    state = jnp.zeros((STATE, CHUNK), F32)
    for chip in range(RING):
        which = s_ref[1] ^ chip
        part = pick((l0, l1, l2, l3), which, slice(0, STATE))
        factor = decay_rows(pick((l0, l1, l2, l3), which, slice(STATE, STATE + 16)))
        state = factor * state + part
    total_out[...] = state.astype(BF16)


def kernel_starts(s_ref, l0, l1, l2, l3, start, r0, r1, r2, r3):
    state = start[...].astype(F32)
    for chip in range(RING):
        which = s_ref[1] ^ chip
        for index, out in enumerate((r0, r1, r2, r3)):

            @pl.when(which == index)
            def _():
                out[...] = state.astype(BF16)

        if chip < RING - 1:
            part = pick((l0, l1, l2, l3), which, slice(0, STATE))
            factor = decay_rows(pick((l0, l1, l2, l3), which, slice(STATE, STATE + 16)))
            state = factor * state + part


def whole_call(kernel, out_shape, name, flops, scratch=()):
    def run(scalars, *args):
        return pl.pallas_call(
            kernel,
            in_specs=[pl.BlockSpec(memory_space=pltpu.SMEM)] + [pl.BlockSpec(memory_space=pltpu.VMEM)] * len(args),
            out_specs=jax.tree.map(lambda _: pl.BlockSpec(memory_space=pltpu.VMEM), out_shape),
            out_shape=out_shape,
            scratch_shapes=list(scratch),
            compiler_params=pltpu.CompilerParams(vmem_limit_bytes=VMEM),
            cost_estimate=pl.CostEstimate(flops=flops, bytes_accessed=3 * 10**6, transcendentals=0),
            name=name,
        )(scalars, *args)

    return run


def kernel_decode(
    s_ref, l0, l1, l2, l3, start, f0, f1, f2, f3, d0, d1, d2, d3,
    wx, bx, wg, bg, vecs, skip, bounds,
    keep_out, send_out,
    final, rows_f32, result,
):
    z, upper = s_ref[1], s_ref[2]
    ls, fs, ds = (l0, l1, l2, l3), (f0, f1, f2, f3), (d0, d1, d2, d3)
    lasts = [bounds[q] - 1 for q in range(PROMPTS)]
    final[...] = jnp.zeros_like(final)
    state = start[...].astype(F32)
    for chip in range(RING):
        which = z ^ chip
        origin = (upper * RING + chip) * CHIP_TOKENS
        part = pick(ls, which, slice(0, STATE))
        factor = decay_rows(pick(ls, which, slice(STATE, STATE + 16)))
        after = factor * state + part
        for q in range(PROMPTS):
            local = lasts[q] - origin

            @pl.when(local == CHIP_TOKENS - 1)
            def _():
                final[q] = after

            @pl.when((local >= 0) & (local < CHIP_TOKENS - 1))
            def _():
                fresh = pick(fs, which, slice(0, STATE))
                reach = decay_rows(pick(fs, which, slice(STATE, STATE + 16)))
                final[q] = fresh + reach * state

        state = after
    cache_x = sum(f[STATE + 16 : STATE + 32].astype(F32) for f in fs)
    cache_g = sum(f[STATE + 32 : STATE + 48].astype(F32) for f in fs)
    spread = spread_matrix(z)
    for index, d in enumerate(ds):
        rows_f32[index] = d[...].astype(F32)

    def step_rows(step, lanes):
        tiles = [
            rows_f32[index, 32 * side + 8 * step : 32 * side + 8 * step + 8, lanes]
            for index in range(RING)
            for side in range(2)
        ]
        return jnp.concatenate(tiles, axis=0)

    prompt = step_rows(0, slice(1024, 1152))[:, 96:97]
    chosen = [prompt == float(q) for q in range(PROMPTS)]
    mine = jnp.zeros_like(prompt)
    for q in range(PROMPTS):
        inside = jnp.where(lasts[q] // (RING * CHIP_TOKENS) == upper, 1.0, 0.0)
        mine = jnp.where(chosen[q], inside, mine)

    def window(cache, lanes):
        rows = []
        for tap in range(CONV - 1):
            row = jnp.zeros((STEPS * 16, CHUNK), F32)
            for q in range(PROMPTS):
                row = jnp.where(chosen[q], cache[3 * q + tap : 3 * q + tap + 1], row)
            rows.append(row)
        return rows + [step_rows(step, lanes) for step in range(STEPS)]

    def convolved(rows, weight, offset):
        out = []
        for step in range(STEPS):
            running = jnp.broadcast_to(offset, rows[0].shape)
            for tap in range(CONV):
                running = running + weight[tap : tap + 1] * rows[step + tap]
            out.append(silu(running).astype(BF16))
        return out

    mixed = convolved(window(cache_x, slice(0, 512)), wx[...].astype(F32), bx[...])
    both = convolved(window(cache_g, slice(512, 1024)), wg[...].astype(F32), bg[...])
    steps, fades = [], []
    fade = jnp.zeros((STEPS * 16, LANES), F32)
    for step in range(STEPS):
        dt = softplus(step_rows(step, slice(1024, 1152)) + vecs[0:1])
        fade = fade + dt * vecs[1:2]
        steps.append(dt)
        fades.append(fade)
    readers = jnp.concatenate([rows[:, STATE:] for rows in both], axis=0)
    readout = jnp.zeros((STEPS * STEPS * 16, CHUNK), F32)
    for q in range(PROMPTS):
        high = final[q].astype(BF16)
        low = (final[q] - high.astype(F32)).astype(BF16)
        value = mm(readers, high) + mm(readers, low)
        readout = jnp.where(jnp.concatenate([chosen[q]] * STEPS, axis=0), value, readout)
    for step in range(STEPS):
        mixed_now = mixed[step].astype(F32)
        total = readout[64 * step : 64 * step + 64] * mm(pack3(jnp.exp2(fades[step])), spread)
        total = total + skip[...] * mixed_now
        reader = both[step][:, STATE:].astype(F32)
        for past in range(step + 1):
            weight = steps[past]
            if past < step:
                weight = weight * jnp.exp2(fades[step] - fades[past])
            product = jnp.sum(reader * both[past][:, 0:STATE].astype(F32), axis=1, keepdims=True)
            total = total + mm(pack3(weight), spread) * (product * mixed[past].astype(F32))
        total = jnp.where(mine > 0.5, total, 0.0)
        for index in range(RING):
            for side in range(2):
                tile = total[8 * (2 * index + side) : 8 * (2 * index + side) + 8]
                result[index, 32 * side + 8 * step : 32 * side + 8 * step + 8, :] = tile
    for index in range(RING):
        keep_out[index] = result[index, pl.ds(pl.multiple_of(32 * upper, 32), 32), :].astype(BF16)
        send_out[index] = result[index, pl.ds(pl.multiple_of(32 * (1 - upper), 32), 32), :].astype(BF16)


def kernel_d(s_ref, local, c_rows, wc3, r0, r1, r2, r3, out):
    m = pl.program_id(0)
    spread = spread_matrix(s_ref[1] ^ m)
    factor = mm(wc3[...], spread)
    for index, r in enumerate((r0, r1, r2, r3)):

        @pl.when(m == index)
        def _():
            out[...] = (local[...] + factor * mm(c_rows[...], r[...])).astype(BF16)


def run_d(scalars, local, bcc, wc3, starts, own):
    half = CHIP_TOKENS // 2

    def row(s):
        return s[0] if own else 1 - s[0]

    return pl.pallas_call(
        kernel_d,
        grid_spec=pltpu.PrefetchScalarGridSpec(
            num_scalar_prefetch=1,
            grid=(RING,),
            in_specs=[
                pl.BlockSpec((half, CHUNK), lambda m, s: (row(s), s[1] ^ m)),
                pl.BlockSpec((half, STATE), lambda m, s: (row(s), 1)),
                pl.BlockSpec((half, LANES), lambda m, s: (row(s), 0)),
            ] + [pl.BlockSpec((STATE, CHUNK), lambda m, s: (0, 0))] * RING,
            out_specs=pl.BlockSpec((half, CHUNK), lambda m, s: (0, s[1] ^ m)),
        ),
        out_shape=jax.ShapeDtypeStruct((half, GROUP_CH), BF16),
        compiler_params=pltpu.CompilerParams(vmem_limit_bytes=VMEM),
        cost_estimate=pl.CostEstimate(flops=10**9, bytes_accessed=4 * 10**6, transcendentals=0),
        name="carried_own" if own else "carried_other",
    )(scalars, local, bcc, wc3, *starts)


def on_device(
    x_in, bc_in, dt_raw, conv_w_x, conv_b_x, conv_w_bc, conv_b_bc, dt_bias, a_log, d_skip,
    lengths, decode_prompt, dec_x, dec_bc, dec_dt,
):
    count = lax.axis_size("dp")
    place = lax.axis_index("dp")
    core = place % CORES
    z = (place // CORES) % RING
    upper = place // (CORES * RING)
    anchor = (place // CORES) * CHIP_TOKENS
    bounds = jnp.cumsum(lengths[0]).astype(jnp.int32)
    zero = jnp.int32(0)
    scalars = jnp.stack([core, z, upper, anchor, bounds[0] - anchor, bounds[1] - anchor, zero, zero]).astype(jnp.int32)
    both = ("pool", "dp")

    def group_part(x, bc, dt, group, extra=None):
        rows = x.shape[0]
        channels = lax.dynamic_slice_in_dim(x, group * GROUP_CH, GROUP_CH, 1)
        return jnp.concatenate([channels, group_side(bc, dt, group, extra)], axis=1).reshape(rows, WIDE)

    def group_side(bc, dt, group, extra=None):
        rows = bc.shape[0]
        b_c = lax.dynamic_slice_in_dim(bc, group * STATE, STATE, 2).reshape(rows, 2 * STATE)
        steps = lax.dynamic_slice_in_dim(dt, group * REP, REP, 1)
        last = jnp.zeros((rows, REP), BF16) if extra is None else jnp.broadcast_to(extra, (rows, REP))
        return jnp.concatenate([b_c, steps, steps, steps, last, jnp.zeros((rows, 384), BF16)], axis=1)

    tokens, bc_rows, dt_rows = x_in[0], bc_in[0], dt_raw[0]
    recv = lax.ppermute(
        group_part(tokens, bc_rows, dt_rows, 1 - core), "dp", [(i, i ^ 1) for i in range(count)]
    )
    rim = CONV - 1
    halo = None
    for group in range(CORES):
        rows = group_part(tokens[-rim:], bc_rows[-rim:], dt_rows[-rim:], group)
        rows = jnp.pad(rows, ((8 - rim, 0), (0, 0)))
        part = lax.ppermute(rows, "dp", [(i, i + 1 + group) for i in range(1, count - 1, 2)])
        halo = part if halo is None else halo + part

    dec_rows = STEPS * ROWS
    d_x = dec_x[0, 0].reshape(dec_rows, -1)
    d_bc = dec_bc[0, 0].reshape(dec_rows, 2, -1)
    d_dt = dec_dt[0, 0].reshape(dec_rows, -1)
    d_prompt = jnp.tile(decode_prompt[0, 0].astype(BF16), STEPS)[:, None]
    total = 2 * count
    same = lax.ppermute(
        group_part(d_x, d_bc, d_dt, core, d_prompt), both, [(i, (i + count) % total) for i in range(total)]
    )
    cross = lax.ppermute(
        group_part(d_x, d_bc, d_dt, 1 - core, d_prompt), both, [(i, ((i + count) % total) ^ 1) for i in range(total)]
    )
    pair = jnp.where(core == 0, jnp.stack([same, cross]), jnp.stack([cross, same]))
    pair = pair.reshape(CORES, STEPS, ROWS, WIDE).swapaxes(0, 1).reshape(CORES * dec_rows, WIDE)
    far = lax.ppermute(pair, "dp", [(i, i ^ (CORES * RING)) for i in range(count)])
    queries = jnp.where(upper == 0, jnp.concatenate([pair, far]), jnp.concatenate([far, pair]))

    def z_swap(value, m):
        if m == 0:
            return value
        return lax.ppermute(value, "dp", [(i, i ^ (CORES * m)) for i in range(count)])

    dec_parts = []
    for m in range(RING):
        channels = lax.dynamic_slice_in_dim(queries, (z ^ m) * CHUNK, CHUNK, 1)
        dec_parts.append(z_swap(jnp.concatenate([channels, queries[:, GROUP_CH : GROUP_CH + 640]], axis=1), m))

    w_group = lax.dynamic_slice_in_dim(conv_w_bc, core * STATE, STATE, 2).reshape(CONV, 2 * STATE)
    b_group = lax.dynamic_slice_in_dim(conv_b_bc, core * STATE, STATE, 1).reshape(1, 2 * STATE)
    rates = -LOG2E * jnp.exp(a_log)
    heads = jnp.stack([dt_bias, rates])
    heads = lax.dynamic_slice_in_dim(heads, core * REP, REP, 1)
    vecs = jnp.pad(jnp.tile(heads, (1, 3)), ((0, 6), (0, LANES - 3 * REP)))
    skip = jnp.repeat(d_skip, HEAD_DIM)[None]
    b_x = conv_b_x[None]
    g_own = group_side(bc_rows, dt_rows, core)

    *ls, xc, bcc, dtc, wc3, cx, cg = run_a(scalars, tokens, recv, halo, conv_w_x, b_x, g_own, w_group, b_group, vecs)
    ls = [z_swap(part, m) for m, part in enumerate(ls)]
    *fs, local = run_b(scalars, xc, bcc, dtc, skip, cx, cg)
    fs = [z_swap(part, m) for m, part in enumerate(fs)]

    state_shape = jax.ShapeDtypeStruct((STATE, CHUNK), BF16)
    half_total = whole_call(kernel_total, state_shape, "half_total", 10**6)(scalars, *ls)
    start = lax.ppermute(half_total, "dp", [(i, i + CORES * RING) for i in range(CORES * RING)])
    starts = whole_call(kernel_starts, [state_shape] * RING, "chip_starts", 10**6)(scalars, *ls, start)
    starts = [z_swap(part, m) for m, part in enumerate(starts)]

    def own_columns(value):
        return lax.dynamic_slice_in_dim(value, core * GROUP_CH + z * CHUNK, CHUNK, 1)

    def decode(bounds_ref_args):
        shape = jax.ShapeDtypeStruct((RING, 32, CHUNK), BF16)
        args = [*ls, start, *fs, *dec_parts, own_columns(conv_w_x), own_columns(b_x), w_group, b_group, vecs, own_columns(skip)]
        return pl.pallas_call(
            kernel_decode,
            in_specs=[pl.BlockSpec(memory_space=pltpu.SMEM)]
            + [pl.BlockSpec(memory_space=pltpu.VMEM)] * len(args)
            + [pl.BlockSpec(memory_space=pltpu.SMEM)],
            out_specs=[pl.BlockSpec(memory_space=pltpu.VMEM)] * 2,
            out_shape=[shape, shape],
            scratch_shapes=[
                pltpu.VMEM((PROMPTS, STATE, CHUNK), F32),
                pltpu.VMEM((RING, 64, 1152), F32),
                pltpu.VMEM((RING, 64, CHUNK), F32),
            ],
            compiler_params=pltpu.CompilerParams(vmem_limit_bytes=VMEM),
            cost_estimate=pl.CostEstimate(flops=4 * 10**9, bytes_accessed=6 * 10**6, transcendentals=0),
            name="decode_rows",
        )(scalars, *args, bounds_ref_args)

    kept, sent = decode(bounds)
    answers = kept + lax.ppermute(sent, "dp", [(i, i ^ (CORES * RING)) for i in range(count)])
    answers = jnp.stack([z_swap(answers[m], m) for m in range(RING)])
    answers = jnp.concatenate(
        [lax.dynamic_index_in_dim(answers, z ^ j, 0, keepdims=False) for j in range(RING)], axis=1
    )
    answers = answers.reshape(STEPS, CORES, ROWS, GROUP_CH)

    def answers_of(source):
        return lax.dynamic_index_in_dim(answers, source, 1, keepdims=False).reshape(dec_rows, GROUP_CH)

    same = lax.ppermute(answers_of(core), both, [(i, (i + count) % total) for i in range(total)])
    cross = lax.ppermute(answers_of(1 - core), both, [(i, ((i + count) % total) ^ 1) for i in range(total)])
    decoded = jnp.where(core == 0, jnp.concatenate([same, cross], axis=1), jnp.concatenate([cross, same], axis=1))

    other_rows = run_d(scalars, local, bcc, wc3, starts, False)
    other_group = lax.ppermute(other_rows, "dp", [(i, i ^ 1) for i in range(count)])
    own_group = run_d(scalars, local, bcc, wc3, starts, True)
    out = jnp.where(
        core == 0,
        jnp.concatenate([own_group, other_group], axis=1),
        jnp.concatenate([other_group, own_group], axis=1),
    )
    return out[None], decoded.reshape(dec_x.shape)


def solution(mesh):
    in_specs = (
        P("pool", "dp", "tp"),
        P("pool", "dp", None, "tp"),
        P("pool", "dp", "tp"),
        P(None, "tp"),
        P("tp"),
        P(None, None, "tp"),
        P(None, "tp"),
        P("tp"),
        P("tp"),
        P("tp"),
        P("pool", None),
        P("pool", "dp", None),
        P("pool", "dp", None, None, "tp"),
        P("pool", "dp", None, None, None, "tp"),
        P("pool", "dp", None, None, "tp"),
    )
    out_specs = (P("pool", "dp", "tp"), P("pool", "dp", None, None, "tp"))
    return jax.shard_map(on_device, mesh=mesh, in_specs=in_specs, out_specs=out_specs, check_vma=False)
```

```python
import functools

import jax
import jax.numpy as jnp
from jax import lax
from jax.experimental import pallas as pl
from jax.experimental.pallas import tpu as pltpu
from jax.sharding import PartitionSpec as P

HEAD_DIM = 64
STATE = 256
CONV = 4
BLOCK = 128
PROMPTS = 3
STEPS = 4
ROWS = 4
CORES = 2
RING = 4
LANES = 128
DEC = STATE + 48
MSG = DEC + 144
REP = 32
CHIP_TOKENS = 512
BLOCKS = CHIP_TOKENS // BLOCK
GROUP_CH = 2048
CHUNK = GROUP_CH // RING
WIDE = GROUP_CH + 1024
LOG2E = 1.4426950408889634
F32 = jnp.float32
BF16 = jnp.bfloat16
MIB = 1024 * 1024


def split3(value):
    high = value.astype(BF16).astype(F32)
    rest = value - high
    middle = rest.astype(BF16).astype(F32)
    return high, middle, rest - middle


def pack3(value):
    high, middle, low = split3(value)
    lane = lax.broadcasted_iota(jnp.int32, value.shape, 1)
    return jnp.where(lane < REP, high, jnp.where(lane < 2 * REP, middle, low)).astype(BF16)


def spread_matrix(chunk):
    lane = lax.broadcasted_iota(jnp.int32, (LANES, CHUNK), 0)
    head = (lax.broadcasted_iota(jnp.int32, (LANES, CHUNK), 1) >> 6) + chunk * (CHUNK // HEAD_DIM)
    hit = ((lane & (REP - 1)) == head) & (lane < 3 * REP)
    return jnp.where(hit, 1.0, 0.0).astype(BF16)


def in_hbm(value):
    return pltpu.with_memory_space_constraint(value, pltpu.HBM)


def mm(a, b):
    return jnp.dot(a, b, preferred_element_type=F32)


def silu(value):
    half = 0.5 * value
    return half + half * jnp.tanh(half)


def softplus(value):
    return jnp.maximum(value, 0.0) + jnp.log1p(jnp.exp(-jnp.abs(value)))


def seg_vec(s_ref, pos):
    anchor, lo0, lo1 = s_ref[3], s_ref[4], s_ref[5]
    seg = (pos >= lo0).astype(jnp.int32) + (pos >= lo1).astype(jnp.int32)
    return jnp.where(pos < -anchor, -1, seg)


def seg_at(s_ref, pos):
    anchor, lo0, lo1 = s_ref[3], s_ref[4], s_ref[5]
    seg = jnp.where(pos >= lo0, 1, 0) + jnp.where(pos >= lo1, 1, 0)
    return jnp.where(pos + anchor < 0, -1, seg)


def rows_of(parts, count, width):
    row = lax.broadcasted_iota(jnp.int32, (count, width), 0)
    out = jnp.zeros((count, width), F32)
    for index, part in enumerate(parts):
        out = jnp.where(row == index, part, out)
    return out


def conv_tile(src, start, lanes, weight, offset, mask):
    tile = src[pl.ds(start, BLOCK + 8), lanes]
    running = jnp.broadcast_to(offset[:, lanes], (BLOCK, LANES))
    for tap in range(CONV - 1):
        moved = pltpu.roll(tile, CONV - 1 - tap, 0)[8:]
        running = running + weight[tap : tap + 1, lanes] * (moved * mask[tap, pl.ds(start, BLOCK), :])
    return silu(running + weight[CONV - 1 : CONV, lanes] * tile[8:])


def cache_rows(s_ref, src, out):
    out[...] = jnp.zeros_like(out)
    for prompt in range(PROMPTS):
        last = (s_ref[4] - 1, s_ref[5] - 1, RING * CORES * CHIP_TOKENS - 1 - s_ref[3])[prompt]

        @pl.when((last >= 0) & (last < CHIP_TOKENS))
        def _():
            for tap in range(CONV - 1):
                row = last - (CONV - 2) + tap
                same = jnp.where(seg_at(s_ref, row) == seg_at(s_ref, last), 1.0, 0.0)
                value = src[pl.ds(row + 8, 1), :]
                out[pl.ds(prompt * 3 + tap, 1), :] = jnp.where(same > 0.5, value, 0.0)


def cut_of(s_ref):
    first, second = s_ref[4] - 1, s_ref[5] - 1
    limit = CHIP_TOKENS - 1
    one = jnp.where((second >= 0) & (second < limit), second, -1)
    return jnp.where((first >= 0) & (first < limit), first, one)


def kernel_a(
    s_ref, x_own, x_rec, halo_x, wx, bx, g_own, g_rec, halo_g, wg, bg, vecs,
    l0, l1, l2, l3, xc_out, bcc_out, dtc_out, wc3_out, cx_out, cg_out,
    xs, gs, mask, wp3, keep3, bt, cache, wide, scaled,
):
    m = pl.program_id(0)
    core = s_ref[0]
    chunk = s_ref[1] ^ m
    first = core == 0
    half = CHIP_TOKENS // 2

    @pl.when(m == 0)
    def _():
        pos = lax.broadcasted_iota(jnp.int32, (CHIP_TOKENS, LANES), 0)
        own_seg = seg_vec(s_ref, pos)
        for tap in range(CONV - 1):
            mask[tap] = jnp.where(seg_vec(s_ref, pos - 3 + tap) == own_seg, 1.0, 0.0)
        gs[0:8] = halo_g[:, 0:512].astype(F32)[8:]
        gs[8 : 8 + half] = jnp.where(first, g_own[:, 0:512], g_rec[:, 0:512]).astype(F32)
        gs[8 + half :] = jnp.where(first, g_rec[:, 0:512], g_own[:, 0:512]).astype(F32)
        weight = wg[...].astype(F32)
        for j in range(BLOCKS):
            for strip in range(4):
                lanes = slice(strip * LANES, (strip + 1) * LANES)
                tile = conv_tile(gs, j * BLOCK, lanes, weight, bg, mask).astype(BF16)
                bcc_out[pl.ds(j * BLOCK, BLOCK), lanes] = tile
                if strip < 2:
                    bt[j, lanes, :] = tile.astype(F32).T.astype(BF16)
        cache_rows(s_ref, gs, cache)
        cg_out[...] = cache[...].astype(BF16)
        raw_a = jnp.where(first, g_own[:, 512:640], g_rec[:, 512:640]).astype(F32)
        raw_b = jnp.where(first, g_rec[:, 512:640], g_own[:, 512:640]).astype(F32)
        dt = softplus(jnp.concatenate([raw_a, raw_b], axis=0) + vecs[0:1])
        decay = dt * vecs[1:2]
        row = lax.broadcasted_iota(jnp.int32, (BLOCK, BLOCK), 0)
        col = lax.broadcasted_iota(jnp.int32, (BLOCK, BLOCK), 1)
        lower = jnp.where(row >= col, 1.0, 0.0).astype(BF16)
        dtc_out[0:CHIP_TOKENS] = dt
        total = jnp.zeros((1, LANES), F32)
        before = seg_at(s_ref, -1)
        keeps = []
        for j in range(BLOCKS):
            rows = slice(j * BLOCK, (j + 1) * BLOCK)
            high, middle, low = split3(decay[rows])
            cum = mm(lower, high.astype(BF16)) + mm(lower, middle.astype(BF16)) + mm(lower, low.astype(BF16))
            dtc_out[CHIP_TOKENS + j * BLOCK : CHIP_TOKENS + (j + 1) * BLOCK] = cum
            end = cum[BLOCK - 1 :]
            end_seg = seg_at(s_ref, (j + 1) * BLOCK - 1)
            weight_p = jnp.where(own_seg[rows] == end_seg, jnp.exp2(end - cum) * dt[rows], 0.0)
            wp3[pl.ds(j * BLOCK, BLOCK), :] = pack3(weight_p)
            reach = jnp.where(own_seg[rows] == before, jnp.exp2(total + cum), 0.0)
            wc3_out[pl.ds(j * BLOCK, BLOCK), :] = pack3(reach)
            keeps.append(jnp.where(seg_at(s_ref, j * BLOCK - 1) == end_seg, jnp.exp2(end), 0.0))
            total = total + end
        keeps.append(jnp.where(before == seg_at(s_ref, CHIP_TOKENS - 1), jnp.exp2(total), 0.0))
        keep3[...] = pack3(rows_of(keeps, 16, LANES))

    xs[0:8] = halo_x[...].astype(F32)[8:]
    xs[8 : 8 + half] = jnp.where(first, x_own[...], x_rec[...]).astype(F32)
    xs[8 + half :] = jnp.where(first, x_rec[...], x_own[...]).astype(F32)
    weight = wx[...].astype(F32)
    spread = spread_matrix(chunk)
    keep = mm(keep3[...], spread)
    for j in range(BLOCKS):
        rows = pl.ds(j * BLOCK, BLOCK)
        wide[...] = mm(wp3[rows, :], spread)
        for strip in range(CHUNK // LANES):
            lanes = slice(strip * LANES, (strip + 1) * LANES)
            xc = conv_tile(xs, j * BLOCK, lanes, weight, bx, mask).astype(BF16)
            xc_out[rows, lanes] = xc
            scaled[rows, lanes] = (xc.astype(F32) * wide[:, lanes]).astype(BF16)
    state = mm(bt[0], scaled[0:BLOCK, :])
    for j in range(1, BLOCKS):
        state = keep[j : j + 1] * state + mm(bt[j], scaled[pl.ds(j * BLOCK, BLOCK), :])
    cache_rows(s_ref, xs, cache)
    cx_out[...] = cache[...].astype(BF16)
    tail = rows_of(split3(keep[BLOCKS : BLOCKS + 1]), 16, CHUNK).astype(BF16)
    for index, out in enumerate((l0, l1, l2, l3)):

        @pl.when(m == index)
        def _():
            out[0:STATE] = state.astype(BF16)
            out[STATE:] = tail


def run_a(scalars, x_in, recv, halo, wx, bx, g_own, wg, bg, vecs):
    def fixed(shape):
        return pl.BlockSpec(shape, lambda m, s: (0,) * len(shape))

    def chunked(rows, per_core=0):
        return pl.BlockSpec((rows, CHUNK), lambda m, s: (0, s[0] * per_core + (s[1] ^ m)))

    half = CHIP_TOKENS // 2
    side = pl.BlockSpec((half, 1024), lambda m, s: (0, 2))
    return pl.pallas_call(
        kernel_a,
        grid_spec=pltpu.PrefetchScalarGridSpec(
            num_scalar_prefetch=1,
            grid=(RING,),
            in_specs=[
                chunked(half, RING), chunked(half), chunked(16), chunked(CONV, RING), chunked(1, RING),
                fixed((half, 1024)), side, pl.BlockSpec((16, 1024), lambda m, s: (0, 2)),
                fixed((CONV, 512)), fixed((1, 512)), fixed((8, LANES)),
            ],
            out_specs=[fixed((STATE + 16, CHUNK))] * RING + [
                chunked(CHIP_TOKENS), fixed((CHIP_TOKENS, 512)), fixed((2 * CHIP_TOKENS, LANES)),
                fixed((CHIP_TOKENS, LANES)), chunked(16), fixed((16, 512)),
            ],
            scratch_shapes=[
                pltpu.VMEM((CHIP_TOKENS + 8, CHUNK), F32),
                pltpu.VMEM((CHIP_TOKENS + 8, 512), F32),
                pltpu.VMEM((CONV - 1, CHIP_TOKENS, LANES), F32),
                pltpu.VMEM((CHIP_TOKENS, LANES), BF16),
                pltpu.VMEM((16, LANES), BF16),
                pltpu.VMEM((BLOCKS, STATE, BLOCK), BF16),
                pltpu.VMEM((16, CHUNK), F32),
                pltpu.VMEM((BLOCK, CHUNK), F32),
                pltpu.VMEM((CHIP_TOKENS, CHUNK), BF16),
            ],
        ),
        out_shape=[jax.ShapeDtypeStruct((STATE + 16, CHUNK), BF16)] * RING + [
            jax.ShapeDtypeStruct((CHIP_TOKENS, GROUP_CH), BF16),
            jax.ShapeDtypeStruct((CHIP_TOKENS, 512), BF16),
            jax.ShapeDtypeStruct((2 * CHIP_TOKENS, LANES), F32),
            jax.ShapeDtypeStruct((CHIP_TOKENS, LANES), BF16),
            jax.ShapeDtypeStruct((16, GROUP_CH), BF16),
            jax.ShapeDtypeStruct((16, 512), BF16),
        ],
        compiler_params=pltpu.CompilerParams(vmem_limit_bytes=16 * MIB),
        cost_estimate=pl.CostEstimate(flops=6 * 10**9, bytes_accessed=8 * 10**6, transcendentals=10**6),
        name="conv_and_states",
    )(scalars, x_in, recv, halo, wx, bx, g_own, recv, halo, wg, bg, vecs)


def kernel_b(
    s_ref, xc_ref, bcc, dtc, skip, cx, cg, near_same, near_cross, far_same, far_cross,
    f0, f1, f2, f3, local_out,
    wp3, wb3, keep3, bt, gm, cum_t, dt_t, wf3, wide, reach, carried, scaled, parts, dec_rows,
):
    m = pl.program_id(0)
    chunk = s_ref[1] ^ m
    cut = cut_of(s_ref)
    cut_block = cut // BLOCK

    @pl.when(m == 0)
    def _():
        pos = lax.broadcasted_iota(jnp.int32, (BLOCK, LANES), 0)
        row = lax.broadcasted_iota(jnp.int32, (BLOCK, BLOCK), 0)
        col = lax.broadcasted_iota(jnp.int32, (BLOCK, BLOCK), 1)
        total = jnp.zeros((1, LANES), F32)
        before = seg_at(s_ref, -1)
        keeps = []
        cut_keep = jnp.zeros((1, LANES), F32)
        cut_reach = jnp.zeros((1, LANES), F32)
        cut_row = dtc[pl.ds(CHIP_TOKENS + jnp.maximum(cut, 0), 1), :]
        cut_seg = seg_at(s_ref, cut)
        wf3[...] = jnp.zeros_like(wf3)
        for j in range(BLOCKS):
            dt = dtc[j * BLOCK : (j + 1) * BLOCK]
            cum = dtc[CHIP_TOKENS + j * BLOCK : CHIP_TOKENS + (j + 1) * BLOCK]
            end = cum[BLOCK - 1 :]
            seg = seg_vec(s_ref, pos + j * BLOCK)
            end_seg = seg_at(s_ref, (j + 1) * BLOCK - 1)
            prev_seg = seg_at(s_ref, j * BLOCK - 1)
            wp3[pl.ds(j * BLOCK, BLOCK), :] = pack3(jnp.where(seg == end_seg, jnp.exp2(end - cum) * dt, 0.0))
            wb3[pl.ds(j * BLOCK, BLOCK), :] = pack3(jnp.where(seg == prev_seg, jnp.exp2(cum), 0.0))
            keeps.append(jnp.where(prev_seg == end_seg, jnp.exp2(end), 0.0))
            b_rows = bcc[pl.ds(j * BLOCK, BLOCK), 0:STATE]
            c_rows = bcc[pl.ds(j * BLOCK, BLOCK), STATE : 2 * STATE]
            b_t = b_rows.astype(F32).T.astype(BF16)
            bt[j] = b_t
            scores = mm(c_rows, b_t)
            same = seg_vec(s_ref, row + j * BLOCK) == seg_vec(s_ref, col + j * BLOCK)
            gm[j] = jnp.where((row >= col) & same, scores, 0.0)
            cum_t[j] = cum.T
            dt_t[j] = dt.T
            here = cut_block == j
            cut_keep = jnp.where(here & (cut_seg == prev_seg), jnp.exp2(cut_row), cut_keep)
            cut_reach = jnp.where(here & (cut_seg == before), jnp.exp2(total + cut_row), cut_reach)

            @pl.when((cut >= 0) & here)
            def _():
                chosen = (seg == cut_seg) & (pos + j * BLOCK <= cut)
                wf3[...] = pack3(jnp.where(chosen, jnp.exp2(jnp.minimum(cut_row - cum, 0.0)) * dt, 0.0))

            total = total + end
        keep3[...] = pack3(rows_of(keeps + [cut_keep, cut_reach], 16, LANES))
        core, upper = s_ref[0], s_ref[2]
        for top in range(2):
            for source in range(CORES):
                near = jnp.where(core == source, near_same[...], near_cross[...])
                far = jnp.where(core == source, far_same[...], far_cross[...])
                value = jnp.where(upper == top, near, far).astype(F32)
                for step in range(STEPS):
                    at = 32 * top + 8 * step + ROWS * source
                    dec_rows[at : at + ROWS, :] = value[ROWS * step : ROWS * step + ROWS, :]

    spread = spread_matrix(chunk)
    keep = mm(keep3[...], spread)
    half_lane = lax.broadcasted_iota(jnp.int32, (BLOCK, LANES), 1) < HEAD_DIM
    outs = (f0, f1, f2, f3)
    for index, out in enumerate(outs):

        @pl.when(m == index)
        def _():
            out[0:STATE] = jnp.zeros((STATE, CHUNK), BF16)
            out[STATE : STATE + 16] = rows_of(split3(keep[BLOCKS + 1 : BLOCKS + 2]), 16, CHUNK).astype(BF16)
            out[STATE + 16 : STATE + 32] = cx[...]
            out[STATE + 32 : STATE + 48] = cg[...]
            at = pl.multiple_of(chunk * CHUNK, CHUNK)
            out[DEC : DEC + 64] = dec_rows[:, pl.ds(at, CHUNK)].astype(BF16)
            out[DEC + 64 : DEC + 128] = dec_rows[:, GROUP_CH : GROUP_CH + 512].astype(BF16)
            for part in range(4):
                steps = dec_rows[16 * part : 16 * part + 16, GROUP_CH + 512 : GROUP_CH + 640]
                out[DEC + 128 : DEC + 144, part * LANES : (part + 1) * LANES] = steps.astype(BF16)

    state = None
    pairs = CHUNK // LANES
    heads = chunk * (CHUNK // HEAD_DIM)
    heads_tile = pl.ds(pl.multiple_of(heads, 8), 8)
    for j in range(BLOCKS):
        rows = slice(j * BLOCK, (j + 1) * BLOCK)
        if j > 0:
            high = state.astype(BF16)
            parts[0:STATE] = high
            parts[STATE:] = (state - high.astype(F32)).astype(BF16)
            c_rows = bcc[rows, STATE : 2 * STATE]
            carried[...] = mm(jnp.concatenate([c_rows, c_rows], axis=1), parts[...])
            reach[...] = mm(wb3[rows], spread)

        @pl.when((cut >= 0) & (cut_block == j))
        def _():
            wide[...] = mm(wf3[...], spread)
            fresh = mm(bt[j], (xc_ref[rows].astype(F32) * wide[...]).astype(BF16))
            if j > 0:
                fresh = keep[BLOCKS : BLOCKS + 1] * state + fresh
            for index, out in enumerate(outs):

                @pl.when(m == index)
                def _():
                    out[0:STATE] = fresh.astype(BF16)

        if j < BLOCKS - 1:
            wide[...] = mm(wp3[rows], spread)
            for pair in range(pairs):
                lanes = slice(pair * LANES, (pair + 1) * LANES)
                scaled[:, lanes] = (xc_ref[rows, lanes].astype(F32) * wide[:, lanes]).astype(BF16)
            fresh = mm(bt[j], scaled[...])
            state = fresh if j == 0 else keep[j : j + 1] * state + fresh
        cum = dtc[CHIP_TOKENS + j * BLOCK : CHIP_TOKENS + (j + 1) * BLOCK]
        turned = pltpu.roll(cum, LANES - heads, 1)
        cum_rows = cum_t[j, heads_tile, :]
        dt_rows = dt_t[j, heads_tile, :]
        for pair in range(pairs):
            weights = []
            for head in (2 * pair, 2 * pair + 1):
                gap = jnp.minimum(turned[:, head : head + 1] - cum_rows[head : head + 1], 0.0)
                weights.append((jnp.exp2(gap) * (gm[j] * dt_rows[head : head + 1])).astype(BF16))
            lanes = slice(pair * LANES, (pair + 1) * LANES)
            two = xc_ref[rows, lanes]
            zero = jnp.zeros_like(two)
            stacked = jnp.concatenate([jnp.where(half_lane, two, zero), jnp.where(half_lane, zero, two)], axis=0)
            value = mm(jnp.concatenate(weights, axis=1), stacked) + skip[:, lanes] * two.astype(F32)
            if j > 0:
                value = value + reach[:, lanes] * carried[:, lanes]
            local_out[rows, lanes] = value


def run_b(scalars, xc, bcc, dtc, skip, cx, cg, dec_hops):
    def fixed(shape):
        return pl.BlockSpec(shape, lambda m, s: (0,) * len(shape))

    def chunked(rows, per_core=0):
        return pl.BlockSpec((rows, CHUNK), lambda m, s: (0, s[0] * per_core + (s[1] ^ m)))

    return pl.pallas_call(
        kernel_b,
        grid_spec=pltpu.PrefetchScalarGridSpec(
            num_scalar_prefetch=1,
            grid=(RING,),
            in_specs=[
                chunked(CHIP_TOKENS), fixed((CHIP_TOKENS, 512)), fixed((2 * CHIP_TOKENS, LANES)),
                chunked(1, RING), chunked(16), fixed((16, 512)),
            ] + [fixed((16, WIDE))] * 4,
            out_specs=[fixed((MSG, CHUNK))] * RING + [chunked(CHIP_TOKENS)],
            scratch_shapes=[
                pltpu.VMEM((CHIP_TOKENS, LANES), BF16),
                pltpu.VMEM((CHIP_TOKENS, LANES), BF16),
                pltpu.VMEM((16, LANES), BF16),
                pltpu.VMEM((BLOCKS, STATE, BLOCK), BF16),
                pltpu.VMEM((BLOCKS, BLOCK, BLOCK), F32),
                pltpu.VMEM((BLOCKS, LANES, BLOCK), F32),
                pltpu.VMEM((BLOCKS, LANES, BLOCK), F32),
                pltpu.VMEM((BLOCK, LANES), BF16),
                pltpu.VMEM((BLOCK, CHUNK), F32),
                pltpu.VMEM((BLOCK, CHUNK), F32),
                pltpu.VMEM((BLOCK, CHUNK), F32),
                pltpu.VMEM((BLOCK, CHUNK), BF16),
                pltpu.VMEM((2 * STATE, CHUNK), BF16),
                pltpu.VMEM((64, WIDE), F32),
            ],
        ),
        out_shape=[jax.ShapeDtypeStruct((MSG, CHUNK), BF16)] * RING
        + [pltpu.HBM((CHIP_TOKENS, GROUP_CH), F32)],
        compiler_params=pltpu.CompilerParams(vmem_limit_bytes=14 * MIB),
        cost_estimate=pl.CostEstimate(flops=12 * 10**9, bytes_accessed=8 * 10**6, transcendentals=2 * 10**6),
        name="output_within_chip",
    )(scalars, xc, bcc, dtc, skip, cx, cg, *dec_hops)


def pick(refs, which, rows):
    out = refs[0][rows]
    for index in range(1, len(refs)):
        out = jnp.where(which == index, refs[index][rows], out)
    return out.astype(F32)


def decay_rows(tile):
    return tile[0:1] + tile[1:2] + tile[2:3]


def kernel_total(s_ref, l0, l1, l2, l3, total_out):
    state = jnp.zeros((STATE, CHUNK), F32)
    for chip in range(RING):
        which = s_ref[1] ^ chip
        part = pick((l0, l1, l2, l3), which, slice(0, STATE))
        factor = decay_rows(pick((l0, l1, l2, l3), which, slice(STATE, STATE + 16)))
        state = factor * state + part
    total_out[...] = state.astype(BF16)


def kernel_starts(s_ref, l0, l1, l2, l3, start, r0, r1, r2, r3):
    state = start[...].astype(F32)
    for chip in range(RING):
        which = s_ref[1] ^ chip
        for index, out in enumerate((r0, r1, r2, r3)):

            @pl.when(which == index)
            def _():
                out[...] = state.astype(BF16)

        if chip < RING - 1:
            part = pick((l0, l1, l2, l3), which, slice(0, STATE))
            factor = decay_rows(pick((l0, l1, l2, l3), which, slice(STATE, STATE + 16)))
            state = factor * state + part


def whole_call(kernel, out_shape, name, flops, scratch=()):
    def run(scalars, *args):
        return pl.pallas_call(
            kernel,
            in_specs=[pl.BlockSpec(memory_space=pltpu.SMEM)] + [pl.BlockSpec(memory_space=pltpu.VMEM)] * len(args),
            out_specs=jax.tree.map(lambda _: pl.BlockSpec(memory_space=pltpu.VMEM), out_shape),
            out_shape=out_shape,
            scratch_shapes=list(scratch),
            compiler_params=pltpu.CompilerParams(vmem_limit_bytes=8 * MIB),
            cost_estimate=pl.CostEstimate(flops=flops, bytes_accessed=3 * 10**6, transcendentals=0),
            name=name,
        )(scalars, *args)

    return run


def kernel_decode(
    s_ref, l0, l1, l2, l3, start, f0, f1, f2, f3,
    wx, bx, wg, bg, vecs, skip, bounds,
    keep_out, send_out,
    final, rows_f32, result,
):
    z, upper = s_ref[1], s_ref[2]
    ls, fs = (l0, l1, l2, l3), (f0, f1, f2, f3)
    lasts = [bounds[q] - 1 for q in range(PROMPTS)]
    final[...] = jnp.zeros_like(final)
    state = start[...].astype(F32)
    for chip in range(RING):
        which = z ^ chip
        origin = (upper * RING + chip) * CHIP_TOKENS
        part = pick(ls, which, slice(0, STATE))
        factor = decay_rows(pick(ls, which, slice(STATE, STATE + 16)))
        after = factor * state + part
        for q in range(PROMPTS):
            local = lasts[q] - origin

            @pl.when(local == CHIP_TOKENS - 1)
            def _():
                final[q] = after

            @pl.when((local >= 0) & (local < CHIP_TOKENS - 1))
            def _():
                fresh = pick(fs, which, slice(0, STATE))
                reach = decay_rows(pick(fs, which, slice(STATE, STATE + 16)))
                final[q] = fresh + reach * state

        state = after
    cache_x = sum(f[STATE + 16 : STATE + 32].astype(F32) for f in fs)
    cache_g = sum(f[STATE + 32 : STATE + 48].astype(F32) for f in fs)
    spread = spread_matrix(z)
    for index, f in enumerate(fs):
        rows_f32[index, :, 0:CHUNK] = f[DEC : DEC + 64].astype(F32)
        rows_f32[index, :, CHUNK : CHUNK + 512] = f[DEC + 64 : DEC + 128].astype(F32)
        for part in range(4):
            steps = f[DEC + 128 : DEC + 144, part * LANES : (part + 1) * LANES].astype(F32)
            rows_f32[index, 16 * part : 16 * part + 16, CHUNK + 512 :] = steps

    def step_rows(step, lanes):
        tiles = [
            rows_f32[index, 32 * side + 8 * step : 32 * side + 8 * step + 8, lanes]
            for index in range(RING)
            for side in range(2)
        ]
        return jnp.concatenate(tiles, axis=0)

    prompt = step_rows(0, slice(1024, 1152))[:, 96:97]
    chosen = [prompt == float(q) for q in range(PROMPTS)]
    mine = jnp.zeros_like(prompt)
    for q in range(PROMPTS):
        inside = jnp.where(lasts[q] // (RING * CHIP_TOKENS) == upper, 1.0, 0.0)
        mine = jnp.where(chosen[q], inside, mine)

    def window(cache, lanes):
        rows = []
        for tap in range(CONV - 1):
            row = jnp.zeros((STEPS * 16, CHUNK), F32)
            for q in range(PROMPTS):
                row = jnp.where(chosen[q], cache[3 * q + tap : 3 * q + tap + 1], row)
            rows.append(row)
        return rows + [step_rows(step, lanes) for step in range(STEPS)]

    def convolved(rows, weight, offset):
        out = []
        for step in range(STEPS):
            running = jnp.broadcast_to(offset, rows[0].shape)
            for tap in range(CONV):
                running = running + weight[tap : tap + 1] * rows[step + tap]
            out.append(silu(running).astype(BF16))
        return out

    mixed = convolved(window(cache_x, slice(0, 512)), wx[...].astype(F32), bx[...])
    both = convolved(window(cache_g, slice(512, 1024)), wg[...].astype(F32), bg[...])
    steps, fades = [], []
    fade = jnp.zeros((STEPS * 16, LANES), F32)
    for step in range(STEPS):
        dt = softplus(step_rows(step, slice(1024, 1152)) + vecs[0:1])
        fade = fade + dt * vecs[1:2]
        steps.append(dt)
        fades.append(fade)
    readers = jnp.concatenate([rows[:, STATE:] for rows in both], axis=0)
    readout = jnp.zeros((STEPS * STEPS * 16, CHUNK), F32)
    for q in range(PROMPTS):
        high = final[q].astype(BF16)
        low = (final[q] - high.astype(F32)).astype(BF16)
        value = mm(readers, high) + mm(readers, low)
        readout = jnp.where(jnp.concatenate([chosen[q]] * STEPS, axis=0), value, readout)
    for step in range(STEPS):
        mixed_now = mixed[step].astype(F32)
        total = readout[64 * step : 64 * step + 64] * mm(pack3(jnp.exp2(fades[step])), spread)
        total = total + skip[...] * mixed_now
        reader = both[step][:, STATE:].astype(F32)
        for past in range(step + 1):
            weight = steps[past]
            if past < step:
                weight = weight * jnp.exp2(fades[step] - fades[past])
            product = jnp.sum(reader * both[past][:, 0:STATE].astype(F32), axis=1, keepdims=True)
            total = total + mm(pack3(weight), spread) * (product * mixed[past].astype(F32))
        total = jnp.where(mine > 0.5, total, 0.0)
        for index in range(RING):
            for side in range(2):
                tile = total[8 * (2 * index + side) : 8 * (2 * index + side) + 8]
                result[index, 32 * side + 8 * step : 32 * side + 8 * step + 8, :] = tile
    for index in range(RING):
        keep_out[index] = result[index, pl.ds(pl.multiple_of(32 * upper, 32), 32), :].astype(BF16)
        send_out[index] = result[index, pl.ds(pl.multiple_of(32 * (1 - upper), 32), 32), :].astype(BF16)


def kernel_d(s_ref, local, c_rows, wc3, r0, r1, r2, r3, out):
    m = pl.program_id(0)
    spread = spread_matrix(s_ref[1] ^ m)
    for index, r in enumerate((r0, r1, r2, r3)):

        @pl.when(m == index)
        def _():
            for lanes in (slice(0, 256), slice(256, 512)):
                factor = mm(wc3[...], spread[:, lanes])
                out[:, lanes] = (local[:, lanes] + factor * mm(c_rows[...], r[:, lanes])).astype(BF16)


def run_d(scalars, local, bcc, wc3, starts, own):
    half = CHIP_TOKENS // 2

    def row(s):
        return s[0] if own else 1 - s[0]

    width = CORES * GROUP_CH if own else GROUP_CH
    return pl.pallas_call(
        kernel_d,
        grid_spec=pltpu.PrefetchScalarGridSpec(
            num_scalar_prefetch=1,
            grid=(RING,),
            in_specs=[
                pl.BlockSpec((half, CHUNK), lambda m, s: (row(s), s[1] ^ m)),
                pl.BlockSpec((half, STATE), lambda m, s: (row(s), 1)),
                pl.BlockSpec((half, LANES), lambda m, s: (row(s), 0)),
            ] + [pl.BlockSpec((STATE, CHUNK), lambda m, s: (0, 0))] * RING,
            out_specs=pl.BlockSpec((half, CHUNK), lambda m, s: (0, (s[0] * RING if own else 0) + (s[1] ^ m))),
        ),
        out_shape=jax.ShapeDtypeStruct((half, width), BF16),
        compiler_params=pltpu.CompilerParams(vmem_limit_bytes=8 * MIB),
        cost_estimate=pl.CostEstimate(flops=10**9, bytes_accessed=4 * 10**6, transcendentals=0),
        name="carried_own" if own else "carried_other",
    )(scalars, local, bcc, wc3, *starts)


def kernel_put(s_ref, part, whole, out):
    out[...] = part[...]


def put_group(scalars, whole, part):
    half = CHIP_TOKENS // 2
    return pl.pallas_call(
        kernel_put,
        grid_spec=pltpu.PrefetchScalarGridSpec(
            num_scalar_prefetch=1,
            grid=(2,),
            in_specs=[
                pl.BlockSpec((half, GROUP_CH // 2), lambda m, s: (0, m)),
                pl.BlockSpec(memory_space=pl.ANY),
            ],
            out_specs=pl.BlockSpec((half, GROUP_CH // 2), lambda m, s: (0, (1 - s[0]) * 2 + m)),
        ),
        out_shape=jax.ShapeDtypeStruct(whole.shape, BF16),
        input_output_aliases={2: 0},
        compiler_params=pltpu.CompilerParams(vmem_limit_bytes=4 * MIB),
        cost_estimate=pl.CostEstimate(flops=0, bytes_accessed=2 * 10**6, transcendentals=0),
        name="put_group",
    )(scalars, part, whole)


def side_tiles(bc, dt, group):
    lane = lax.broadcasted_iota(jnp.int32, (64, LANES), 1)
    head = lax.broadcasted_iota(jnp.int32, (64, LANES), 0)
    copies = jnp.where(((lane & (REP - 1)) + group * REP == head) & (lane < 3 * REP), 1.0, 0.0).astype(BF16)
    first = group == 0
    return [
        jnp.where(first, bc[:, 0, 0:STATE], bc[:, 0, STATE : 2 * STATE]),
        jnp.where(first, bc[:, 1, 0:STATE], bc[:, 1, STATE : 2 * STATE]),
        mm(dt[...], copies).astype(BF16),
    ]


def kernel_pack(s_ref, x, bc, dt, x_last, bc_last, dt_last, send, halo0, halo1, side):
    core = s_ref[0]
    rows = x.shape[0]
    send[:, 0:GROUP_CH] = x[...]
    for target, group, offset in ((send, 1 - core, GROUP_CH), (side, core, 0)):
        b_tile, c_tile, steps = side_tiles(bc, dt, group)
        target[:, offset : offset + STATE] = b_tile
        target[:, offset + STATE : offset + 2 * STATE] = c_tile
        target[:, offset + 2 * STATE : offset + 2 * STATE + LANES] = steps
        target[:, offset + 2 * STATE + LANES : offset + 1024] = jnp.zeros((rows, 384), BF16)

    @pl.when(pl.program_id(0) == 0)
    def _():
        for group, halo in ((0, halo0), (1, halo1)):
            b_tile, c_tile, _ = side_tiles(bc_last, dt_last, jnp.int32(group))
            halo[:, 0:GROUP_CH] = x_last[:, group * GROUP_CH : (group + 1) * GROUP_CH]
            halo[:, GROUP_CH : GROUP_CH + STATE] = b_tile
            halo[:, GROUP_CH + STATE : GROUP_CH + 2 * STATE] = c_tile
            halo[:, GROUP_CH + 2 * STATE :] = jnp.zeros((16, 512), BF16)


def run_pack(core, x, bc, dt):
    rows = x.shape[0]
    tile = rows // RING
    last = rows // 16 - 1
    return pl.pallas_call(
        kernel_pack,
        grid_spec=pltpu.PrefetchScalarGridSpec(
            num_scalar_prefetch=1,
            grid=(RING,),
            in_specs=[
                pl.BlockSpec((tile, GROUP_CH), lambda i, s: (i, 1 - s[0])),
                pl.BlockSpec((tile, 2, 512), lambda i, s: (i, 0, 0)),
                pl.BlockSpec((tile, 64), lambda i, s: (i, 0)),
                pl.BlockSpec((16, CORES * GROUP_CH), lambda i, s: (last, 0)),
                pl.BlockSpec((16, 2, 512), lambda i, s: (last, 0, 0)),
                pl.BlockSpec((16, 64), lambda i, s: (last, 0)),
            ],
            out_specs=[
                pl.BlockSpec((tile, WIDE), lambda i, s: (i, 0)),
                pl.BlockSpec((16, WIDE), lambda i, s: (0, 0)),
                pl.BlockSpec((16, WIDE), lambda i, s: (0, 0)),
                pl.BlockSpec((tile, 1024), lambda i, s: (i, 0)),
            ],
        ),
        out_shape=[jax.ShapeDtypeStruct(shape, BF16) for shape in ((rows, WIDE), (16, WIDE), (16, WIDE), (rows, 1024))],
        compiler_params=pltpu.CompilerParams(vmem_limit_bytes=8 * MIB),
        cost_estimate=pl.CostEstimate(flops=10**6, bytes_accessed=4 * 10**6, transcendentals=0),
        name="pack",
    )(core[None], x, bc, dt, x, bc, dt)


def on_device(
    x_in, bc_in, dt_raw, conv_w_x, conv_b_x, conv_w_bc, conv_b_bc, dt_bias, a_log, d_skip,
    lengths, decode_prompt, dec_x, dec_bc, dec_dt,
):
    count = lax.axis_size("dp")
    place = lax.axis_index("dp")
    core = place % CORES
    z = (place // CORES) % RING
    upper = place // (CORES * RING)
    anchor = (place // CORES) * CHIP_TOKENS
    bounds = jnp.stack([lengths[0, 0], lengths[0, 0] + lengths[0, 1], jnp.sum(lengths[0])]).astype(jnp.int32)
    zero = jnp.int32(0)
    scalars = jnp.stack([core, z, upper, anchor, bounds[0] - anchor, bounds[1] - anchor, zero, zero]).astype(jnp.int32)
    both = ("pool", "dp")

    def group_part(x, bc, dt, group, extra=None):
        rows = x.shape[0]
        channels = lax.dynamic_slice_in_dim(x, group * GROUP_CH, GROUP_CH, 1)
        return jnp.concatenate([channels, group_side(bc, dt, group, extra)], axis=1).reshape(rows, WIDE)

    def group_side(bc, dt, group, extra=None):
        rows = bc.shape[0]
        b_c = lax.dynamic_slice_in_dim(bc, group * STATE, STATE, 2).reshape(rows, 2 * STATE)
        steps = lax.dynamic_slice_in_dim(dt, group * REP, REP, 1)
        last = jnp.zeros((rows, REP), BF16) if extra is None else jnp.broadcast_to(extra, (rows, REP))
        return jnp.concatenate([b_c, steps, steps, steps, last, jnp.zeros((rows, 384), BF16)], axis=1)

    x_rows, bc_rows, dt_rows = (in_hbm(value[0]) for value in (x_in, bc_in, dt_raw))
    packed, halo0, halo1, g_own = run_pack(core.astype(jnp.int32), x_rows, bc_rows, dt_rows)
    recv = lax.ppermute(packed, "dp", [(i, i ^ 1) for i in range(count)])
    halo = lax.ppermute(halo0, "dp", [(i, i + 1) for i in range(1, count - 1, 2)])
    halo = halo + lax.ppermute(halo1, "dp", [(i, i + 2) for i in range(1, count - 1, 2)])

    def after(value, other):
        return lax.optimization_barrier((value, other))[0]

    dec_rows = STEPS * ROWS
    d_x, d_bc, d_dt = after((dec_x, dec_bc, dec_dt), halo1)
    d_x = d_x[0, 0].reshape(dec_rows, -1)
    d_bc = d_bc[0, 0].reshape(dec_rows, 2, -1)
    d_dt = d_dt[0, 0].reshape(dec_rows, -1)
    d_prompt = jnp.tile(decode_prompt[0, 0].astype(BF16), STEPS)[:, None]
    total = 2 * count
    d_same = group_part(d_x, d_bc, d_dt, core, d_prompt)
    d_cross = group_part(d_x, d_bc, d_dt, 1 - core, d_prompt)

    def hop(value, flip):
        return lax.ppermute(value, both, [(i, ((i + count) % total) ^ flip) for i in range(total)])

    dec_hops = [hop(d_same, 0), hop(d_cross, 1), hop(d_same, CORES * RING), hop(d_cross, CORES * RING + 1)]

    def z_swap(value, m):
        if m == 0:
            return value
        return lax.ppermute(value, "dp", [(i, i ^ (CORES * m)) for i in range(count)])

    w_group = lax.dynamic_slice_in_dim(conv_w_bc, core * STATE, STATE, 2).reshape(CONV, 2 * STATE)
    b_group = lax.dynamic_slice_in_dim(conv_b_bc, core * STATE, STATE, 1).reshape(1, 2 * STATE)
    rates = -LOG2E * jnp.exp(a_log)
    heads = jnp.stack([dt_bias, rates])
    heads = lax.dynamic_slice_in_dim(heads, core * REP, REP, 1)
    vecs = jnp.pad(jnp.tile(heads, (1, 3)), ((0, 6), (0, LANES - 3 * REP)))
    skip = jnp.repeat(d_skip, HEAD_DIM)[None]
    b_x = conv_b_x[None]

    *ls, xc, bcc, dtc, wc3, cx, cg = run_a(scalars, x_rows, recv, halo, conv_w_x, b_x, g_own, w_group, b_group, vecs)
    sent_ls = [z_swap(part, m) for m, part in enumerate(ls)]
    *fs, local = run_b(scalars, xc, bcc, dtc, skip, cx, cg, dec_hops)
    local = in_hbm(local)
    ls = after(tuple(sent_ls), fs[0])
    fs = [z_swap(part, m) for m, part in enumerate(fs)]

    state_shape = jax.ShapeDtypeStruct((STATE, CHUNK), BF16)
    half_total = whole_call(kernel_total, state_shape, "half_total", 10**6)(scalars, *ls)
    start = lax.ppermute(half_total, "dp", [(i, i + CORES * RING) for i in range(CORES * RING)])
    starts = whole_call(kernel_starts, [state_shape] * RING, "chip_starts", 10**6)(scalars, *ls, start)
    starts = [z_swap(part, m) for m, part in enumerate(starts)]

    def own_columns(value):
        return lax.dynamic_slice_in_dim(value, core * GROUP_CH + z * CHUNK, CHUNK, 1)

    def decode(bounds_ref_args):
        shape = jax.ShapeDtypeStruct((RING, 32, CHUNK), BF16)
        args = [*ls, start, *fs, own_columns(conv_w_x), own_columns(b_x), w_group, b_group, vecs, own_columns(skip)]
        return pl.pallas_call(
            kernel_decode,
            in_specs=[pl.BlockSpec(memory_space=pltpu.SMEM)]
            + [pl.BlockSpec(memory_space=pltpu.VMEM)] * len(args)
            + [pl.BlockSpec(memory_space=pltpu.SMEM)],
            out_specs=[pl.BlockSpec(memory_space=pltpu.VMEM)] * 2,
            out_shape=[shape, shape],
            scratch_shapes=[
                pltpu.VMEM((PROMPTS, STATE, CHUNK), F32),
                pltpu.VMEM((RING, 64, 1152), F32),
                pltpu.VMEM((RING, 64, CHUNK), F32),
            ],
            compiler_params=pltpu.CompilerParams(vmem_limit_bytes=14 * MIB),
            cost_estimate=pl.CostEstimate(flops=20 * 10**9, bytes_accessed=6 * 10**6, transcendentals=0),
            name="decode_rows",
        )(scalars, *args, bounds_ref_args)

    kept, sent = after(tuple(decode(bounds)), starts[1])
    other_rows = run_d(scalars, local, bcc, wc3, starts, False)
    other_group = lax.ppermute(other_rows, "dp", [(i, i ^ 1) for i in range(count)])
    straight = lax.ppermute(kept, both, [(i, (i + count) % total) for i in range(total)])
    crossed = lax.ppermute(sent, both, [(i, ((i + count) % total) ^ (CORES * RING)) for i in range(total)])
    answers = after(straight + crossed, other_rows)
    answers = [z_swap(answers[m], m) for m in range(RING)]
    columns = [
        functools.reduce(lambda a, m: jnp.where(z == j ^ m, answers[m], a), range(1, RING), answers[0])
        for j in range(RING)
    ]
    answers = jnp.concatenate(columns, axis=1).reshape(STEPS, CORES, ROWS, GROUP_CH)
    first, second = (answers[:, i].reshape(dec_rows, GROUP_CH) for i in range(CORES))
    mine = jnp.where(core == 0, first, second)
    theirs = lax.ppermute(jnp.where(core == 0, second, first), "dp", [(i, i ^ 1) for i in range(count)])
    decoded = jnp.where(core == 0, jnp.concatenate([mine, theirs], axis=1), jnp.concatenate([theirs, mine], axis=1))
    own_group = run_d(scalars, local, bcc, wc3, starts, True)
    out = put_group(scalars, own_group, other_group)
    return out[None], decoded.reshape(dec_x.shape)


def solution(mesh):
    in_specs = (
        P("pool", "dp", "tp"),
        P("pool", "dp", None, "tp"),
        P("pool", "dp", "tp"),
        P(None, "tp"),
        P("tp"),
        P(None, None, "tp"),
        P(None, "tp"),
        P("tp"),
        P("tp"),
        P("tp"),
        P("pool", None),
        P("pool", "dp", None),
        P("pool", "dp", None, None, "tp"),
        P("pool", "dp", None, None, None, "tp"),
        P("pool", "dp", None, None, "tp"),
    )
    out_specs = (P("pool", "dp", "tp"), P("pool", "dp", None, None, "tp"))
    return jax.shard_map(on_device, mesh=mesh, in_specs=in_specs, out_specs=out_specs, check_vma=False)
```

```python
import functools

import jax
import jax.numpy as jnp
from jax import lax
from jax.experimental import pallas as pl
from jax.experimental.pallas import tpu as pltpu
from jax.sharding import PartitionSpec as P

HEAD_DIM = 64
STATE = 256
CONV = 4
BLOCK = 128
PROMPTS = 3
STEPS = 4
ROWS = 4
CORES = 2
RING = 4
LANES = 128
DEC = STATE + 48
MSG = DEC + 144
SCRATCH_B = 14
REP = 32
CHIP_TOKENS = 512
BLOCKS = CHIP_TOKENS // BLOCK
GROUP_CH = 2048
CHUNK = GROUP_CH // RING
WIDE = GROUP_CH + 1024
LOG2E = 1.4426950408889634
F32 = jnp.float32
BF16 = jnp.bfloat16
MIB = 1024 * 1024


def split3(value):
    high = value.astype(BF16).astype(F32)
    rest = value - high
    middle = rest.astype(BF16).astype(F32)
    return high, middle, rest - middle


def pack3(value):
    high, middle, low = split3(value)
    lane = lax.broadcasted_iota(jnp.int32, value.shape, 1)
    return jnp.where(lane < REP, high, jnp.where(lane < 2 * REP, middle, low)).astype(BF16)


def spread_matrix(chunk):
    lane = lax.broadcasted_iota(jnp.int32, (LANES, CHUNK), 0)
    head = (lax.broadcasted_iota(jnp.int32, (LANES, CHUNK), 1) >> 6) + chunk * (CHUNK // HEAD_DIM)
    hit = ((lane & (REP - 1)) == head) & (lane < 3 * REP)
    return jnp.where(hit, 1.0, 0.0).astype(BF16)


def in_hbm(value):
    return pltpu.with_memory_space_constraint(value, pltpu.HBM)


def mm(a, b):
    return jnp.dot(a, b, preferred_element_type=F32)


def silu(value):
    half = 0.5 * value
    return half + half * jnp.tanh(half)


def softplus(value):
    return jnp.maximum(value, 0.0) + jnp.log1p(jnp.exp(-jnp.abs(value)))


def seg_vec(s_ref, pos):
    anchor, lo0, lo1 = s_ref[3], s_ref[4], s_ref[5]
    seg = (pos >= lo0).astype(jnp.int32) + (pos >= lo1).astype(jnp.int32)
    return jnp.where(pos < -anchor, -1, seg)


def seg_at(s_ref, pos):
    anchor, lo0, lo1 = s_ref[3], s_ref[4], s_ref[5]
    seg = jnp.where(pos >= lo0, 1, 0) + jnp.where(pos >= lo1, 1, 0)
    return jnp.where(pos + anchor < 0, -1, seg)


def rows_of(parts, count, width):
    row = lax.broadcasted_iota(jnp.int32, (count, width), 0)
    out = jnp.zeros((count, width), F32)
    for index, part in enumerate(parts):
        out = jnp.where(row == index, part, out)
    return out


def conv_tile(src, start, lanes, weight, offset, mask):
    tile = src[pl.ds(start, BLOCK + 8), lanes]
    running = jnp.broadcast_to(offset[:, lanes], (BLOCK, LANES))
    for tap in range(CONV - 1):
        moved = pltpu.roll(tile, CONV - 1 - tap, 0)[8:]
        running = running + weight[tap : tap + 1, lanes] * (moved * mask[tap, pl.ds(start, BLOCK), :])
    return silu(running + weight[CONV - 1 : CONV, lanes] * tile[8:])


def cache_rows(s_ref, src, out):
    out[...] = jnp.zeros_like(out)
    for prompt in range(PROMPTS):
        last = (s_ref[4] - 1, s_ref[5] - 1, RING * CORES * CHIP_TOKENS - 1 - s_ref[3])[prompt]

        @pl.when((last >= 0) & (last < CHIP_TOKENS))
        def _():
            for tap in range(CONV - 1):
                row = last - (CONV - 2) + tap
                same = jnp.where(seg_at(s_ref, row) == seg_at(s_ref, last), 1.0, 0.0)
                value = src[pl.ds(row + 8, 1), :]
                out[pl.ds(prompt * 3 + tap, 1), :] = jnp.where(same > 0.5, value, 0.0)


def cut_of(s_ref):
    first, second = s_ref[4] - 1, s_ref[5] - 1
    limit = CHIP_TOKENS - 1
    one = jnp.where((second >= 0) & (second < limit), second, -1)
    return jnp.where((first >= 0) & (first < limit), first, one)


def kernel_a(
    s_ref, x_own, x_rec, halo_x, wx, bx, g_own, g_rec, halo_g, wg, bg, vecs,
    l0, l1, l2, l3, xc_out, bcc_out, dtc_out, wc3_out, cx_out, cg_out,
    xs, gs, mask, wp3, keep3, bt, cache, wide, scaled,
):
    m = pl.program_id(0)
    core = s_ref[0]
    chunk = s_ref[1] ^ m
    first = core == 0
    half = CHIP_TOKENS // 2

    @pl.when(m == 0)
    def _():
        pos = lax.broadcasted_iota(jnp.int32, (CHIP_TOKENS, LANES), 0)
        own_seg = seg_vec(s_ref, pos)
        for tap in range(CONV - 1):
            mask[tap] = jnp.where(seg_vec(s_ref, pos - 3 + tap) == own_seg, 1.0, 0.0)
        gs[0:8] = halo_g[:, 0:512].astype(F32)[8:]
        gs[8 : 8 + half] = jnp.where(first, g_own[:, 0:512], g_rec[:, 0:512]).astype(F32)
        gs[8 + half :] = jnp.where(first, g_rec[:, 0:512], g_own[:, 0:512]).astype(F32)
        weight = wg[...].astype(F32)
        for j in range(BLOCKS):
            for strip in range(4):
                lanes = slice(strip * LANES, (strip + 1) * LANES)
                tile = conv_tile(gs, j * BLOCK, lanes, weight, bg, mask).astype(BF16)
                bcc_out[pl.ds(j * BLOCK, BLOCK), lanes] = tile
                if strip < 2:
                    bt[j, lanes, :] = tile.astype(F32).T.astype(BF16)
        cache_rows(s_ref, gs, cache)
        cg_out[...] = cache[...].astype(BF16)
        raw_a = jnp.where(first, g_own[:, 512:640], g_rec[:, 512:640]).astype(F32)
        raw_b = jnp.where(first, g_rec[:, 512:640], g_own[:, 512:640]).astype(F32)
        dt = softplus(jnp.concatenate([raw_a, raw_b], axis=0) + vecs[0:1])
        decay = dt * vecs[1:2]
        row = lax.broadcasted_iota(jnp.int32, (BLOCK, BLOCK), 0)
        col = lax.broadcasted_iota(jnp.int32, (BLOCK, BLOCK), 1)
        lower = jnp.where(row >= col, 1.0, 0.0).astype(BF16)
        dtc_out[0:CHIP_TOKENS] = dt
        total = jnp.zeros((1, LANES), F32)
        before = seg_at(s_ref, -1)
        keeps = []
        for j in range(BLOCKS):
            rows = slice(j * BLOCK, (j + 1) * BLOCK)
            high, middle, low = split3(decay[rows])
            cum = mm(lower, high.astype(BF16)) + mm(lower, middle.astype(BF16)) + mm(lower, low.astype(BF16))
            dtc_out[CHIP_TOKENS + j * BLOCK : CHIP_TOKENS + (j + 1) * BLOCK] = cum
            end = cum[BLOCK - 1 :]
            end_seg = seg_at(s_ref, (j + 1) * BLOCK - 1)
            weight_p = jnp.where(own_seg[rows] == end_seg, jnp.exp2(end - cum) * dt[rows], 0.0)
            wp3[pl.ds(j * BLOCK, BLOCK), :] = pack3(weight_p)
            reach = jnp.where(own_seg[rows] == before, jnp.exp2(total + cum), 0.0)
            wc3_out[pl.ds(j * BLOCK, BLOCK), :] = pack3(reach)
            keeps.append(jnp.where(seg_at(s_ref, j * BLOCK - 1) == end_seg, jnp.exp2(end), 0.0))
            total = total + end
        keeps.append(jnp.where(before == seg_at(s_ref, CHIP_TOKENS - 1), jnp.exp2(total), 0.0))
        keep3[...] = pack3(rows_of(keeps, 16, LANES))

    xs[0:8] = halo_x[...].astype(F32)[8:]
    xs[8 : 8 + half] = jnp.where(first, x_own[...], x_rec[...]).astype(F32)
    xs[8 + half :] = jnp.where(first, x_rec[...], x_own[...]).astype(F32)
    weight = wx[...].astype(F32)
    spread = spread_matrix(chunk)
    keep = mm(keep3[...], spread)
    for j in range(BLOCKS):
        rows = pl.ds(j * BLOCK, BLOCK)
        wide[...] = mm(wp3[rows, :], spread)
        for strip in range(CHUNK // LANES):
            lanes = slice(strip * LANES, (strip + 1) * LANES)
            xc = conv_tile(xs, j * BLOCK, lanes, weight, bx, mask).astype(BF16)
            xc_out[rows, lanes] = xc
            scaled[rows, lanes] = (xc.astype(F32) * wide[:, lanes]).astype(BF16)
    state = mm(bt[0], scaled[0:BLOCK, :])
    for j in range(1, BLOCKS):
        state = keep[j : j + 1] * state + mm(bt[j], scaled[pl.ds(j * BLOCK, BLOCK), :])
    cache_rows(s_ref, xs, cache)
    cx_out[...] = cache[...].astype(BF16)
    tail = rows_of(split3(keep[BLOCKS : BLOCKS + 1]), 16, CHUNK).astype(BF16)
    for index, out in enumerate((l0, l1, l2, l3)):

        @pl.when(m == index)
        def _():
            out[0:STATE] = state.astype(BF16)
            out[STATE:] = tail


def run_a(scalars, x_in, recv, halo, wx, bx, g_own, wg, bg, vecs):
    def fixed(shape):
        return pl.BlockSpec(shape, lambda m, s: (0,) * len(shape))

    def chunked(rows, per_core=0):
        return pl.BlockSpec((rows, CHUNK), lambda m, s: (0, s[0] * per_core + (s[1] ^ m)))

    half = CHIP_TOKENS // 2
    side = pl.BlockSpec((half, 1024), lambda m, s: (0, 2))
    return pl.pallas_call(
        kernel_a,
        grid_spec=pltpu.PrefetchScalarGridSpec(
            num_scalar_prefetch=1,
            grid=(RING,),
            in_specs=[
                chunked(half, RING), chunked(half), chunked(16), chunked(CONV, RING), chunked(1, RING),
                fixed((half, 1024)), side, pl.BlockSpec((16, 1024), lambda m, s: (0, 2)),
                fixed((CONV, 512)), fixed((1, 512)), fixed((8, LANES)),
            ],
            out_specs=[fixed((STATE + 16, CHUNK))] * RING + [
                chunked(CHIP_TOKENS), fixed((CHIP_TOKENS, 512)), fixed((2 * CHIP_TOKENS, LANES)),
                fixed((CHIP_TOKENS, LANES)), chunked(16), fixed((16, 512)),
            ],
            scratch_shapes=[
                pltpu.VMEM((CHIP_TOKENS + 8, CHUNK), F32),
                pltpu.VMEM((CHIP_TOKENS + 8, 512), F32),
                pltpu.VMEM((CONV - 1, CHIP_TOKENS, LANES), F32),
                pltpu.VMEM((CHIP_TOKENS, LANES), BF16),
                pltpu.VMEM((16, LANES), BF16),
                pltpu.VMEM((BLOCKS, STATE, BLOCK), BF16),
                pltpu.VMEM((16, CHUNK), F32),
                pltpu.VMEM((BLOCK, CHUNK), F32),
                pltpu.VMEM((CHIP_TOKENS, CHUNK), BF16),
            ],
        ),
        out_shape=[jax.ShapeDtypeStruct((STATE + 16, CHUNK), BF16)] * RING + [
            jax.ShapeDtypeStruct((CHIP_TOKENS, GROUP_CH), BF16),
            jax.ShapeDtypeStruct((CHIP_TOKENS, 512), BF16),
            jax.ShapeDtypeStruct((2 * CHIP_TOKENS, LANES), F32),
            jax.ShapeDtypeStruct((CHIP_TOKENS, LANES), BF16),
            jax.ShapeDtypeStruct((16, GROUP_CH), BF16),
            jax.ShapeDtypeStruct((16, 512), BF16),
        ],
        compiler_params=pltpu.CompilerParams(vmem_limit_bytes=16 * MIB),
        cost_estimate=pl.CostEstimate(flops=6 * 10**9, bytes_accessed=8 * 10**6, transcendentals=10**6),
        name="conv_and_states",
    )(scalars, x_in, recv, halo, wx, bx, g_own, recv, halo, wg, bg, vecs)


def kernel_b(
    base, count, s_ref, xc_ref, bcc, dtc, skip, cx, cg, near_same, near_cross, far_same, far_cross, *rest
):
    *outs, local_out = rest[-SCRATCH_B - count - 1 : -SCRATCH_B]
    (wp3, wb3, keep3, bt, gm, cum_t, dt_t, wf3, wide, reach, carried, scaled, parts, dec_rows) = rest[-SCRATCH_B:]
    m = pl.program_id(0) + base
    chunk = s_ref[1] ^ m
    cut = cut_of(s_ref)
    cut_block = cut // BLOCK

    @pl.when(m == base)
    def _():
        pos = lax.broadcasted_iota(jnp.int32, (BLOCK, LANES), 0)
        row = lax.broadcasted_iota(jnp.int32, (BLOCK, BLOCK), 0)
        col = lax.broadcasted_iota(jnp.int32, (BLOCK, BLOCK), 1)
        total = jnp.zeros((1, LANES), F32)
        before = seg_at(s_ref, -1)
        keeps = []
        cut_keep = jnp.zeros((1, LANES), F32)
        cut_reach = jnp.zeros((1, LANES), F32)
        cut_row = dtc[pl.ds(CHIP_TOKENS + jnp.maximum(cut, 0), 1), :]
        cut_seg = seg_at(s_ref, cut)
        wf3[...] = jnp.zeros_like(wf3)
        for j in range(BLOCKS):
            dt = dtc[j * BLOCK : (j + 1) * BLOCK]
            cum = dtc[CHIP_TOKENS + j * BLOCK : CHIP_TOKENS + (j + 1) * BLOCK]
            end = cum[BLOCK - 1 :]
            seg = seg_vec(s_ref, pos + j * BLOCK)
            end_seg = seg_at(s_ref, (j + 1) * BLOCK - 1)
            prev_seg = seg_at(s_ref, j * BLOCK - 1)
            wp3[pl.ds(j * BLOCK, BLOCK), :] = pack3(jnp.where(seg == end_seg, jnp.exp2(end - cum) * dt, 0.0))
            wb3[pl.ds(j * BLOCK, BLOCK), :] = pack3(jnp.where(seg == prev_seg, jnp.exp2(cum), 0.0))
            keeps.append(jnp.where(prev_seg == end_seg, jnp.exp2(end), 0.0))
            b_rows = bcc[pl.ds(j * BLOCK, BLOCK), 0:STATE]
            c_rows = bcc[pl.ds(j * BLOCK, BLOCK), STATE : 2 * STATE]
            b_t = b_rows.astype(F32).T.astype(BF16)
            bt[j] = b_t
            scores = mm(c_rows, b_t)
            same = seg_vec(s_ref, row + j * BLOCK) == seg_vec(s_ref, col + j * BLOCK)
            gm[j] = jnp.where((row >= col) & same, scores, 0.0)
            cum_t[j] = cum.T
            dt_t[j] = dt.T
            here = cut_block == j
            cut_keep = jnp.where(here & (cut_seg == prev_seg), jnp.exp2(cut_row), cut_keep)
            cut_reach = jnp.where(here & (cut_seg == before), jnp.exp2(total + cut_row), cut_reach)

            @pl.when((cut >= 0) & here)
            def _():
                chosen = (seg == cut_seg) & (pos + j * BLOCK <= cut)
                wf3[...] = pack3(jnp.where(chosen, jnp.exp2(jnp.minimum(cut_row - cum, 0.0)) * dt, 0.0))

            total = total + end
        keep3[...] = pack3(rows_of(keeps + [cut_keep, cut_reach], 16, LANES))
        core, upper = s_ref[0], s_ref[2]
        for top in range(2):
            for source in range(CORES):
                near = jnp.where(core == source, near_same[...], near_cross[...])
                far = jnp.where(core == source, far_same[...], far_cross[...])
                value = jnp.where(upper == top, near, far).astype(F32)
                for step in range(STEPS):
                    at = 32 * top + 8 * step + ROWS * source
                    dec_rows[at : at + ROWS, :] = value[ROWS * step : ROWS * step + ROWS, :]

    spread = spread_matrix(chunk)
    keep = mm(keep3[...], spread)
    half_lane = lax.broadcasted_iota(jnp.int32, (BLOCK, LANES), 1) < HEAD_DIM
    for index, out in enumerate(outs):

        @pl.when(m == base + index)
        def _():
            out[0:STATE] = jnp.zeros((STATE, CHUNK), BF16)
            out[STATE : STATE + 16] = rows_of(split3(keep[BLOCKS + 1 : BLOCKS + 2]), 16, CHUNK).astype(BF16)
            out[STATE + 16 : STATE + 32] = cx[...]
            out[STATE + 32 : STATE + 48] = cg[...]
            at = pl.multiple_of(chunk * CHUNK, CHUNK)
            out[DEC : DEC + 64] = dec_rows[:, pl.ds(at, CHUNK)].astype(BF16)
            out[DEC + 64 : DEC + 128] = dec_rows[:, GROUP_CH : GROUP_CH + 512].astype(BF16)
            for part in range(4):
                steps = dec_rows[16 * part : 16 * part + 16, GROUP_CH + 512 : GROUP_CH + 640]
                out[DEC + 128 : DEC + 144, part * LANES : (part + 1) * LANES] = steps.astype(BF16)

    state = None
    pairs = CHUNK // LANES
    heads = chunk * (CHUNK // HEAD_DIM)
    heads_tile = pl.ds(pl.multiple_of(heads, 8), 8)
    for j in range(BLOCKS):
        rows = slice(j * BLOCK, (j + 1) * BLOCK)
        if j > 0:
            high = state.astype(BF16)
            parts[0:STATE] = high
            parts[STATE:] = (state - high.astype(F32)).astype(BF16)
            c_rows = bcc[rows, STATE : 2 * STATE]
            carried[...] = mm(jnp.concatenate([c_rows, c_rows], axis=1), parts[...])
            reach[...] = mm(wb3[rows], spread)

        @pl.when((cut >= 0) & (cut_block == j))
        def _():
            wide[...] = mm(wf3[...], spread)
            fresh = mm(bt[j], (xc_ref[rows].astype(F32) * wide[...]).astype(BF16))
            if j > 0:
                fresh = keep[BLOCKS : BLOCKS + 1] * state + fresh
            for index, out in enumerate(outs):

                @pl.when(m == base + index)
                def _():
                    out[0:STATE] = fresh.astype(BF16)

        if j < BLOCKS - 1:
            wide[...] = mm(wp3[rows], spread)
            for pair in range(pairs):
                lanes = slice(pair * LANES, (pair + 1) * LANES)
                scaled[:, lanes] = (xc_ref[rows, lanes].astype(F32) * wide[:, lanes]).astype(BF16)
            fresh = mm(bt[j], scaled[...])
            state = fresh if j == 0 else keep[j : j + 1] * state + fresh
        cum = dtc[CHIP_TOKENS + j * BLOCK : CHIP_TOKENS + (j + 1) * BLOCK]
        turned = pltpu.roll(cum, LANES - heads, 1)
        cum_rows = cum_t[j, heads_tile, :]
        dt_rows = dt_t[j, heads_tile, :]
        for pair in range(pairs):
            weights = []
            for head in (2 * pair, 2 * pair + 1):
                gap = jnp.minimum(turned[:, head : head + 1] - cum_rows[head : head + 1], 0.0)
                weights.append((jnp.exp2(gap) * (gm[j] * dt_rows[head : head + 1])).astype(BF16))
            lanes = slice(pair * LANES, (pair + 1) * LANES)
            two = xc_ref[rows, lanes]
            zero = jnp.zeros_like(two)
            stacked = jnp.concatenate([jnp.where(half_lane, two, zero), jnp.where(half_lane, zero, two)], axis=0)
            value = mm(jnp.concatenate(weights, axis=1), stacked) + skip[:, lanes] * two.astype(F32)
            if j > 0:
                value = value + reach[:, lanes] * carried[:, lanes]
            local_out[rows, lanes] = value


def run_b(scalars, xc, bcc, dtc, skip, cx, cg, dec_hops, base, count, local=None):
    def fixed(shape):
        return pl.BlockSpec(shape, lambda m, s: (0,) * len(shape))

    def chunked(rows, per_core=0):
        return pl.BlockSpec((rows, CHUNK), lambda m, s: (0, s[0] * per_core + (s[1] ^ (m + base))))

    args = [scalars, xc, bcc, dtc, skip, cx, cg, *dec_hops]
    in_specs = [
        chunked(CHIP_TOKENS), fixed((CHIP_TOKENS, 512)), fixed((2 * CHIP_TOKENS, LANES)),
        chunked(1, RING), chunked(16), fixed((16, 512)),
    ] + [fixed((16, WIDE))] * 4
    aliases = {}
    if local is not None:
        aliases = {len(args): count}
        args.append(local)
        in_specs.append(pl.BlockSpec(memory_space=pl.ANY))
    scratch = [
        pltpu.VMEM((CHIP_TOKENS, LANES), BF16),
        pltpu.VMEM((CHIP_TOKENS, LANES), BF16),
        pltpu.VMEM((16, LANES), BF16),
        pltpu.VMEM((BLOCKS, STATE, BLOCK), BF16),
        pltpu.VMEM((BLOCKS, BLOCK, BLOCK), F32),
        pltpu.VMEM((BLOCKS, LANES, BLOCK), F32),
        pltpu.VMEM((BLOCKS, LANES, BLOCK), F32),
        pltpu.VMEM((BLOCK, LANES), BF16),
        pltpu.VMEM((BLOCK, CHUNK), F32),
        pltpu.VMEM((BLOCK, CHUNK), F32),
        pltpu.VMEM((BLOCK, CHUNK), F32),
        pltpu.VMEM((BLOCK, CHUNK), BF16),
        pltpu.VMEM((2 * STATE, CHUNK), BF16),
        pltpu.VMEM((64, WIDE), F32),
    ]
    assert len(scratch) == SCRATCH_B
    return pl.pallas_call(
        functools.partial(kernel_b, base, count),
        grid_spec=pltpu.PrefetchScalarGridSpec(
            num_scalar_prefetch=1,
            grid=(count,),
            in_specs=in_specs,
            out_specs=[fixed((MSG, CHUNK))] * count + [chunked(CHIP_TOKENS)],
            scratch_shapes=scratch,
        ),
        out_shape=[jax.ShapeDtypeStruct((MSG, CHUNK), BF16)] * count + [pltpu.HBM((CHIP_TOKENS, GROUP_CH), F32)],
        input_output_aliases=aliases,
        compiler_params=pltpu.CompilerParams(vmem_limit_bytes=14 * MIB),
        cost_estimate=pl.CostEstimate(
            flops=3 * count * 10**9, bytes_accessed=2 * count * 10**6, transcendentals=count * 10**5
        ),
        name=f"output_within_chip_{base}",
    )(*args)


def pick(refs, which, rows):
    out = refs[0][rows]
    for index in range(1, len(refs)):
        out = jnp.where(which == index, refs[index][rows], out)
    return out.astype(F32)


def decay_rows(tile):
    return tile[0:1] + tile[1:2] + tile[2:3]


def kernel_total(s_ref, l0, l1, l2, l3, total_out):
    state = jnp.zeros((STATE, CHUNK), F32)
    for chip in range(RING):
        which = s_ref[1] ^ chip
        part = pick((l0, l1, l2, l3), which, slice(0, STATE))
        factor = decay_rows(pick((l0, l1, l2, l3), which, slice(STATE, STATE + 16)))
        state = factor * state + part
    total_out[...] = state.astype(BF16)


def kernel_starts(s_ref, l0, l1, l2, l3, start, r0, r1, r2, r3):
    state = start[...].astype(F32)
    for chip in range(RING):
        which = s_ref[1] ^ chip
        for index, out in enumerate((r0, r1, r2, r3)):

            @pl.when(which == index)
            def _():
                out[...] = state.astype(BF16)

        if chip < RING - 1:
            part = pick((l0, l1, l2, l3), which, slice(0, STATE))
            factor = decay_rows(pick((l0, l1, l2, l3), which, slice(STATE, STATE + 16)))
            state = factor * state + part


def whole_call(kernel, out_shape, name, flops, scratch=()):
    def run(scalars, *args):
        return pl.pallas_call(
            kernel,
            in_specs=[pl.BlockSpec(memory_space=pltpu.SMEM)] + [pl.BlockSpec(memory_space=pltpu.VMEM)] * len(args),
            out_specs=jax.tree.map(lambda _: pl.BlockSpec(memory_space=pltpu.VMEM), out_shape),
            out_shape=out_shape,
            scratch_shapes=list(scratch),
            compiler_params=pltpu.CompilerParams(vmem_limit_bytes=8 * MIB),
            cost_estimate=pl.CostEstimate(flops=flops, bytes_accessed=3 * 10**6, transcendentals=0),
            name=name,
        )(scalars, *args)

    return run


def kernel_decode(
    s_ref, l0, l1, l2, l3, start, f0, f1, f2, f3,
    wx, bx, wg, bg, vecs, skip, bounds,
    keep_out, send_out,
    final, rows_f32, result,
):
    z, upper = s_ref[1], s_ref[2]
    ls, fs = (l0, l1, l2, l3), (f0, f1, f2, f3)
    lasts = [bounds[q] - 1 for q in range(PROMPTS)]
    final[...] = jnp.zeros_like(final)
    state = start[...].astype(F32)
    for chip in range(RING):
        which = z ^ chip
        origin = (upper * RING + chip) * CHIP_TOKENS
        part = pick(ls, which, slice(0, STATE))
        factor = decay_rows(pick(ls, which, slice(STATE, STATE + 16)))
        after = factor * state + part
        for q in range(PROMPTS):
            local = lasts[q] - origin

            @pl.when(local == CHIP_TOKENS - 1)
            def _():
                final[q] = after

            @pl.when((local >= 0) & (local < CHIP_TOKENS - 1))
            def _():
                fresh = pick(fs, which, slice(0, STATE))
                reach = decay_rows(pick(fs, which, slice(STATE, STATE + 16)))
                final[q] = fresh + reach * state

        state = after
    cache_x = sum(f[STATE + 16 : STATE + 32].astype(F32) for f in fs)
    cache_g = sum(f[STATE + 32 : STATE + 48].astype(F32) for f in fs)
    spread = spread_matrix(z)
    for index, f in enumerate(fs):
        rows_f32[index, :, 0:CHUNK] = f[DEC : DEC + 64].astype(F32)
        rows_f32[index, :, CHUNK : CHUNK + 512] = f[DEC + 64 : DEC + 128].astype(F32)
        for part in range(4):
            steps = f[DEC + 128 : DEC + 144, part * LANES : (part + 1) * LANES].astype(F32)
            rows_f32[index, 16 * part : 16 * part + 16, CHUNK + 512 :] = steps

    def step_rows(step, lanes):
        tiles = [
            rows_f32[index, 32 * side + 8 * step : 32 * side + 8 * step + 8, lanes]
            for index in range(RING)
            for side in range(2)
        ]
        return jnp.concatenate(tiles, axis=0)

    prompt = step_rows(0, slice(1024, 1152))[:, 96:97]
    chosen = [prompt == float(q) for q in range(PROMPTS)]
    mine = jnp.zeros_like(prompt)
    for q in range(PROMPTS):
        inside = jnp.where(lasts[q] // (RING * CHIP_TOKENS) == upper, 1.0, 0.0)
        mine = jnp.where(chosen[q], inside, mine)

    def window(cache, lanes):
        rows = []
        for tap in range(CONV - 1):
            row = jnp.zeros((STEPS * 16, CHUNK), F32)
            for q in range(PROMPTS):
                row = jnp.where(chosen[q], cache[3 * q + tap : 3 * q + tap + 1], row)
            rows.append(row)
        return rows + [step_rows(step, lanes) for step in range(STEPS)]

    def convolved(rows, weight, offset):
        out = []
        for step in range(STEPS):
            running = jnp.broadcast_to(offset, rows[0].shape)
            for tap in range(CONV):
                running = running + weight[tap : tap + 1] * rows[step + tap]
            out.append(silu(running).astype(BF16))
        return out

    mixed = convolved(window(cache_x, slice(0, 512)), wx[...].astype(F32), bx[...])
    both = convolved(window(cache_g, slice(512, 1024)), wg[...].astype(F32), bg[...])
    steps, fades = [], []
    fade = jnp.zeros((STEPS * 16, LANES), F32)
    for step in range(STEPS):
        dt = softplus(step_rows(step, slice(1024, 1152)) + vecs[0:1])
        fade = fade + dt * vecs[1:2]
        steps.append(dt)
        fades.append(fade)
    readers = jnp.concatenate([rows[:, STATE:] for rows in both], axis=0)
    readout = jnp.zeros((STEPS * STEPS * 16, CHUNK), F32)
    for q in range(PROMPTS):
        high = final[q].astype(BF16)
        low = (final[q] - high.astype(F32)).astype(BF16)
        value = mm(readers, high) + mm(readers, low)
        readout = jnp.where(jnp.concatenate([chosen[q]] * STEPS, axis=0), value, readout)
    for step in range(STEPS):
        mixed_now = mixed[step].astype(F32)
        total = readout[64 * step : 64 * step + 64] * mm(pack3(jnp.exp2(fades[step])), spread)
        total = total + skip[...] * mixed_now
        reader = both[step][:, STATE:].astype(F32)
        for past in range(step + 1):
            weight = steps[past]
            if past < step:
                weight = weight * jnp.exp2(fades[step] - fades[past])
            product = jnp.sum(reader * both[past][:, 0:STATE].astype(F32), axis=1, keepdims=True)
            total = total + mm(pack3(weight), spread) * (product * mixed[past].astype(F32))
        total = jnp.where(mine > 0.5, total, 0.0)
        for index in range(RING):
            for side in range(2):
                tile = total[8 * (2 * index + side) : 8 * (2 * index + side) + 8]
                result[index, 32 * side + 8 * step : 32 * side + 8 * step + 8, :] = tile
    for index in range(RING):
        keep_out[index] = result[index, pl.ds(pl.multiple_of(32 * upper, 32), 32), :].astype(BF16)
        send_out[index] = result[index, pl.ds(pl.multiple_of(32 * (1 - upper), 32), 32), :].astype(BF16)


def kernel_d(s_ref, local, c_rows, wc3, r0, r1, r2, r3, out):
    m = pl.program_id(0)
    spread = spread_matrix(s_ref[1] ^ m)
    for index, r in enumerate((r0, r1, r2, r3)):

        @pl.when(m == index)
        def _():
            for lanes in (slice(0, 256), slice(256, 512)):
                factor = mm(wc3[...], spread[:, lanes])
                out[:, lanes] = (local[:, lanes] + factor * mm(c_rows[...], r[:, lanes])).astype(BF16)


def run_d(scalars, local, bcc, wc3, starts, own):
    half = CHIP_TOKENS // 2

    def row(s):
        return s[0] if own else 1 - s[0]

    width = CORES * GROUP_CH if own else GROUP_CH
    return pl.pallas_call(
        kernel_d,
        grid_spec=pltpu.PrefetchScalarGridSpec(
            num_scalar_prefetch=1,
            grid=(RING,),
            in_specs=[
                pl.BlockSpec((half, CHUNK), lambda m, s: (row(s), s[1] ^ m)),
                pl.BlockSpec((half, STATE), lambda m, s: (row(s), 1)),
                pl.BlockSpec((half, LANES), lambda m, s: (row(s), 0)),
            ] + [pl.BlockSpec((STATE, CHUNK), lambda m, s: (0, 0))] * RING,
            out_specs=pl.BlockSpec((half, CHUNK), lambda m, s: (0, (s[0] * RING if own else 0) + (s[1] ^ m))),
        ),
        out_shape=jax.ShapeDtypeStruct((half, width), BF16),
        compiler_params=pltpu.CompilerParams(vmem_limit_bytes=8 * MIB),
        cost_estimate=pl.CostEstimate(flops=10**9, bytes_accessed=4 * 10**6, transcendentals=0),
        name="carried_own" if own else "carried_other",
    )(scalars, local, bcc, wc3, *starts)


def kernel_put(s_ref, part, whole, out):
    out[...] = part[...]


def put_group(scalars, whole, part):
    half = CHIP_TOKENS // 2
    return pl.pallas_call(
        kernel_put,
        grid_spec=pltpu.PrefetchScalarGridSpec(
            num_scalar_prefetch=1,
            grid=(2,),
            in_specs=[
                pl.BlockSpec((half, GROUP_CH // 2), lambda m, s: (0, m)),
                pl.BlockSpec(memory_space=pl.ANY),
            ],
            out_specs=pl.BlockSpec((half, GROUP_CH // 2), lambda m, s: (0, (1 - s[0]) * 2 + m)),
        ),
        out_shape=jax.ShapeDtypeStruct(whole.shape, BF16),
        input_output_aliases={2: 0},
        compiler_params=pltpu.CompilerParams(vmem_limit_bytes=4 * MIB),
        cost_estimate=pl.CostEstimate(flops=0, bytes_accessed=2 * 10**6, transcendentals=0),
        name="put_group",
    )(scalars, part, whole)


def head_copies(group):
    lane = lax.broadcasted_iota(jnp.int32, (64, LANES), 1)
    head = lax.broadcasted_iota(jnp.int32, (64, LANES), 0)
    hit = ((lane & (REP - 1)) + group * REP == head) & (lane < 3 * REP)
    return jnp.where(hit, 1.0, 0.0).astype(BF16)


def kernel_pack(s_ref, x, bc, dt_t, x_last, bc_last, dx, dbc, ddt, send, halo0, halo1, side, d_own, d_other, rows_f32):
    core = s_ref[0]
    first = core == 0
    rows = x.shape[0]
    start = pl.multiple_of(pl.program_id(0) * rows, rows)
    dt = dt_t[:, pl.ds(start, rows)].astype(F32).T.astype(BF16)
    b_rows, c_rows = bc[:, 0, :], bc[:, 1, :]
    send[:, 0:GROUP_CH] = x[...]
    for target, group, offset in ((send, 1 - core, GROUP_CH), (side, core, 0)):
        low = group == 0
        target[:, offset : offset + STATE] = jnp.where(low, b_rows[:, 0:STATE], b_rows[:, STATE:])
        target[:, offset + STATE : offset + 2 * STATE] = jnp.where(low, c_rows[:, 0:STATE], c_rows[:, STATE:])
        target[:, offset + 512 : offset + 640] = mm(dt, head_copies(group)).astype(BF16)
        target[:, offset + 640 : offset + 1024] = jnp.zeros((rows, 384), BF16)

    @pl.when(pl.program_id(0) == 0)
    def _():
        b_last, c_last = bc_last[:, 0, :], bc_last[:, 1, :]
        for group, halo in ((0, halo0), (1, halo1)):
            halo[:, 0:GROUP_CH] = x_last[:, group * GROUP_CH : (group + 1) * GROUP_CH]
            halo[:, GROUP_CH : GROUP_CH + STATE] = b_last[:, group * STATE : (group + 1) * STATE]
            halo[:, GROUP_CH + STATE : GROUP_CH + 512] = c_last[:, group * STATE : (group + 1) * STATE]
            halo[:, GROUP_CH + 512 :] = jnp.zeros((16, 512), BF16)
        lane = lax.broadcasted_iota(jnp.int32, (ROWS, LANES), 1)
        row = lax.broadcasted_iota(jnp.int32, (ROWS, LANES), 0)
        prompt = jnp.zeros((ROWS, LANES), F32)
        for r in range(ROWS):
            prompt = jnp.where(row == r, s_ref[1 + r].astype(F32), prompt)
        for out, group in ((d_own, core), (d_other, 1 - core)):
            low = group == 0
            rows_f32[...] = jnp.zeros_like(rows_f32)
            for step in range(STEPS):
                at = slice(ROWS * step, ROWS * step + ROWS)
                value = dx[step].astype(F32)
                rows_f32[at, 0:GROUP_CH] = jnp.where(low, value[:, 0:GROUP_CH], value[:, GROUP_CH:])
                for part in range(2):
                    value = dbc[step, :, part, :].astype(F32)
                    to = GROUP_CH + part * STATE
                    rows_f32[at, to : to + STATE] = jnp.where(low, value[:, 0:STATE], value[:, STATE:])
                steps = mm(ddt[step], head_copies(group))
                rows_f32[at, GROUP_CH + 512 : GROUP_CH + 640] = jnp.where(lane < 3 * REP, steps, prompt)
            out[...] = rows_f32[...].astype(BF16)


def run_pack(scalars, x, bc, dt_t, dx, dbc, ddt):
    rows = x.shape[0]
    tile = rows // 2
    last = rows // 16 - 1
    small = (16, WIDE)

    def fixed(shape):
        return pl.BlockSpec(shape, lambda i, s: (0,) * len(shape))

    return pl.pallas_call(
        kernel_pack,
        grid_spec=pltpu.PrefetchScalarGridSpec(
            num_scalar_prefetch=1,
            grid=(2,),
            in_specs=[
                pl.BlockSpec((tile, GROUP_CH), lambda i, s: (i, 1 - s[0])),
                pl.BlockSpec((tile, 2, 512), lambda i, s: (i, 0, 0)),
                fixed(dt_t.shape),
                pl.BlockSpec((16, CORES * GROUP_CH), lambda i, s: (last, 0)),
                pl.BlockSpec((16, 2, 512), lambda i, s: (last, 0, 0)),
                fixed(dx.shape),
                fixed(dbc.shape),
                fixed(ddt.shape),
            ],
            out_specs=[
                pl.BlockSpec((tile, WIDE), lambda i, s: (i, 0)),
                fixed(small),
                fixed(small),
                pl.BlockSpec((tile, 1024), lambda i, s: (i, 0)),
                fixed(small),
                fixed(small),
            ],
            scratch_shapes=[pltpu.VMEM(small, F32)],
        ),
        out_shape=[pltpu.HBM(shape, BF16) for shape in ((rows, WIDE), small, small, (rows, 1024), small, small)],
        compiler_params=pltpu.CompilerParams(vmem_limit_bytes=12 * MIB),
        cost_estimate=pl.CostEstimate(flops=10**6, bytes_accessed=4 * 10**6, transcendentals=0),
        name="pack",
    )(scalars, x, bc, dt_t, x, bc, dx, dbc, ddt)


def on_device(
    x_in, bc_in, dt_raw, conv_w_x, conv_b_x, conv_w_bc, conv_b_bc, dt_bias, a_log, d_skip,
    lengths, decode_prompt, dec_x, dec_bc, dec_dt,
):
    count = lax.axis_size("dp")
    place = lax.axis_index("dp")
    core = place % CORES
    z = (place // CORES) % RING
    upper = place // (CORES * RING)
    anchor = (place // CORES) * CHIP_TOKENS
    bounds = jnp.stack([lengths[0, 0], lengths[0, 0] + lengths[0, 1], jnp.sum(lengths[0])]).astype(jnp.int32)
    zero = jnp.int32(0)
    scalars = jnp.stack([core, z, upper, anchor, bounds[0] - anchor, bounds[1] - anchor, zero, zero]).astype(jnp.int32)
    both = ("pool", "dp")

    x_rows, bc_rows = in_hbm(x_in[0]), in_hbm(bc_in[0])
    own = jnp.concatenate([core[None], decode_prompt[0, 0]]).astype(jnp.int32)
    packed, halo0, halo1, g_own, d_own, d_other = run_pack(
        own, x_rows, bc_rows, in_hbm(dt_raw[0].T), in_hbm(dec_x[0, 0]), in_hbm(dec_bc[0, 0]), in_hbm(dec_dt[0, 0])
    )
    recv = in_hbm(lax.ppermute(packed, "dp", [(i, i ^ 1) for i in range(count)]))
    g_own = in_hbm(g_own)
    halo = lax.ppermute(halo0, "dp", [(i, i + 1) for i in range(1, count - 1, 2)])
    halo = halo + lax.ppermute(halo1, "dp", [(i, i + 2) for i in range(1, count - 1, 2)])

    def after(value, other):
        return lax.optimization_barrier((value, other))[0]

    dec_rows = STEPS * ROWS
    total = 2 * count

    def hop(value, flip):
        return lax.ppermute(value, both, [(i, ((i + count) % total) ^ flip) for i in range(total)])

    dec_hops = [hop(d_own, 0), hop(d_other, 1), hop(d_own, CORES * RING), hop(d_other, CORES * RING + 1)]

    def z_swap(value, m):
        if m == 0:
            return value
        return lax.ppermute(value, "dp", [(i, i ^ (CORES * m)) for i in range(count)])

    w_group = lax.dynamic_slice_in_dim(conv_w_bc, core * STATE, STATE, 2).reshape(CONV, 2 * STATE)
    b_group = lax.dynamic_slice_in_dim(conv_b_bc, core * STATE, STATE, 1).reshape(1, 2 * STATE)
    rates = -LOG2E * jnp.exp(a_log)
    heads = jnp.stack([dt_bias, rates])
    heads = lax.dynamic_slice_in_dim(heads, core * REP, REP, 1)
    vecs = jnp.pad(jnp.tile(heads, (1, 3)), ((0, 6), (0, LANES - 3 * REP)))
    skip = jnp.repeat(d_skip, HEAD_DIM)[None]
    b_x = conv_b_x[None]

    *ls, xc, bcc, dtc, wc3, cx, cg = run_a(scalars, x_rows, recv, halo, conv_w_x, b_x, g_own, w_group, b_group, vecs)
    sent_ls = [z_swap(part, m) for m, part in enumerate(ls)]
    *fs, local = run_b(scalars, xc, bcc, dtc, skip, cx, cg, dec_hops, 1, 3)
    ls = after(tuple(sent_ls), fs[0])
    state_shape = jax.ShapeDtypeStruct((STATE, CHUNK), BF16)
    half_total = whole_call(kernel_total, state_shape, "half_total", 10**6)(scalars, *ls)
    own_end, local = run_b(scalars, xc, bcc, dtc, skip, cx, cg, after(tuple(dec_hops), half_total), 0, 1, in_hbm(local))
    fs = [z_swap(part, m) for m, part in enumerate([own_end, *fs])]
    local = in_hbm(local)
    start = lax.ppermute(half_total, "dp", [(i, i + CORES * RING) for i in range(CORES * RING)])
    starts = whole_call(kernel_starts, [state_shape] * RING, "chip_starts", 10**6)(scalars, *ls, start)
    starts = [z_swap(part, m) for m, part in enumerate(starts)]

    def own_columns(value):
        return lax.dynamic_slice_in_dim(value, core * GROUP_CH + z * CHUNK, CHUNK, 1)

    def decode(bounds_ref_args):
        shape = jax.ShapeDtypeStruct((RING, 32, CHUNK), BF16)
        args = [*ls, start, *fs, own_columns(conv_w_x), own_columns(b_x), w_group, b_group, vecs, own_columns(skip)]
        return pl.pallas_call(
            kernel_decode,
            in_specs=[pl.BlockSpec(memory_space=pltpu.SMEM)]
            + [pl.BlockSpec(memory_space=pltpu.VMEM)] * len(args)
            + [pl.BlockSpec(memory_space=pltpu.SMEM)],
            out_specs=[pl.BlockSpec(memory_space=pltpu.VMEM)] * 2,
            out_shape=[shape, shape],
            scratch_shapes=[
                pltpu.VMEM((PROMPTS, STATE, CHUNK), F32),
                pltpu.VMEM((RING, 64, 1152), F32),
                pltpu.VMEM((RING, 64, CHUNK), F32),
            ],
            compiler_params=pltpu.CompilerParams(vmem_limit_bytes=14 * MIB),
            cost_estimate=pl.CostEstimate(flops=20 * 10**9, bytes_accessed=6 * 10**6, transcendentals=0),
            name="decode_rows",
        )(scalars, *args, bounds_ref_args)

    kept, sent = after(tuple(decode(bounds)), starts[1])
    other_rows = run_d(scalars, local, bcc, wc3, starts, False)
    other_group = lax.ppermute(other_rows, "dp", [(i, i ^ 1) for i in range(count)])
    straight = lax.ppermute(kept, both, [(i, (i + count) % total) for i in range(total)])
    crossed = lax.ppermute(sent, both, [(i, ((i + count) % total) ^ (CORES * RING)) for i in range(total)])
    answers = after(straight + crossed, other_rows)
    answers = [z_swap(answers[m], m) for m in range(RING)]
    own_group = run_d(scalars, local, bcc, wc3, starts, True)
    answers = after(tuple(answers), own_group)
    columns = [
        functools.reduce(lambda a, m: jnp.where(z == j ^ m, answers[m], a), range(1, RING), answers[0])
        for j in range(RING)
    ]
    answers = jnp.concatenate(columns, axis=1).reshape(STEPS, CORES, ROWS, GROUP_CH)
    first, second = (answers[:, i].reshape(dec_rows, GROUP_CH) for i in range(CORES))
    mine = jnp.where(core == 0, first, second)
    theirs = lax.ppermute(jnp.where(core == 0, second, first), "dp", [(i, i ^ 1) for i in range(count)])
    decoded = jnp.where(core == 0, jnp.concatenate([mine, theirs], axis=1), jnp.concatenate([theirs, mine], axis=1))
    out = put_group(scalars, own_group, other_group)
    return out[None], decoded.reshape(dec_x.shape)


def solution(mesh):
    in_specs = (
        P("pool", "dp", "tp"),
        P("pool", "dp", None, "tp"),
        P("pool", "dp", "tp"),
        P(None, "tp"),
        P("tp"),
        P(None, None, "tp"),
        P(None, "tp"),
        P("tp"),
        P("tp"),
        P("tp"),
        P("pool", None),
        P("pool", "dp", None),
        P("pool", "dp", None, None, "tp"),
        P("pool", "dp", None, None, None, "tp"),
        P("pool", "dp", None, None, "tp"),
    )
    out_specs = (P("pool", "dp", "tp"), P("pool", "dp", None, None, "tp"))
    return jax.shard_map(on_device, mesh=mesh, in_specs=in_specs, out_specs=out_specs, check_vma=False)
```

```python
import functools

import jax
import jax.numpy as jnp
from jax import lax
from jax.experimental import pallas as pl
from jax.experimental.pallas import tpu as pltpu
from jax.sharding import PartitionSpec as P

HEAD_DIM = 64
STATE = 256
CONV = 4
BLOCK = 128
PROMPTS = 3
STEPS = 4
ROWS = 4
CORES = 2
RING = 4
LANES = 128
DEC = STATE + 48
MSG = DEC + 144
SCRATCH_B = 14
REP = 32
CHIP_TOKENS = 512
BLOCKS = CHIP_TOKENS // BLOCK
GROUP_CH = 2048
CHUNK = GROUP_CH // RING
WIDE = GROUP_CH + 1024
LOG2E = 1.4426950408889634
F32 = jnp.float32
BF16 = jnp.bfloat16
MIB = 1024 * 1024


def split3(value):
    high = value.astype(BF16).astype(F32)
    rest = value - high
    middle = rest.astype(BF16).astype(F32)
    return high, middle, rest - middle


def pack3(value):
    high, middle, low = split3(value)
    lane = lax.broadcasted_iota(jnp.int32, value.shape, 1)
    return jnp.where(lane < REP, high, jnp.where(lane < 2 * REP, middle, low)).astype(BF16)


def spread_matrix(chunk):
    lane = lax.broadcasted_iota(jnp.int32, (LANES, CHUNK), 0)
    head = (lax.broadcasted_iota(jnp.int32, (LANES, CHUNK), 1) >> 6) + chunk * (CHUNK // HEAD_DIM)
    hit = ((lane & (REP - 1)) == head) & (lane < 3 * REP)
    return jnp.where(hit, 1.0, 0.0).astype(BF16)


def in_hbm(value):
    return pltpu.with_memory_space_constraint(value, pltpu.HBM)


def mm(a, b):
    return jnp.dot(a, b, preferred_element_type=F32)


def silu(value):
    half = 0.5 * value
    return half + half * jnp.tanh(half)


def softplus(value):
    return jnp.maximum(value, 0.0) + jnp.log1p(jnp.exp(-jnp.abs(value)))


def seg_vec(s_ref, pos):
    anchor, lo0, lo1 = s_ref[3], s_ref[4], s_ref[5]
    seg = (pos >= lo0).astype(jnp.int32) + (pos >= lo1).astype(jnp.int32)
    return jnp.where(pos < -anchor, -1, seg)


def seg_at(s_ref, pos):
    anchor, lo0, lo1 = s_ref[3], s_ref[4], s_ref[5]
    seg = jnp.where(pos >= lo0, 1, 0) + jnp.where(pos >= lo1, 1, 0)
    return jnp.where(pos + anchor < 0, -1, seg)


def rows_of(parts, count, width):
    row = lax.broadcasted_iota(jnp.int32, (count, width), 0)
    out = jnp.zeros((count, width), F32)
    for index, part in enumerate(parts):
        out = jnp.where(row == index, part, out)
    return out


def conv_tile(src, start, lanes, weight, offset, mask):
    tile = src[pl.ds(start, BLOCK + 8), lanes]
    running = jnp.broadcast_to(offset[:, lanes], (BLOCK, LANES))
    for tap in range(CONV - 1):
        moved = pltpu.roll(tile, CONV - 1 - tap, 0)[8:]
        running = running + weight[tap : tap + 1, lanes] * (moved * mask[tap, pl.ds(start, BLOCK), :])
    return silu(running + weight[CONV - 1 : CONV, lanes] * tile[8:])


def cache_rows(s_ref, src, out):
    out[...] = jnp.zeros_like(out)
    for prompt in range(PROMPTS):
        last = (s_ref[4] - 1, s_ref[5] - 1, RING * CORES * CHIP_TOKENS - 1 - s_ref[3])[prompt]

        @pl.when((last >= 0) & (last < CHIP_TOKENS))
        def _():
            for tap in range(CONV - 1):
                row = last - (CONV - 2) + tap
                same = jnp.where(seg_at(s_ref, row) == seg_at(s_ref, last), 1.0, 0.0)
                value = src[pl.ds(row + 8, 1), :]
                out[pl.ds(prompt * 3 + tap, 1), :] = jnp.where(same > 0.5, value, 0.0)


def cut_of(s_ref):
    first, second = s_ref[4] - 1, s_ref[5] - 1
    limit = CHIP_TOKENS - 1
    one = jnp.where((second >= 0) & (second < limit), second, -1)
    return jnp.where((first >= 0) & (first < limit), first, one)


def kernel_a(
    s_ref, x_own, x_rec, halo_x, wx, bx, g_own, g_rec, halo_g, wg, bg, vecs,
    l0, l1, l2, l3, xc_out, bcc_out, dtc_out, wc3_out, cx_out, cg_out,
    xs, gs, mask, wp3, keep3, bt, cache, wide, scaled,
):
    m = pl.program_id(0)
    core = s_ref[0]
    chunk = s_ref[1] ^ m
    first = core == 0
    half = CHIP_TOKENS // 2

    @pl.when(m == 0)
    def _():
        pos = lax.broadcasted_iota(jnp.int32, (CHIP_TOKENS, LANES), 0)
        own_seg = seg_vec(s_ref, pos)
        for tap in range(CONV - 1):
            mask[tap] = jnp.where(seg_vec(s_ref, pos - 3 + tap) == own_seg, 1.0, 0.0)
        gs[0:8] = halo_g[:, 0:512].astype(F32)[8:]
        gs[8 : 8 + half] = jnp.where(first, g_own[:, 0:512], g_rec[:, 0:512]).astype(F32)
        gs[8 + half :] = jnp.where(first, g_rec[:, 0:512], g_own[:, 0:512]).astype(F32)
        weight = wg[...].astype(F32)
        for j in range(BLOCKS):
            for strip in range(4):
                lanes = slice(strip * LANES, (strip + 1) * LANES)
                tile = conv_tile(gs, j * BLOCK, lanes, weight, bg, mask).astype(BF16)
                bcc_out[pl.ds(j * BLOCK, BLOCK), lanes] = tile
                if strip < 2:
                    bt[j, lanes, :] = tile.astype(F32).T.astype(BF16)
        cache_rows(s_ref, gs, cache)
        cg_out[...] = cache[...].astype(BF16)
        raw_a = jnp.where(first, g_own[:, 512:640], g_rec[:, 512:640]).astype(F32)
        raw_b = jnp.where(first, g_rec[:, 512:640], g_own[:, 512:640]).astype(F32)
        dt = softplus(jnp.concatenate([raw_a, raw_b], axis=0) + vecs[0:1])
        decay = dt * vecs[1:2]
        row = lax.broadcasted_iota(jnp.int32, (BLOCK, BLOCK), 0)
        col = lax.broadcasted_iota(jnp.int32, (BLOCK, BLOCK), 1)
        lower = jnp.where(row >= col, 1.0, 0.0).astype(BF16)
        dtc_out[0:CHIP_TOKENS] = dt
        total = jnp.zeros((1, LANES), F32)
        before = seg_at(s_ref, -1)
        keeps = []
        for j in range(BLOCKS):
            rows = slice(j * BLOCK, (j + 1) * BLOCK)
            high, middle, low = split3(decay[rows])
            cum = mm(lower, high.astype(BF16)) + mm(lower, middle.astype(BF16)) + mm(lower, low.astype(BF16))
            dtc_out[CHIP_TOKENS + j * BLOCK : CHIP_TOKENS + (j + 1) * BLOCK] = cum
            end = cum[BLOCK - 1 :]
            end_seg = seg_at(s_ref, (j + 1) * BLOCK - 1)
            weight_p = jnp.where(own_seg[rows] == end_seg, jnp.exp2(end - cum) * dt[rows], 0.0)
            wp3[pl.ds(j * BLOCK, BLOCK), :] = pack3(weight_p)
            reach = jnp.where(own_seg[rows] == before, jnp.exp2(total + cum), 0.0)
            wc3_out[pl.ds(j * BLOCK, BLOCK), :] = pack3(reach)
            keeps.append(jnp.where(seg_at(s_ref, j * BLOCK - 1) == end_seg, jnp.exp2(end), 0.0))
            total = total + end
        keeps.append(jnp.where(before == seg_at(s_ref, CHIP_TOKENS - 1), jnp.exp2(total), 0.0))
        keep3[...] = pack3(rows_of(keeps, 16, LANES))

    xs[0:8] = halo_x[...].astype(F32)[8:]
    xs[8 : 8 + half] = jnp.where(first, x_own[...], x_rec[...]).astype(F32)
    xs[8 + half :] = jnp.where(first, x_rec[...], x_own[...]).astype(F32)
    weight = wx[...].astype(F32)
    spread = spread_matrix(chunk)
    keep = mm(keep3[...], spread)
    for j in range(BLOCKS):
        rows = pl.ds(j * BLOCK, BLOCK)
        wide[...] = mm(wp3[rows, :], spread)
        for strip in range(CHUNK // LANES):
            lanes = slice(strip * LANES, (strip + 1) * LANES)
            xc = conv_tile(xs, j * BLOCK, lanes, weight, bx, mask).astype(BF16)
            xc_out[rows, lanes] = xc
            scaled[rows, lanes] = (xc.astype(F32) * wide[:, lanes]).astype(BF16)
    state = mm(bt[0], scaled[0:BLOCK, :])
    for j in range(1, BLOCKS):
        state = keep[j : j + 1] * state + mm(bt[j], scaled[pl.ds(j * BLOCK, BLOCK), :])
    cache_rows(s_ref, xs, cache)
    cx_out[...] = cache[...].astype(BF16)
    tail = rows_of(split3(keep[BLOCKS : BLOCKS + 1]), 16, CHUNK).astype(BF16)
    for index, out in enumerate((l0, l1, l2, l3)):

        @pl.when(m == index)
        def _():
            out[0:STATE] = state.astype(BF16)
            out[STATE:] = tail


def run_a(scalars, x_in, recv, halo, wx, bx, g_own, wg, bg, vecs):
    def fixed(shape):
        return pl.BlockSpec(shape, lambda m, s: (0,) * len(shape))

    def chunked(rows, per_core=0):
        return pl.BlockSpec((rows, CHUNK), lambda m, s: (0, s[0] * per_core + (s[1] ^ m)))

    half = CHIP_TOKENS // 2
    side = pl.BlockSpec((half, 1024), lambda m, s: (0, 2))
    return pl.pallas_call(
        kernel_a,
        grid_spec=pltpu.PrefetchScalarGridSpec(
            num_scalar_prefetch=1,
            grid=(RING,),
            in_specs=[
                chunked(half, RING), chunked(half), chunked(16), chunked(CONV, RING), chunked(1, RING),
                fixed((half, 1024)), side, pl.BlockSpec((16, 1024), lambda m, s: (0, 2)),
                fixed((CONV, 512)), fixed((1, 512)), fixed((8, LANES)),
            ],
            out_specs=[fixed((STATE + 16, CHUNK))] * RING + [
                chunked(CHIP_TOKENS), fixed((CHIP_TOKENS, 512)), fixed((2 * CHIP_TOKENS, LANES)),
                fixed((CHIP_TOKENS, LANES)), chunked(16), fixed((16, 512)),
            ],
            scratch_shapes=[
                pltpu.VMEM((CHIP_TOKENS + 8, CHUNK), F32),
                pltpu.VMEM((CHIP_TOKENS + 8, 512), F32),
                pltpu.VMEM((CONV - 1, CHIP_TOKENS, LANES), F32),
                pltpu.VMEM((CHIP_TOKENS, LANES), BF16),
                pltpu.VMEM((16, LANES), BF16),
                pltpu.VMEM((BLOCKS, STATE, BLOCK), BF16),
                pltpu.VMEM((16, CHUNK), F32),
                pltpu.VMEM((BLOCK, CHUNK), F32),
                pltpu.VMEM((CHIP_TOKENS, CHUNK), BF16),
            ],
        ),
        out_shape=[jax.ShapeDtypeStruct((STATE + 16, CHUNK), BF16)] * RING + [
            jax.ShapeDtypeStruct((CHIP_TOKENS, GROUP_CH), BF16),
            jax.ShapeDtypeStruct((CHIP_TOKENS, 512), BF16),
            jax.ShapeDtypeStruct((2 * CHIP_TOKENS, LANES), F32),
            jax.ShapeDtypeStruct((CHIP_TOKENS, LANES), BF16),
            jax.ShapeDtypeStruct((16, GROUP_CH), BF16),
            jax.ShapeDtypeStruct((16, 512), BF16),
        ],
        compiler_params=pltpu.CompilerParams(vmem_limit_bytes=16 * MIB),
        cost_estimate=pl.CostEstimate(flops=6 * 10**9, bytes_accessed=8 * 10**6, transcendentals=10**6),
        name="conv_and_states",
    )(scalars, x_in, recv, halo, wx, bx, g_own, recv, halo, wg, bg, vecs)


def kernel_b(
    base, count, s_ref, xc_ref, bcc, dtc, skip, cx, cg, near_same, near_cross, far_same, far_cross, *rest
):
    *outs, local_out = rest[-SCRATCH_B - count - 1 : -SCRATCH_B]
    (wp3, wb3, keep3, bt, gm, cum_t, dt_t, wf3, wide, reach, carried, scaled, parts, dec_rows) = rest[-SCRATCH_B:]
    m = pl.program_id(0) + base
    chunk = s_ref[1] ^ m
    cut = cut_of(s_ref)
    cut_block = cut // BLOCK

    @pl.when(m == base)
    def _():
        pos = lax.broadcasted_iota(jnp.int32, (BLOCK, LANES), 0)
        row = lax.broadcasted_iota(jnp.int32, (BLOCK, BLOCK), 0)
        col = lax.broadcasted_iota(jnp.int32, (BLOCK, BLOCK), 1)
        total = jnp.zeros((1, LANES), F32)
        before = seg_at(s_ref, -1)
        keeps = []
        cut_keep = jnp.zeros((1, LANES), F32)
        cut_reach = jnp.zeros((1, LANES), F32)
        cut_row = dtc[pl.ds(CHIP_TOKENS + jnp.maximum(cut, 0), 1), :]
        cut_seg = seg_at(s_ref, cut)
        wf3[...] = jnp.zeros_like(wf3)
        for j in range(BLOCKS):
            dt = dtc[j * BLOCK : (j + 1) * BLOCK]
            cum = dtc[CHIP_TOKENS + j * BLOCK : CHIP_TOKENS + (j + 1) * BLOCK]
            end = cum[BLOCK - 1 :]
            seg = seg_vec(s_ref, pos + j * BLOCK)
            end_seg = seg_at(s_ref, (j + 1) * BLOCK - 1)
            prev_seg = seg_at(s_ref, j * BLOCK - 1)
            wp3[pl.ds(j * BLOCK, BLOCK), :] = pack3(jnp.where(seg == end_seg, jnp.exp2(end - cum) * dt, 0.0))
            wb3[pl.ds(j * BLOCK, BLOCK), :] = pack3(jnp.where(seg == prev_seg, jnp.exp2(cum), 0.0))
            keeps.append(jnp.where(prev_seg == end_seg, jnp.exp2(end), 0.0))
            b_rows = bcc[pl.ds(j * BLOCK, BLOCK), 0:STATE]
            c_rows = bcc[pl.ds(j * BLOCK, BLOCK), STATE : 2 * STATE]
            b_t = b_rows.astype(F32).T.astype(BF16)
            bt[j] = b_t
            scores = mm(c_rows, b_t)
            same = seg_vec(s_ref, row + j * BLOCK) == seg_vec(s_ref, col + j * BLOCK)
            gm[j] = jnp.where((row >= col) & same, scores, 0.0)
            cum_t[j] = cum.T
            dt_t[j] = dt.T
            here = cut_block == j
            cut_keep = jnp.where(here & (cut_seg == prev_seg), jnp.exp2(cut_row), cut_keep)
            cut_reach = jnp.where(here & (cut_seg == before), jnp.exp2(total + cut_row), cut_reach)

            @pl.when((cut >= 0) & here)
            def _():
                chosen = (seg == cut_seg) & (pos + j * BLOCK <= cut)
                wf3[...] = pack3(jnp.where(chosen, jnp.exp2(jnp.minimum(cut_row - cum, 0.0)) * dt, 0.0))

            total = total + end
        keep3[...] = pack3(rows_of(keeps + [cut_keep, cut_reach], 16, LANES))
        core, upper = s_ref[0], s_ref[2]
        for top in range(2):
            for source in range(CORES):
                near = jnp.where(core == source, near_same[...], near_cross[...])
                far = jnp.where(core == source, far_same[...], far_cross[...])
                value = jnp.where(upper == top, near, far).astype(F32)
                for step in range(STEPS):
                    at = 32 * top + 8 * step + ROWS * source
                    dec_rows[at : at + ROWS, :] = value[ROWS * step : ROWS * step + ROWS, :]

    spread = spread_matrix(chunk)
    keep = mm(keep3[...], spread)
    half_lane = lax.broadcasted_iota(jnp.int32, (BLOCK, LANES), 1) < HEAD_DIM
    for index, out in enumerate(outs):

        @pl.when(m == base + index)
        def _():
            out[0:STATE] = jnp.zeros((STATE, CHUNK), BF16)
            out[STATE : STATE + 16] = rows_of(split3(keep[BLOCKS + 1 : BLOCKS + 2]), 16, CHUNK).astype(BF16)
            out[STATE + 16 : STATE + 32] = cx[...]
            out[STATE + 32 : STATE + 48] = cg[...]
            at = pl.multiple_of(chunk * CHUNK, CHUNK)
            out[DEC : DEC + 64] = dec_rows[:, pl.ds(at, CHUNK)].astype(BF16)
            out[DEC + 64 : DEC + 128] = dec_rows[:, GROUP_CH : GROUP_CH + 512].astype(BF16)
            for part in range(4):
                steps = dec_rows[16 * part : 16 * part + 16, GROUP_CH + 512 : GROUP_CH + 640]
                out[DEC + 128 : DEC + 144, part * LANES : (part + 1) * LANES] = steps.astype(BF16)

    state = None
    pairs = CHUNK // LANES
    heads = chunk * (CHUNK // HEAD_DIM)
    heads_tile = pl.ds(pl.multiple_of(heads, 8), 8)
    for j in range(BLOCKS):
        rows = slice(j * BLOCK, (j + 1) * BLOCK)
        if j > 0:
            high = state.astype(BF16)
            parts[0:STATE] = high
            parts[STATE:] = (state - high.astype(F32)).astype(BF16)
            c_rows = bcc[rows, STATE : 2 * STATE]
            carried[...] = mm(jnp.concatenate([c_rows, c_rows], axis=1), parts[...])
            reach[...] = mm(wb3[rows], spread)

        @pl.when((cut >= 0) & (cut_block == j))
        def _():
            wide[...] = mm(wf3[...], spread)
            fresh = mm(bt[j], (xc_ref[rows].astype(F32) * wide[...]).astype(BF16))
            if j > 0:
                fresh = keep[BLOCKS : BLOCKS + 1] * state + fresh
            for index, out in enumerate(outs):

                @pl.when(m == base + index)
                def _():
                    out[0:STATE] = fresh.astype(BF16)

        if j < BLOCKS - 1:
            wide[...] = mm(wp3[rows], spread)
            for pair in range(pairs):
                lanes = slice(pair * LANES, (pair + 1) * LANES)
                scaled[:, lanes] = (xc_ref[rows, lanes].astype(F32) * wide[:, lanes]).astype(BF16)
            fresh = mm(bt[j], scaled[...])
            state = fresh if j == 0 else keep[j : j + 1] * state + fresh
        cum = dtc[CHIP_TOKENS + j * BLOCK : CHIP_TOKENS + (j + 1) * BLOCK]
        turned = pltpu.roll(cum, LANES - heads, 1)
        cum_rows = cum_t[j, heads_tile, :]
        dt_rows = dt_t[j, heads_tile, :]
        for pair in range(pairs):
            weights = []
            for head in (2 * pair, 2 * pair + 1):
                gap = jnp.minimum(turned[:, head : head + 1] - cum_rows[head : head + 1], 0.0)
                weights.append((jnp.exp2(gap) * (gm[j] * dt_rows[head : head + 1])).astype(BF16))
            lanes = slice(pair * LANES, (pair + 1) * LANES)
            two = xc_ref[rows, lanes]
            zero = jnp.zeros_like(two)
            stacked = jnp.concatenate([jnp.where(half_lane, two, zero), jnp.where(half_lane, zero, two)], axis=0)
            value = mm(jnp.concatenate(weights, axis=1), stacked) + skip[:, lanes] * two.astype(F32)
            if j > 0:
                value = value + reach[:, lanes] * carried[:, lanes]
            local_out[rows, lanes] = value


def run_b(scalars, xc, bcc, dtc, skip, cx, cg, dec_hops, base, count, local=None):
    def fixed(shape):
        return pl.BlockSpec(shape, lambda m, s: (0,) * len(shape))

    def chunked(rows, per_core=0):
        return pl.BlockSpec((rows, CHUNK), lambda m, s: (0, s[0] * per_core + (s[1] ^ (m + base))))

    args = [scalars, xc, bcc, dtc, skip, cx, cg, *dec_hops]
    in_specs = [
        chunked(CHIP_TOKENS), fixed((CHIP_TOKENS, 512)), fixed((2 * CHIP_TOKENS, LANES)),
        chunked(1, RING), chunked(16), fixed((16, 512)),
    ] + [fixed((16, WIDE))] * 4
    aliases = {}
    if local is not None:
        aliases = {len(args): count}
        args.append(local)
        in_specs.append(pl.BlockSpec(memory_space=pl.ANY))
    scratch = [
        pltpu.VMEM((CHIP_TOKENS, LANES), BF16),
        pltpu.VMEM((CHIP_TOKENS, LANES), BF16),
        pltpu.VMEM((16, LANES), BF16),
        pltpu.VMEM((BLOCKS, STATE, BLOCK), BF16),
        pltpu.VMEM((BLOCKS, BLOCK, BLOCK), F32),
        pltpu.VMEM((BLOCKS, LANES, BLOCK), F32),
        pltpu.VMEM((BLOCKS, LANES, BLOCK), F32),
        pltpu.VMEM((BLOCK, LANES), BF16),
        pltpu.VMEM((BLOCK, CHUNK), F32),
        pltpu.VMEM((BLOCK, CHUNK), F32),
        pltpu.VMEM((BLOCK, CHUNK), F32),
        pltpu.VMEM((BLOCK, CHUNK), BF16),
        pltpu.VMEM((2 * STATE, CHUNK), BF16),
        pltpu.VMEM((64, WIDE), F32),
    ]
    assert len(scratch) == SCRATCH_B
    return pl.pallas_call(
        functools.partial(kernel_b, base, count),
        grid_spec=pltpu.PrefetchScalarGridSpec(
            num_scalar_prefetch=1,
            grid=(count,),
            in_specs=in_specs,
            out_specs=[fixed((MSG, CHUNK))] * count + [chunked(CHIP_TOKENS)],
            scratch_shapes=scratch,
        ),
        out_shape=[jax.ShapeDtypeStruct((MSG, CHUNK), BF16)] * count + [pltpu.HBM((CHIP_TOKENS, GROUP_CH), F32)],
        input_output_aliases=aliases,
        compiler_params=pltpu.CompilerParams(vmem_limit_bytes=14 * MIB),
        cost_estimate=pl.CostEstimate(
            flops=3 * count * 10**9, bytes_accessed=2 * count * 10**6, transcendentals=count * 10**5
        ),
        name=f"output_within_chip_{base}",
    )(*args)


def pick(refs, which, rows):
    out = refs[0][rows]
    for index in range(1, len(refs)):
        out = jnp.where(which == index, refs[index][rows], out)
    return out.astype(F32)


def decay_rows(tile):
    return tile[0:1] + tile[1:2] + tile[2:3]


def kernel_total(s_ref, l0, l1, l2, l3, total_out):
    state = jnp.zeros((STATE, CHUNK), F32)
    for chip in range(RING):
        which = s_ref[1] ^ chip
        part = pick((l0, l1, l2, l3), which, slice(0, STATE))
        factor = decay_rows(pick((l0, l1, l2, l3), which, slice(STATE, STATE + 16)))
        state = factor * state + part
    total_out[...] = state.astype(BF16)


def kernel_starts(s_ref, l0, l1, l2, l3, start, r0, r1, r2, r3):
    state = start[...].astype(F32)
    for chip in range(RING):
        which = s_ref[1] ^ chip
        for index, out in enumerate((r0, r1, r2, r3)):

            @pl.when(which == index)
            def _():
                out[...] = state.astype(BF16)

        if chip < RING - 1:
            part = pick((l0, l1, l2, l3), which, slice(0, STATE))
            factor = decay_rows(pick((l0, l1, l2, l3), which, slice(STATE, STATE + 16)))
            state = factor * state + part


def whole_call(kernel, out_shape, name, flops, scratch=()):
    def run(scalars, *args):
        return pl.pallas_call(
            kernel,
            in_specs=[pl.BlockSpec(memory_space=pltpu.SMEM)] + [pl.BlockSpec(memory_space=pltpu.VMEM)] * len(args),
            out_specs=jax.tree.map(lambda _: pl.BlockSpec(memory_space=pltpu.VMEM), out_shape),
            out_shape=out_shape,
            scratch_shapes=list(scratch),
            compiler_params=pltpu.CompilerParams(vmem_limit_bytes=8 * MIB),
            cost_estimate=pl.CostEstimate(flops=flops, bytes_accessed=3 * 10**6, transcendentals=0),
            name=name,
        )(scalars, *args)

    return run


def kernel_decode(
    s_ref, l0, l1, l2, l3, start, f0, f1, f2, f3,
    wx, bx, wg, bg, vecs, skip, bounds,
    keep_out, send_out,
    final, rows_f32, result,
):
    z, upper = s_ref[1], s_ref[2]
    ls, fs = (l0, l1, l2, l3), (f0, f1, f2, f3)
    first, second = bounds[0, 0], bounds[0, 0] + bounds[0, 1]
    lasts = [first - 1, second - 1, second + bounds[0, 2] - 1]
    final[...] = jnp.zeros_like(final)
    state = start[...].astype(F32)
    for chip in range(RING):
        which = z ^ chip
        origin = (upper * RING + chip) * CHIP_TOKENS
        part = pick(ls, which, slice(0, STATE))
        factor = decay_rows(pick(ls, which, slice(STATE, STATE + 16)))
        after = factor * state + part
        for q in range(PROMPTS):
            local = lasts[q] - origin

            @pl.when(local == CHIP_TOKENS - 1)
            def _():
                final[q] = after

            @pl.when((local >= 0) & (local < CHIP_TOKENS - 1))
            def _():
                fresh = pick(fs, which, slice(0, STATE))
                reach = decay_rows(pick(fs, which, slice(STATE, STATE + 16)))
                final[q] = fresh + reach * state

        state = after
    cache_x = sum(f[STATE + 16 : STATE + 32].astype(F32) for f in fs)
    cache_g = sum(f[STATE + 32 : STATE + 48].astype(F32) for f in fs)
    spread = spread_matrix(z)
    for index, f in enumerate(fs):
        rows_f32[index, :, 0:CHUNK] = f[DEC : DEC + 64].astype(F32)
        rows_f32[index, :, CHUNK : CHUNK + 512] = f[DEC + 64 : DEC + 128].astype(F32)
        for part in range(4):
            steps = f[DEC + 128 : DEC + 144, part * LANES : (part + 1) * LANES].astype(F32)
            rows_f32[index, 16 * part : 16 * part + 16, CHUNK + 512 :] = steps

    def step_rows(step, lanes):
        tiles = [
            rows_f32[index, 32 * side + 8 * step : 32 * side + 8 * step + 8, lanes]
            for index in range(RING)
            for side in range(2)
        ]
        return jnp.concatenate(tiles, axis=0)

    prompt = step_rows(0, slice(1024, 1152))[:, 96:97]
    chosen = [prompt == float(q) for q in range(PROMPTS)]
    mine = jnp.zeros_like(prompt)
    for q in range(PROMPTS):
        inside = jnp.where(lasts[q] // (RING * CHIP_TOKENS) == upper, 1.0, 0.0)
        mine = jnp.where(chosen[q], inside, mine)

    def window(cache, lanes):
        rows = []
        for tap in range(CONV - 1):
            row = jnp.zeros((STEPS * 16, CHUNK), F32)
            for q in range(PROMPTS):
                row = jnp.where(chosen[q], cache[3 * q + tap : 3 * q + tap + 1], row)
            rows.append(row)
        return rows + [step_rows(step, lanes) for step in range(STEPS)]

    def convolved(rows, weight, offset):
        out = []
        for step in range(STEPS):
            running = jnp.broadcast_to(offset, rows[0].shape)
            for tap in range(CONV):
                running = running + weight[tap : tap + 1] * rows[step + tap]
            out.append(silu(running).astype(BF16))
        return out

    mixed = convolved(window(cache_x, slice(0, 512)), wx[...].astype(F32), bx[...])
    both = convolved(window(cache_g, slice(512, 1024)), wg[...].astype(F32), bg[...])
    steps, fades = [], []
    fade = jnp.zeros((STEPS * 16, LANES), F32)
    for step in range(STEPS):
        dt = softplus(step_rows(step, slice(1024, 1152)) + vecs[0:1])
        fade = fade + dt * vecs[1:2]
        steps.append(dt)
        fades.append(fade)
    readers = jnp.concatenate([rows[:, STATE:] for rows in both], axis=0)
    readout = jnp.zeros((STEPS * STEPS * 16, CHUNK), F32)
    for q in range(PROMPTS):
        high = final[q].astype(BF16)
        low = (final[q] - high.astype(F32)).astype(BF16)
        value = mm(readers, high) + mm(readers, low)
        readout = jnp.where(jnp.concatenate([chosen[q]] * STEPS, axis=0), value, readout)
    for step in range(STEPS):
        mixed_now = mixed[step].astype(F32)
        total = readout[64 * step : 64 * step + 64] * mm(pack3(jnp.exp2(fades[step])), spread)
        total = total + skip[...] * mixed_now
        reader = both[step][:, STATE:].astype(F32)
        for past in range(step + 1):
            weight = steps[past]
            if past < step:
                weight = weight * jnp.exp2(fades[step] - fades[past])
            product = jnp.sum(reader * both[past][:, 0:STATE].astype(F32), axis=1, keepdims=True)
            total = total + mm(pack3(weight), spread) * (product * mixed[past].astype(F32))
        total = jnp.where(mine > 0.5, total, 0.0)
        for index in range(RING):
            for side in range(2):
                tile = total[8 * (2 * index + side) : 8 * (2 * index + side) + 8]
                result[index, 32 * side + 8 * step : 32 * side + 8 * step + 8, :] = tile
    for index in range(RING):
        keep_out[index] = result[index, pl.ds(pl.multiple_of(32 * upper, 32), 32), :].astype(BF16)
        send_out[index] = result[index, pl.ds(pl.multiple_of(32 * (1 - upper), 32), 32), :].astype(BF16)


def kernel_d(s_ref, local, c_rows, wc3, r0, r1, r2, r3, out):
    z = s_ref[1]
    block = (z >> 1) ^ pl.program_id(0)
    for side in range(2):
        chunk = 2 * block + side
        spread = spread_matrix(chunk)
        for index, r in enumerate((r0, r1, r2, r3)):

            @pl.when((chunk ^ z) == index)
            def _():
                for part in range(2):
                    lanes = slice(part * 256, (part + 1) * 256)
                    to = slice(side * CHUNK + part * 256, side * CHUNK + (part + 1) * 256)
                    factor = mm(wc3[...], spread[:, lanes])
                    out[:, to] = (local[:, to] + factor * mm(c_rows[...], r[:, lanes])).astype(BF16)


def run_d(scalars, local, bcc, wc3, starts, own):
    half = CHIP_TOKENS // 2

    def row(s):
        return s[0] if own else 1 - s[0]

    width = CORES * GROUP_CH if own else GROUP_CH
    return pl.pallas_call(
        kernel_d,
        grid_spec=pltpu.PrefetchScalarGridSpec(
            num_scalar_prefetch=1,
            grid=(2,),
            in_specs=[
                pl.BlockSpec((half, 2 * CHUNK), lambda m, s: (row(s), (s[1] >> 1) ^ m)),
                pl.BlockSpec((half, STATE), lambda m, s: (row(s), 1)),
                pl.BlockSpec((half, LANES), lambda m, s: (row(s), 0)),
            ] + [pl.BlockSpec((STATE, CHUNK), lambda m, s: (0, 0))] * RING,
            out_specs=pl.BlockSpec((half, 2 * CHUNK), lambda m, s: (0, (s[0] * 2 if own else 0) + ((s[1] >> 1) ^ m))),
        ),
        out_shape=jax.ShapeDtypeStruct((half, width), BF16),
        compiler_params=pltpu.CompilerParams(vmem_limit_bytes=12 * MIB),
        cost_estimate=pl.CostEstimate(flops=10**9, bytes_accessed=4 * 10**6, transcendentals=0),
        name="carried_own" if own else "carried_other",
    )(scalars, local, bcc, wc3, *starts)


def kernel_put(s_ref, part, whole, out):
    out[...] = part[...]


def put_group(scalars, whole, part):
    half = CHIP_TOKENS // 2
    return pl.pallas_call(
        kernel_put,
        grid_spec=pltpu.PrefetchScalarGridSpec(
            num_scalar_prefetch=1,
            grid=(2,),
            in_specs=[
                pl.BlockSpec((half, GROUP_CH // 2), lambda m, s: (0, m)),
                pl.BlockSpec(memory_space=pl.ANY),
            ],
            out_specs=pl.BlockSpec((half, GROUP_CH // 2), lambda m, s: (0, (1 - s[0]) * 2 + m)),
        ),
        out_shape=jax.ShapeDtypeStruct(whole.shape, BF16),
        input_output_aliases={2: 0},
        compiler_params=pltpu.CompilerParams(vmem_limit_bytes=4 * MIB),
        cost_estimate=pl.CostEstimate(flops=0, bytes_accessed=2 * 10**6, transcendentals=0),
        name="put_group",
    )(scalars, part, whole)


def head_copies(group):
    lane = lax.broadcasted_iota(jnp.int32, (64, LANES), 1)
    head = lax.broadcasted_iota(jnp.int32, (64, LANES), 0)
    hit = ((lane & (REP - 1)) + group * REP == head) & (lane < 3 * REP)
    return jnp.where(hit, 1.0, 0.0).astype(BF16)


def kernel_pack(s_ref, x, bc, dt_t, x_last, bc_last, dx, dbc, ddt, send, halo0, halo1, side, d_own, d_other, rows_f32):
    core = s_ref[0]
    first = core == 0
    rows = x.shape[0]
    start = pl.multiple_of(pl.program_id(0) * rows, rows)
    dt = dt_t[:, pl.ds(start, rows)].astype(F32).T.astype(BF16)
    b_rows, c_rows = bc[:, 0, :], bc[:, 1, :]
    send[:, 0:GROUP_CH] = x[...]
    for target, group, offset in ((send, 1 - core, GROUP_CH), (side, core, 0)):
        low = group == 0
        target[:, offset : offset + STATE] = jnp.where(low, b_rows[:, 0:STATE], b_rows[:, STATE:])
        target[:, offset + STATE : offset + 2 * STATE] = jnp.where(low, c_rows[:, 0:STATE], c_rows[:, STATE:])
        target[:, offset + 512 : offset + 640] = mm(dt, head_copies(group)).astype(BF16)
        target[:, offset + 640 : offset + 1024] = jnp.zeros((rows, 384), BF16)

    @pl.when(pl.program_id(0) == 0)
    def _():
        b_last, c_last = bc_last[:, 0, :], bc_last[:, 1, :]
        for group, halo in ((0, halo0), (1, halo1)):
            halo[:, 0:GROUP_CH] = x_last[:, group * GROUP_CH : (group + 1) * GROUP_CH]
            halo[:, GROUP_CH : GROUP_CH + STATE] = b_last[:, group * STATE : (group + 1) * STATE]
            halo[:, GROUP_CH + STATE : GROUP_CH + 512] = c_last[:, group * STATE : (group + 1) * STATE]
            halo[:, GROUP_CH + 512 :] = jnp.zeros((16, 512), BF16)
        lane = lax.broadcasted_iota(jnp.int32, (ROWS, LANES), 1)
        row = lax.broadcasted_iota(jnp.int32, (ROWS, LANES), 0)
        prompt = jnp.zeros((ROWS, LANES), F32)
        for r in range(ROWS):
            prompt = jnp.where(row == r, s_ref[1 + r].astype(F32), prompt)
        for out, group in ((d_own, core), (d_other, 1 - core)):
            low = group == 0
            rows_f32[...] = jnp.zeros_like(rows_f32)
            for step in range(STEPS):
                at = slice(ROWS * step, ROWS * step + ROWS)
                value = dx[step].astype(F32)
                rows_f32[at, 0:GROUP_CH] = jnp.where(low, value[:, 0:GROUP_CH], value[:, GROUP_CH:])
                for part in range(2):
                    value = dbc[step, :, part, :].astype(F32)
                    to = GROUP_CH + part * STATE
                    rows_f32[at, to : to + STATE] = jnp.where(low, value[:, 0:STATE], value[:, STATE:])
                steps = mm(ddt[step], head_copies(group))
                rows_f32[at, GROUP_CH + 512 : GROUP_CH + 640] = jnp.where(lane < 3 * REP, steps, prompt)
            out[...] = rows_f32[...].astype(BF16)


def run_pack(scalars, x, bc, dt_t, dx, dbc, ddt):
    rows = x.shape[0]
    tile = rows // 2
    last = rows // 16 - 1
    small = (16, WIDE)

    def fixed(shape):
        return pl.BlockSpec(shape, lambda i, s: (0,) * len(shape))

    return pl.pallas_call(
        kernel_pack,
        grid_spec=pltpu.PrefetchScalarGridSpec(
            num_scalar_prefetch=1,
            grid=(2,),
            in_specs=[
                pl.BlockSpec((tile, GROUP_CH), lambda i, s: (i, 1 - s[0])),
                pl.BlockSpec((tile, 2, 512), lambda i, s: (i, 0, 0)),
                fixed(dt_t.shape),
                pl.BlockSpec((16, CORES * GROUP_CH), lambda i, s: (last, 0)),
                pl.BlockSpec((16, 2, 512), lambda i, s: (last, 0, 0)),
                fixed(dx.shape),
                fixed(dbc.shape),
                fixed(ddt.shape),
            ],
            out_specs=[
                pl.BlockSpec((tile, WIDE), lambda i, s: (i, 0)),
                fixed(small),
                fixed(small),
                pl.BlockSpec((tile, 1024), lambda i, s: (i, 0)),
                fixed(small),
                fixed(small),
            ],
            scratch_shapes=[pltpu.VMEM(small, F32)],
        ),
        out_shape=[pltpu.HBM(shape, BF16) for shape in ((rows, WIDE), small, small, (rows, 1024), small, small)],
        compiler_params=pltpu.CompilerParams(vmem_limit_bytes=12 * MIB),
        cost_estimate=pl.CostEstimate(flops=10**6, bytes_accessed=4 * 10**6, transcendentals=0),
        name="pack",
    )(scalars, x, bc, dt_t, x, bc, dx, dbc, ddt)


def on_device(
    x_in, bc_in, dt_raw, conv_w_x, conv_b_x, conv_w_bc, conv_b_bc, dt_bias, a_log, d_skip,
    lengths, decode_prompt, dec_x, dec_bc, dec_dt,
):
    count = lax.axis_size("dp")
    place = lax.axis_index("dp")
    core = place % CORES
    z = (place // CORES) % RING
    upper = place // (CORES * RING)
    anchor = (place // CORES) * CHIP_TOKENS
    bounds = (lengths[0, 0], lengths[0, 0] + lengths[0, 1])
    zero = jnp.int32(0)
    scalars = jnp.stack([core, z, upper, anchor, bounds[0] - anchor, bounds[1] - anchor, zero, zero]).astype(jnp.int32)
    both = ("pool", "dp")

    x_rows, bc_rows = in_hbm(x_in[0]), in_hbm(bc_in[0])
    own = jnp.concatenate([core[None], decode_prompt[0, 0]]).astype(jnp.int32)
    packed, halo0, halo1, g_own, d_own, d_other = run_pack(
        own, x_rows, bc_rows, in_hbm(dt_raw[0].T), in_hbm(dec_x[0, 0]), in_hbm(dec_bc[0, 0]), in_hbm(dec_dt[0, 0])
    )
    recv = in_hbm(lax.ppermute(packed, "dp", [(i, i ^ 1) for i in range(count)]))
    g_own = in_hbm(g_own)
    halo = lax.ppermute(halo0, "dp", [(i, i + 1) for i in range(1, count - 1, 2)])
    halo = halo + lax.ppermute(halo1, "dp", [(i, i + 2) for i in range(1, count - 1, 2)])

    def after(value, other):
        return lax.optimization_barrier((value, other))[0]

    dec_rows = STEPS * ROWS
    total = 2 * count

    def hop(value, flip):
        return lax.ppermute(value, both, [(i, ((i + count) % total) ^ flip) for i in range(total)])

    dec_hops = [hop(d_own, 0), hop(d_other, 1), hop(d_own, CORES * RING), hop(d_other, CORES * RING + 1)]

    def z_swap(value, m):
        if m == 0:
            return value
        return lax.ppermute(value, "dp", [(i, i ^ (CORES * m)) for i in range(count)])

    w_group = lax.dynamic_slice_in_dim(conv_w_bc, core * STATE, STATE, 2).reshape(CONV, 2 * STATE)
    b_group = lax.dynamic_slice_in_dim(conv_b_bc, core * STATE, STATE, 1).reshape(1, 2 * STATE)
    rates = -LOG2E * jnp.exp(a_log)
    heads = jnp.stack([dt_bias, rates])
    heads = lax.dynamic_slice_in_dim(heads, core * REP, REP, 1)
    vecs = jnp.pad(jnp.tile(heads, (1, 3)), ((0, 6), (0, LANES - 3 * REP)))
    skip = jnp.repeat(d_skip, HEAD_DIM)[None]
    b_x = conv_b_x[None]

    *ls, xc, bcc, dtc, wc3, cx, cg = run_a(scalars, x_rows, recv, halo, conv_w_x, b_x, g_own, w_group, b_group, vecs)
    sent_ls = [z_swap(part, m) for m, part in enumerate(ls)]
    *fs, local = run_b(scalars, xc, bcc, dtc, skip, cx, cg, dec_hops, 1, 3)
    ls = after(tuple(sent_ls), fs[0])
    state_shape = jax.ShapeDtypeStruct((STATE, CHUNK), BF16)
    half_total = whole_call(kernel_total, state_shape, "half_total", 10**6)(scalars, *ls)
    own_end, local = run_b(scalars, xc, bcc, dtc, skip, cx, cg, after(tuple(dec_hops), half_total), 0, 1, in_hbm(local))
    fs = [z_swap(part, m) for m, part in enumerate([own_end, *fs])]
    local = in_hbm(local)
    start = lax.ppermute(half_total, "dp", [(i, i + CORES * RING) for i in range(CORES * RING)])
    starts = whole_call(kernel_starts, [state_shape] * RING, "chip_starts", 10**6)(scalars, *ls, start)
    starts = [z_swap(part, m) for m, part in enumerate(starts)]

    def own_columns(value):
        return lax.dynamic_slice_in_dim(value, core * GROUP_CH + z * CHUNK, CHUNK, 1)

    def decode(bounds_ref_args):
        shape = jax.ShapeDtypeStruct((RING, 32, CHUNK), BF16)
        args = [*ls, start, *fs, own_columns(conv_w_x), own_columns(b_x), w_group, b_group, vecs, own_columns(skip)]
        return pl.pallas_call(
            kernel_decode,
            in_specs=[pl.BlockSpec(memory_space=pltpu.SMEM)]
            + [pl.BlockSpec(memory_space=pltpu.VMEM)] * len(args)
            + [pl.BlockSpec(memory_space=pltpu.SMEM)],
            out_specs=[pl.BlockSpec(memory_space=pltpu.VMEM)] * 2,
            out_shape=[shape, shape],
            scratch_shapes=[
                pltpu.VMEM((PROMPTS, STATE, CHUNK), F32),
                pltpu.VMEM((RING, 64, 1152), F32),
                pltpu.VMEM((RING, 64, CHUNK), F32),
            ],
            compiler_params=pltpu.CompilerParams(vmem_limit_bytes=14 * MIB),
            cost_estimate=pl.CostEstimate(flops=20 * 10**9, bytes_accessed=6 * 10**6, transcendentals=0),
            name="decode_rows",
        )(scalars, *args, bounds_ref_args)

    kept, sent = after(tuple(decode(lengths.astype(jnp.int32))), starts[1])
    other_rows = run_d(scalars, local, bcc, wc3, starts, False)
    other_group = lax.ppermute(other_rows, "dp", [(i, i ^ 1) for i in range(count)])
    straight = lax.ppermute(kept, both, [(i, (i + count) % total) for i in range(total)])
    crossed = lax.ppermute(sent, both, [(i, ((i + count) % total) ^ (CORES * RING)) for i in range(total)])
    answers = after(straight + crossed, other_rows)
    answers = [z_swap(answers[m], m) for m in range(RING)]
    own_group = run_d(scalars, local, bcc, wc3, starts, True)
    answers = after(tuple(answers), own_group)
    columns = [
        functools.reduce(lambda a, m: jnp.where(z == j ^ m, answers[m], a), range(1, RING), answers[0])
        for j in range(RING)
    ]
    answers = jnp.concatenate(columns, axis=1).reshape(STEPS, CORES, ROWS, GROUP_CH)
    first, second = (answers[:, i].reshape(dec_rows, GROUP_CH) for i in range(CORES))
    mine = jnp.where(core == 0, first, second)
    theirs = lax.ppermute(jnp.where(core == 0, second, first), "dp", [(i, i ^ 1) for i in range(count)])
    out = put_group(scalars, own_group, other_group)
    theirs = after(theirs, out)
    decoded = jnp.where(core == 0, jnp.concatenate([mine, theirs], axis=1), jnp.concatenate([theirs, mine], axis=1))
    return out[None], decoded.reshape(dec_x.shape)


def solution(mesh):
    in_specs = (
        P("pool", "dp", "tp"),
        P("pool", "dp", None, "tp"),
        P("pool", "dp", "tp"),
        P(None, "tp"),
        P("tp"),
        P(None, None, "tp"),
        P(None, "tp"),
        P("tp"),
        P("tp"),
        P("tp"),
        P("pool", None),
        P("pool", "dp", None),
        P("pool", "dp", None, None, "tp"),
        P("pool", "dp", None, None, None, "tp"),
        P("pool", "dp", None, None, "tp"),
    )
    out_specs = (P("pool", "dp", "tp"), P("pool", "dp", None, None, "tp"))
    return jax.shard_map(on_device, mesh=mesh, in_specs=in_specs, out_specs=out_specs, check_vma=False)
```

```python
import functools

import jax
import jax.numpy as jnp
from jax import lax
from jax.experimental import pallas as pl
from jax.experimental.pallas import tpu as pltpu
from jax.sharding import PartitionSpec as P

HEAD_DIM = 64
STATE = 256
CONV = 4
BLOCK = 128
PROMPTS = 3
STEPS = 4
ROWS = 4
CORES = 2
RING = 4
LANES = 128
DEC = STATE + 32
MSG = DEC + 144
SCRATCH_B = 14
REP = 32
CHIP_TOKENS = 512
BLOCKS = CHIP_TOKENS // BLOCK
GROUP_CH = 2048
CHUNK = GROUP_CH // RING
WIDE = GROUP_CH + 1024
LOG2E = 1.4426950408889634
F32 = jnp.float32
BF16 = jnp.bfloat16
MIB = 1024 * 1024


def split3(value):
    high = value.astype(BF16).astype(F32)
    rest = value - high
    middle = rest.astype(BF16).astype(F32)
    return high, middle, rest - middle


def pack3(value):
    high, middle, low = split3(value)
    lane = lax.broadcasted_iota(jnp.int32, value.shape, 1)
    return jnp.where(lane < REP, high, jnp.where(lane < 2 * REP, middle, low)).astype(BF16)


def spread_matrix(chunk):
    lane = lax.broadcasted_iota(jnp.int32, (LANES, CHUNK), 0)
    head = (lax.broadcasted_iota(jnp.int32, (LANES, CHUNK), 1) >> 6) + chunk * (CHUNK // HEAD_DIM)
    hit = ((lane & (REP - 1)) == head) & (lane < 3 * REP)
    return jnp.where(hit, 1.0, 0.0).astype(BF16)


def in_hbm(value):
    return pltpu.with_memory_space_constraint(value, pltpu.HBM)


def mm(a, b):
    return jnp.dot(a, b, preferred_element_type=F32)


def silu(value):
    half = 0.5 * value
    return half + half * jnp.tanh(half)


def softplus(value):
    return jnp.maximum(value, 0.0) + jnp.log1p(jnp.exp(-jnp.abs(value)))


def seg_vec(s_ref, pos):
    anchor, lo0, lo1 = s_ref[3], s_ref[4], s_ref[5]
    seg = (pos >= lo0).astype(jnp.int32) + (pos >= lo1).astype(jnp.int32)
    return jnp.where(pos < -anchor, -1, seg)


def seg_at(s_ref, pos):
    anchor, lo0, lo1 = s_ref[3], s_ref[4], s_ref[5]
    seg = jnp.where(pos >= lo0, 1, 0) + jnp.where(pos >= lo1, 1, 0)
    return jnp.where(pos + anchor < 0, -1, seg)


def rows_of(parts, count, width):
    row = lax.broadcasted_iota(jnp.int32, (count, width), 0)
    out = jnp.zeros((count, width), F32)
    for index, part in enumerate(parts):
        out = jnp.where(row == index, part, out)
    return out


def conv_tile(src, start, lanes, weight, offset, mask):
    tile = src[pl.ds(start, BLOCK + 8), lanes]
    running = jnp.broadcast_to(offset[:, lanes], (BLOCK, LANES))
    for tap in range(CONV - 1):
        moved = pltpu.roll(tile, CONV - 1 - tap, 0)[8:]
        running = running + weight[tap : tap + 1, lanes] * (moved * mask[tap, pl.ds(start, BLOCK), :])
    return silu(running + weight[CONV - 1 : CONV, lanes] * tile[8:])


def cache_rows(s_ref, src, out):
    out[...] = jnp.zeros_like(out)
    for prompt in range(PROMPTS):
        last = (s_ref[4] - 1, s_ref[5] - 1, RING * CORES * CHIP_TOKENS - 1 - s_ref[3])[prompt]

        @pl.when((last >= 0) & (last < CHIP_TOKENS))
        def _():
            for tap in range(CONV - 1):
                row = last - (CONV - 2) + tap
                same = jnp.where(seg_at(s_ref, row) == seg_at(s_ref, last), 1.0, 0.0)
                value = src[pl.ds(row + 8, 1), :]
                out[pl.ds(prompt * 3 + tap, 1), :] = jnp.where(same > 0.5, value, 0.0)


def cut_of(s_ref):
    first, second = s_ref[4] - 1, s_ref[5] - 1
    limit = CHIP_TOKENS - 1
    one = jnp.where((second >= 0) & (second < limit), second, -1)
    return jnp.where((first >= 0) & (first < limit), first, one)


def kernel_a(
    s_ref, x_own, x_rec, halo_x, wx, bx, g_own, g_rec, halo_g, wg, bg, vecs,
    l0, l1, l2, l3, xc_out, bcc_out, dtc_out, wc3_out, cx_out, cg_out,
    xs, gs, mask, wp3, keep3, bt, cache, wide, scaled,
):
    m = pl.program_id(0)
    core = s_ref[0]
    chunk = s_ref[1] ^ m
    first = core == 0
    half = CHIP_TOKENS // 2

    @pl.when(m == 0)
    def _():
        pos = lax.broadcasted_iota(jnp.int32, (CHIP_TOKENS, LANES), 0)
        own_seg = seg_vec(s_ref, pos)
        for tap in range(CONV - 1):
            mask[tap] = jnp.where(seg_vec(s_ref, pos - 3 + tap) == own_seg, 1.0, 0.0)
        gs[0:8] = halo_g[:, 0:512].astype(F32)[8:]
        gs[8 : 8 + half] = jnp.where(first, g_own[:, 0:512], g_rec[:, 0:512]).astype(F32)
        gs[8 + half :] = jnp.where(first, g_rec[:, 0:512], g_own[:, 0:512]).astype(F32)
        weight = wg[...].astype(F32)
        for j in range(BLOCKS):
            for strip in range(4):
                lanes = slice(strip * LANES, (strip + 1) * LANES)
                tile = conv_tile(gs, j * BLOCK, lanes, weight, bg, mask).astype(BF16)
                bcc_out[pl.ds(j * BLOCK, BLOCK), lanes] = tile
                if strip < 2:
                    bt[j, lanes, :] = tile.astype(F32).T.astype(BF16)
        cache_rows(s_ref, gs, cache)
        cg_out[...] = cache[...].astype(BF16)
        raw_a = jnp.where(first, g_own[:, 512:640], g_rec[:, 512:640]).astype(F32)
        raw_b = jnp.where(first, g_rec[:, 512:640], g_own[:, 512:640]).astype(F32)
        dt = softplus(jnp.concatenate([raw_a, raw_b], axis=0) + vecs[0:1])
        decay = dt * vecs[1:2]
        row = lax.broadcasted_iota(jnp.int32, (BLOCK, BLOCK), 0)
        col = lax.broadcasted_iota(jnp.int32, (BLOCK, BLOCK), 1)
        lower = jnp.where(row >= col, 1.0, 0.0).astype(BF16)
        dtc_out[0:CHIP_TOKENS] = dt
        total = jnp.zeros((1, LANES), F32)
        before = seg_at(s_ref, -1)
        keeps = []
        for j in range(BLOCKS):
            rows = slice(j * BLOCK, (j + 1) * BLOCK)
            high, middle, low = split3(decay[rows])
            cum = mm(lower, high.astype(BF16)) + mm(lower, middle.astype(BF16)) + mm(lower, low.astype(BF16))
            dtc_out[CHIP_TOKENS + j * BLOCK : CHIP_TOKENS + (j + 1) * BLOCK] = cum
            end = cum[BLOCK - 1 :]
            end_seg = seg_at(s_ref, (j + 1) * BLOCK - 1)
            weight_p = jnp.where(own_seg[rows] == end_seg, jnp.exp2(end - cum) * dt[rows], 0.0)
            wp3[pl.ds(j * BLOCK, BLOCK), :] = pack3(weight_p)
            reach = jnp.where(own_seg[rows] == before, jnp.exp2(total + cum), 0.0)
            wc3_out[pl.ds(j * BLOCK, BLOCK), :] = pack3(reach)
            keeps.append(jnp.where(seg_at(s_ref, j * BLOCK - 1) == end_seg, jnp.exp2(end), 0.0))
            total = total + end
        keeps.append(jnp.where(before == seg_at(s_ref, CHIP_TOKENS - 1), jnp.exp2(total), 0.0))
        keep3[...] = pack3(rows_of(keeps, 16, LANES))

    xs[0:8] = halo_x[...].astype(F32)[8:]
    xs[8 : 8 + half] = jnp.where(first, x_own[...], x_rec[...]).astype(F32)
    xs[8 + half :] = jnp.where(first, x_rec[...], x_own[...]).astype(F32)
    weight = wx[...].astype(F32)
    spread = spread_matrix(chunk)
    keep = mm(keep3[...], spread)
    for j in range(BLOCKS):
        rows = pl.ds(j * BLOCK, BLOCK)
        wide[...] = mm(wp3[rows, :], spread)
        for strip in range(CHUNK // LANES):
            lanes = slice(strip * LANES, (strip + 1) * LANES)
            xc = conv_tile(xs, j * BLOCK, lanes, weight, bx, mask).astype(BF16)
            xc_out[rows, lanes] = xc
            scaled[rows, lanes] = (xc.astype(F32) * wide[:, lanes]).astype(BF16)
    state = mm(bt[0], scaled[0:BLOCK, :])
    for j in range(1, BLOCKS):
        state = keep[j : j + 1] * state + mm(bt[j], scaled[pl.ds(j * BLOCK, BLOCK), :])
    cache_rows(s_ref, xs, cache)
    cx_out[...] = cache[...].astype(BF16)
    tail = rows_of(split3(keep[BLOCKS : BLOCKS + 1]), 16, CHUNK).astype(BF16)
    for index, out in enumerate((l0, l1, l2, l3)):

        @pl.when(m == index)
        def _():
            out[0:STATE] = state.astype(BF16)
            out[STATE:] = tail


def run_a(scalars, x_in, recv, halo, wx, bx, g_own, wg, bg, vecs):
    def fixed(shape):
        return pl.BlockSpec(shape, lambda m, s: (0,) * len(shape))

    def chunked(rows, per_core=0):
        return pl.BlockSpec((rows, CHUNK), lambda m, s: (0, s[0] * per_core + (s[1] ^ m)))

    half = CHIP_TOKENS // 2
    side = pl.BlockSpec((half, 1024), lambda m, s: (0, 2))
    return pl.pallas_call(
        kernel_a,
        grid_spec=pltpu.PrefetchScalarGridSpec(
            num_scalar_prefetch=1,
            grid=(RING,),
            in_specs=[
                chunked(half, RING), chunked(half), chunked(16), chunked(CONV, RING), chunked(1, RING),
                fixed((half, 1024)), side, pl.BlockSpec((16, 1024), lambda m, s: (0, 2)),
                fixed((CONV, 512)), fixed((1, 512)), fixed((8, LANES)),
            ],
            out_specs=[fixed((STATE + 16, CHUNK))] * RING + [
                chunked(CHIP_TOKENS), fixed((CHIP_TOKENS, 512)), fixed((2 * CHIP_TOKENS, LANES)),
                fixed((CHIP_TOKENS, LANES)), chunked(16), fixed((16, 512)),
            ],
            scratch_shapes=[
                pltpu.VMEM((CHIP_TOKENS + 8, CHUNK), F32),
                pltpu.VMEM((CHIP_TOKENS + 8, 512), F32),
                pltpu.VMEM((CONV - 1, CHIP_TOKENS, LANES), F32),
                pltpu.VMEM((CHIP_TOKENS, LANES), BF16),
                pltpu.VMEM((16, LANES), BF16),
                pltpu.VMEM((BLOCKS, STATE, BLOCK), BF16),
                pltpu.VMEM((16, CHUNK), F32),
                pltpu.VMEM((BLOCK, CHUNK), F32),
                pltpu.VMEM((CHIP_TOKENS, CHUNK), BF16),
            ],
        ),
        out_shape=[jax.ShapeDtypeStruct((STATE + 16, CHUNK), BF16)] * RING + [
            jax.ShapeDtypeStruct((CHIP_TOKENS, GROUP_CH), BF16),
            jax.ShapeDtypeStruct((CHIP_TOKENS, 512), BF16),
            jax.ShapeDtypeStruct((2 * CHIP_TOKENS, LANES), F32),
            jax.ShapeDtypeStruct((CHIP_TOKENS, LANES), BF16),
            jax.ShapeDtypeStruct((16, GROUP_CH), BF16),
            jax.ShapeDtypeStruct((16, 512), BF16),
        ],
        compiler_params=pltpu.CompilerParams(vmem_limit_bytes=16 * MIB),
        cost_estimate=pl.CostEstimate(flops=6 * 10**9, bytes_accessed=8 * 10**6, transcendentals=10**6),
        name="conv_and_states",
    )(scalars, x_in, recv, halo, wx, bx, g_own, recv, halo, wg, bg, vecs)


def kernel_b(
    base, count, s_ref, xc_ref, bcc, dtc, skip, cx, cg, near_same, near_cross, far_same, far_cross, *rest
):
    *outs, local_out = rest[-SCRATCH_B - count - 1 : -SCRATCH_B]
    (wp3, wb3, keep3, bt, gm, cum_t, dt_t, wf3, wide, reach, carried, scaled, parts, dec_rows) = rest[-SCRATCH_B:]
    m = pl.program_id(0) + base
    chunk = s_ref[1] ^ m
    cut = cut_of(s_ref)
    cut_block = cut // BLOCK

    @pl.when(m == base)
    def _():
        pos = lax.broadcasted_iota(jnp.int32, (BLOCK, LANES), 0)
        row = lax.broadcasted_iota(jnp.int32, (BLOCK, BLOCK), 0)
        col = lax.broadcasted_iota(jnp.int32, (BLOCK, BLOCK), 1)
        total = jnp.zeros((1, LANES), F32)
        before = seg_at(s_ref, -1)
        keeps = []
        cut_keep = jnp.zeros((1, LANES), F32)
        cut_reach = jnp.zeros((1, LANES), F32)
        cut_row = dtc[pl.ds(CHIP_TOKENS + jnp.maximum(cut, 0), 1), :]
        cut_seg = seg_at(s_ref, cut)
        wf3[...] = jnp.zeros_like(wf3)
        for j in range(BLOCKS):
            dt = dtc[j * BLOCK : (j + 1) * BLOCK]
            cum = dtc[CHIP_TOKENS + j * BLOCK : CHIP_TOKENS + (j + 1) * BLOCK]
            end = cum[BLOCK - 1 :]
            seg = seg_vec(s_ref, pos + j * BLOCK)
            end_seg = seg_at(s_ref, (j + 1) * BLOCK - 1)
            prev_seg = seg_at(s_ref, j * BLOCK - 1)
            wp3[pl.ds(j * BLOCK, BLOCK), :] = pack3(jnp.where(seg == end_seg, jnp.exp2(end - cum) * dt, 0.0))
            wb3[pl.ds(j * BLOCK, BLOCK), :] = pack3(jnp.where(seg == prev_seg, jnp.exp2(cum), 0.0))
            keeps.append(jnp.where(prev_seg == end_seg, jnp.exp2(end), 0.0))
            b_rows = bcc[pl.ds(j * BLOCK, BLOCK), 0:STATE]
            c_rows = bcc[pl.ds(j * BLOCK, BLOCK), STATE : 2 * STATE]
            b_t = b_rows.astype(F32).T.astype(BF16)
            bt[j] = b_t
            scores = mm(c_rows, b_t)
            same = seg_vec(s_ref, row + j * BLOCK) == seg_vec(s_ref, col + j * BLOCK)
            gm[j] = jnp.where((row >= col) & same, scores, 0.0)
            cum_t[j] = cum.T
            dt_t[j] = dt.T
            here = cut_block == j
            cut_keep = jnp.where(here & (cut_seg == prev_seg), jnp.exp2(cut_row), cut_keep)
            cut_reach = jnp.where(here & (cut_seg == before), jnp.exp2(total + cut_row), cut_reach)

            @pl.when((cut >= 0) & here)
            def _():
                chosen = (seg == cut_seg) & (pos + j * BLOCK <= cut)
                wf3[...] = pack3(jnp.where(chosen, jnp.exp2(jnp.minimum(cut_row - cum, 0.0)) * dt, 0.0))

            total = total + end
        keep3[...] = pack3(rows_of(keeps + [cut_keep, cut_reach], 16, LANES))
        core, upper = s_ref[0], s_ref[2]
        for top in range(2):
            for source in range(CORES):
                near = jnp.where(core == source, near_same[...], near_cross[...])
                far = jnp.where(core == source, far_same[...], far_cross[...])
                value = jnp.where(upper == top, near, far).astype(F32)
                for step in range(STEPS):
                    at = 32 * top + 8 * step + ROWS * source
                    dec_rows[at : at + ROWS, :] = value[ROWS * step : ROWS * step + ROWS, :]

    spread = spread_matrix(chunk)
    keep = mm(keep3[...], spread)
    half_lane = lax.broadcasted_iota(jnp.int32, (BLOCK, LANES), 1) < HEAD_DIM
    for index, out in enumerate(outs):

        @pl.when(m == base + index)
        def _():
            out[0:STATE] = jnp.zeros((STATE, CHUNK), BF16)
            row = lax.broadcasted_iota(jnp.int32, (16, CHUNK), 0)
            tile = cx[...].astype(F32)
            for part, value in enumerate(split3(keep[BLOCKS + 1 : BLOCKS + 2])):
                tile = jnp.where(row == 9 + part, value, tile)
            out[STATE : STATE + 16] = tile.astype(BF16)
            out[STATE + 16 : STATE + 32] = cg[...]
            at = pl.multiple_of(chunk * CHUNK, CHUNK)
            out[DEC : DEC + 64] = dec_rows[:, pl.ds(at, CHUNK)].astype(BF16)
            out[DEC + 64 : DEC + 128] = dec_rows[:, GROUP_CH : GROUP_CH + 512].astype(BF16)
            for part in range(4):
                steps = dec_rows[16 * part : 16 * part + 16, GROUP_CH + 512 : GROUP_CH + 640]
                out[DEC + 128 : DEC + 144, part * LANES : (part + 1) * LANES] = steps.astype(BF16)

    state = None
    pairs = CHUNK // LANES
    heads = chunk * (CHUNK // HEAD_DIM)
    heads_tile = pl.ds(pl.multiple_of(heads, 8), 8)
    for j in range(BLOCKS):
        rows = slice(j * BLOCK, (j + 1) * BLOCK)
        if j > 0:
            high = state.astype(BF16)
            parts[0:STATE] = high
            parts[STATE:] = (state - high.astype(F32)).astype(BF16)
            c_rows = bcc[rows, STATE : 2 * STATE]
            carried[...] = mm(jnp.concatenate([c_rows, c_rows], axis=1), parts[...])
            reach[...] = mm(wb3[rows], spread)

        @pl.when((cut >= 0) & (cut_block == j))
        def _():
            wide[...] = mm(wf3[...], spread)
            fresh = mm(bt[j], (xc_ref[rows].astype(F32) * wide[...]).astype(BF16))
            if j > 0:
                fresh = keep[BLOCKS : BLOCKS + 1] * state + fresh
            for index, out in enumerate(outs):

                @pl.when(m == base + index)
                def _():
                    out[0:STATE] = fresh.astype(BF16)

        if j < BLOCKS - 1:
            wide[...] = mm(wp3[rows], spread)
            for pair in range(pairs):
                lanes = slice(pair * LANES, (pair + 1) * LANES)
                scaled[:, lanes] = (xc_ref[rows, lanes].astype(F32) * wide[:, lanes]).astype(BF16)
            fresh = mm(bt[j], scaled[...])
            state = fresh if j == 0 else keep[j : j + 1] * state + fresh
        cum = dtc[CHIP_TOKENS + j * BLOCK : CHIP_TOKENS + (j + 1) * BLOCK]
        turned = pltpu.roll(cum, LANES - heads, 1)
        cum_rows = cum_t[j, heads_tile, :]
        dt_rows = dt_t[j, heads_tile, :]
        for pair in range(pairs):
            weights = []
            for head in (2 * pair, 2 * pair + 1):
                gap = jnp.minimum(turned[:, head : head + 1] - cum_rows[head : head + 1], 0.0)
                weights.append((jnp.exp2(gap) * (gm[j] * dt_rows[head : head + 1])).astype(BF16))
            lanes = slice(pair * LANES, (pair + 1) * LANES)
            two = xc_ref[rows, lanes]
            zero = jnp.zeros_like(two)
            stacked = jnp.concatenate([jnp.where(half_lane, two, zero), jnp.where(half_lane, zero, two)], axis=0)
            value = mm(jnp.concatenate(weights, axis=1), stacked) + skip[:, lanes] * two.astype(F32)
            if j > 0:
                value = value + reach[:, lanes] * carried[:, lanes]
            local_out[rows, lanes] = value


def run_b(scalars, xc, bcc, dtc, skip, cx, cg, dec_hops, base, count, local=None):
    def fixed(shape):
        return pl.BlockSpec(shape, lambda m, s: (0,) * len(shape))

    def chunked(rows, per_core=0):
        return pl.BlockSpec((rows, CHUNK), lambda m, s: (0, s[0] * per_core + (s[1] ^ (m + base))))

    args = [scalars, xc, bcc, dtc, skip, cx, cg, *dec_hops]
    in_specs = [
        chunked(CHIP_TOKENS), fixed((CHIP_TOKENS, 512)), fixed((2 * CHIP_TOKENS, LANES)),
        chunked(1, RING), chunked(16), fixed((16, 512)),
    ] + [fixed((16, WIDE))] * 4
    aliases = {}
    if local is not None:
        aliases = {len(args): count}
        args.append(local)
        in_specs.append(pl.BlockSpec(memory_space=pl.ANY))
    scratch = [
        pltpu.VMEM((CHIP_TOKENS, LANES), BF16),
        pltpu.VMEM((CHIP_TOKENS, LANES), BF16),
        pltpu.VMEM((16, LANES), BF16),
        pltpu.VMEM((BLOCKS, STATE, BLOCK), BF16),
        pltpu.VMEM((BLOCKS, BLOCK, BLOCK), F32),
        pltpu.VMEM((BLOCKS, LANES, BLOCK), F32),
        pltpu.VMEM((BLOCKS, LANES, BLOCK), F32),
        pltpu.VMEM((BLOCK, LANES), BF16),
        pltpu.VMEM((BLOCK, CHUNK), F32),
        pltpu.VMEM((BLOCK, CHUNK), F32),
        pltpu.VMEM((BLOCK, CHUNK), F32),
        pltpu.VMEM((BLOCK, CHUNK), BF16),
        pltpu.VMEM((2 * STATE, CHUNK), BF16),
        pltpu.VMEM((64, WIDE), F32),
    ]
    assert len(scratch) == SCRATCH_B
    return pl.pallas_call(
        functools.partial(kernel_b, base, count),
        grid_spec=pltpu.PrefetchScalarGridSpec(
            num_scalar_prefetch=1,
            grid=(count,),
            in_specs=in_specs,
            out_specs=[fixed((MSG, CHUNK))] * count + [chunked(CHIP_TOKENS)],
            scratch_shapes=scratch,
        ),
        out_shape=[jax.ShapeDtypeStruct((MSG, CHUNK), BF16)] * count + [pltpu.HBM((CHIP_TOKENS, GROUP_CH), F32)],
        input_output_aliases=aliases,
        compiler_params=pltpu.CompilerParams(vmem_limit_bytes=14 * MIB),
        cost_estimate=pl.CostEstimate(
            flops=3 * count * 10**9, bytes_accessed=2 * count * 10**6, transcendentals=count * 10**5
        ),
        name=f"output_within_chip_{base}",
    )(*args)


def pick(refs, which, rows):
    out = refs[0][rows]
    for index in range(1, len(refs)):
        out = jnp.where(which == index, refs[index][rows], out)
    return out.astype(F32)


def decay_rows(tile):
    return tile[0:1] + tile[1:2] + tile[2:3]


def kernel_total(s_ref, l0, l1, l2, l3, total_out):
    state = jnp.zeros((STATE, CHUNK), F32)
    for chip in range(RING):
        which = s_ref[1] ^ chip
        part = pick((l0, l1, l2, l3), which, slice(0, STATE))
        factor = decay_rows(pick((l0, l1, l2, l3), which, slice(STATE, STATE + 16)))
        state = factor * state + part
    total_out[...] = state.astype(BF16)


def kernel_starts(s_ref, l0, l1, l2, l3, start, r0, r1, r2, r3):
    state = start[...].astype(F32)
    for chip in range(RING):
        which = s_ref[1] ^ chip
        for index, out in enumerate((r0, r1, r2, r3)):

            @pl.when(which == index)
            def _():
                out[...] = state.astype(BF16)

        if chip < RING - 1:
            part = pick((l0, l1, l2, l3), which, slice(0, STATE))
            factor = decay_rows(pick((l0, l1, l2, l3), which, slice(STATE, STATE + 16)))
            state = factor * state + part


def whole_call(kernel, out_shape, name, flops, scratch=()):
    def run(scalars, *args):
        return pl.pallas_call(
            kernel,
            in_specs=[pl.BlockSpec(memory_space=pltpu.SMEM)] + [pl.BlockSpec(memory_space=pltpu.VMEM)] * len(args),
            out_specs=jax.tree.map(lambda _: pl.BlockSpec(memory_space=pltpu.VMEM), out_shape),
            out_shape=out_shape,
            scratch_shapes=list(scratch),
            compiler_params=pltpu.CompilerParams(vmem_limit_bytes=8 * MIB),
            cost_estimate=pl.CostEstimate(flops=flops, bytes_accessed=3 * 10**6, transcendentals=0),
            name=name,
        )(scalars, *args)

    return run


def kernel_decode(
    s_ref, l0, l1, l2, l3, start, f0, f1, f2, f3,
    wx, bx, wg, bg, vecs, skip, bounds,
    keep_out, send_out,
    final, rows_f32, result,
):
    z, upper = s_ref[1], s_ref[2]
    ls, fs = (l0, l1, l2, l3), (f0, f1, f2, f3)
    first, second = bounds[0, 0], bounds[0, 0] + bounds[0, 1]
    lasts = [first - 1, second - 1, second + bounds[0, 2] - 1]
    final[...] = jnp.zeros_like(final)
    state = start[...].astype(F32)
    for chip in range(RING):
        which = z ^ chip
        origin = (upper * RING + chip) * CHIP_TOKENS
        part = pick(ls, which, slice(0, STATE))
        factor = decay_rows(pick(ls, which, slice(STATE, STATE + 16)))
        after = factor * state + part
        for q in range(PROMPTS):
            local = lasts[q] - origin

            @pl.when(local == CHIP_TOKENS - 1)
            def _():
                final[q] = after

            @pl.when((local >= 0) & (local < CHIP_TOKENS - 1))
            def _():
                fresh = pick(fs, which, slice(0, STATE))
                reach = decay_rows(pick(fs, which, slice(STATE, STATE + 16))[9:12])
                final[q] = fresh + reach * state

        state = after
    cache_x = sum(f[STATE : STATE + 16].astype(F32) for f in fs)
    cache_g = sum(f[STATE + 16 : STATE + 32].astype(F32) for f in fs)
    spread = spread_matrix(z)
    for index, f in enumerate(fs):
        rows_f32[index, :, 0:CHUNK] = f[DEC : DEC + 64].astype(F32)
        rows_f32[index, :, CHUNK : CHUNK + 512] = f[DEC + 64 : DEC + 128].astype(F32)
        for part in range(4):
            steps = f[DEC + 128 : DEC + 144, part * LANES : (part + 1) * LANES].astype(F32)
            rows_f32[index, 16 * part : 16 * part + 16, CHUNK + 512 :] = steps

    def step_rows(step, lanes):
        tiles = [
            rows_f32[index, 32 * side + 8 * step : 32 * side + 8 * step + 8, lanes]
            for index in range(RING)
            for side in range(2)
        ]
        return jnp.concatenate(tiles, axis=0)

    prompt = step_rows(0, slice(1024, 1152))[:, 96:97]
    chosen = [prompt == float(q) for q in range(PROMPTS)]
    mine = jnp.zeros_like(prompt)
    for q in range(PROMPTS):
        inside = jnp.where(lasts[q] // (RING * CHIP_TOKENS) == upper, 1.0, 0.0)
        mine = jnp.where(chosen[q], inside, mine)

    def window(cache, lanes):
        rows = []
        for tap in range(CONV - 1):
            row = jnp.zeros((STEPS * 16, CHUNK), F32)
            for q in range(PROMPTS):
                row = jnp.where(chosen[q], cache[3 * q + tap : 3 * q + tap + 1], row)
            rows.append(row)
        return rows + [step_rows(step, lanes) for step in range(STEPS)]

    def convolved(rows, weight, offset):
        out = []
        for step in range(STEPS):
            running = jnp.broadcast_to(offset, rows[0].shape)
            for tap in range(CONV):
                running = running + weight[tap : tap + 1] * rows[step + tap]
            out.append(silu(running).astype(BF16))
        return out

    mixed = convolved(window(cache_x, slice(0, 512)), wx[...].astype(F32), bx[...])
    both = convolved(window(cache_g, slice(512, 1024)), wg[...].astype(F32), bg[...])
    steps, fades = [], []
    fade = jnp.zeros((STEPS * 16, LANES), F32)
    for step in range(STEPS):
        dt = softplus(step_rows(step, slice(1024, 1152)) + vecs[0:1])
        fade = fade + dt * vecs[1:2]
        steps.append(dt)
        fades.append(fade)
    readers = jnp.concatenate([rows[:, STATE:] for rows in both], axis=0)
    readout = jnp.zeros((STEPS * STEPS * 16, CHUNK), F32)
    for q in range(PROMPTS):
        high = final[q].astype(BF16)
        low = (final[q] - high.astype(F32)).astype(BF16)
        value = mm(readers, high) + mm(readers, low)
        readout = jnp.where(jnp.concatenate([chosen[q]] * STEPS, axis=0), value, readout)
    for step in range(STEPS):
        mixed_now = mixed[step].astype(F32)
        total = readout[64 * step : 64 * step + 64] * mm(pack3(jnp.exp2(fades[step])), spread)
        total = total + skip[...] * mixed_now
        reader = both[step][:, STATE:].astype(F32)
        for past in range(step + 1):
            weight = steps[past]
            if past < step:
                weight = weight * jnp.exp2(fades[step] - fades[past])
            product = jnp.sum(reader * both[past][:, 0:STATE].astype(F32), axis=1, keepdims=True)
            total = total + mm(pack3(weight), spread) * (product * mixed[past].astype(F32))
        total = jnp.where(mine > 0.5, total, 0.0)
        for index in range(RING):
            for side in range(2):
                tile = total[8 * (2 * index + side) : 8 * (2 * index + side) + 8]
                result[index, 32 * side + 8 * step : 32 * side + 8 * step + 8, :] = tile
    for index in range(RING):
        keep_out[index] = result[index, pl.ds(pl.multiple_of(32 * upper, 32), 32), :].astype(BF16)
        send_out[index] = result[index, pl.ds(pl.multiple_of(32 * (1 - upper), 32), 32), :].astype(BF16)


def kernel_d(s_ref, local, c_rows, wc3, r0, r1, r2, r3, out):
    z = s_ref[1]
    block = (z >> 1) ^ pl.program_id(0)
    for side in range(2):
        chunk = 2 * block + side
        spread = spread_matrix(chunk)
        for index, r in enumerate((r0, r1, r2, r3)):

            @pl.when((chunk ^ z) == index)
            def _():
                for part in range(2):
                    lanes = slice(part * 256, (part + 1) * 256)
                    to = slice(side * CHUNK + part * 256, side * CHUNK + (part + 1) * 256)
                    factor = mm(wc3[...], spread[:, lanes])
                    out[:, to] = (local[:, to] + factor * mm(c_rows[...], r[:, lanes])).astype(BF16)


def run_d(scalars, local, bcc, wc3, starts, own):
    half = CHIP_TOKENS // 2

    def row(s):
        return s[0] if own else 1 - s[0]

    width = CORES * GROUP_CH if own else GROUP_CH
    return pl.pallas_call(
        kernel_d,
        grid_spec=pltpu.PrefetchScalarGridSpec(
            num_scalar_prefetch=1,
            grid=(2,),
            in_specs=[
                pl.BlockSpec((half, 2 * CHUNK), lambda m, s: (row(s), (s[1] >> 1) ^ m)),
                pl.BlockSpec((half, STATE), lambda m, s: (row(s), 1)),
                pl.BlockSpec((half, LANES), lambda m, s: (row(s), 0)),
            ] + [pl.BlockSpec((STATE, CHUNK), lambda m, s: (0, 0))] * RING,
            out_specs=pl.BlockSpec((half, 2 * CHUNK), lambda m, s: (0, (s[0] * 2 if own else 0) + ((s[1] >> 1) ^ m))),
        ),
        out_shape=jax.ShapeDtypeStruct((half, width), BF16),
        compiler_params=pltpu.CompilerParams(vmem_limit_bytes=12 * MIB),
        cost_estimate=pl.CostEstimate(flops=10**9, bytes_accessed=4 * 10**6, transcendentals=0),
        name="carried_own" if own else "carried_other",
    )(scalars, local, bcc, wc3, *starts)


def kernel_put(s_ref, part, whole, out):
    out[...] = part[...]


def put_group(scalars, whole, part):
    half = CHIP_TOKENS // 2
    return pl.pallas_call(
        kernel_put,
        grid_spec=pltpu.PrefetchScalarGridSpec(
            num_scalar_prefetch=1,
            grid=(2,),
            in_specs=[
                pl.BlockSpec((half, GROUP_CH // 2), lambda m, s: (0, m)),
                pl.BlockSpec(memory_space=pl.ANY),
            ],
            out_specs=pl.BlockSpec((half, GROUP_CH // 2), lambda m, s: (0, (1 - s[0]) * 2 + m)),
        ),
        out_shape=jax.ShapeDtypeStruct(whole.shape, BF16),
        input_output_aliases={2: 0},
        compiler_params=pltpu.CompilerParams(vmem_limit_bytes=4 * MIB),
        cost_estimate=pl.CostEstimate(flops=0, bytes_accessed=2 * 10**6, transcendentals=0),
        name="put_group",
    )(scalars, part, whole)


def head_copies(group):
    lane = lax.broadcasted_iota(jnp.int32, (64, LANES), 1)
    head = lax.broadcasted_iota(jnp.int32, (64, LANES), 0)
    hit = ((lane & (REP - 1)) + group * REP == head) & (lane < 3 * REP)
    return jnp.where(hit, 1.0, 0.0).astype(BF16)


def kernel_pack(s_ref, x, bc, dt_t, x_last, bc_last, dx, dbc, ddt, send, halo0, halo1, side, d_own, d_other, rows_f32):
    core = s_ref[0]
    first = core == 0
    rows = x.shape[0]
    start = pl.multiple_of(pl.program_id(0) * rows, rows)
    dt = dt_t[:, pl.ds(start, rows)].astype(F32).T.astype(BF16)
    b_rows, c_rows = bc[:, 0, :], bc[:, 1, :]
    send[:, 0:GROUP_CH] = x[...]
    for target, group, offset in ((send, 1 - core, GROUP_CH), (side, core, 0)):
        low = group == 0
        target[:, offset : offset + STATE] = jnp.where(low, b_rows[:, 0:STATE], b_rows[:, STATE:])
        target[:, offset + STATE : offset + 2 * STATE] = jnp.where(low, c_rows[:, 0:STATE], c_rows[:, STATE:])
        target[:, offset + 512 : offset + 640] = mm(dt, head_copies(group)).astype(BF16)
        target[:, offset + 640 : offset + 1024] = jnp.zeros((rows, 384), BF16)

    @pl.when(pl.program_id(0) == 0)
    def _():
        b_last, c_last = bc_last[:, 0, :], bc_last[:, 1, :]
        for group, halo in ((0, halo0), (1, halo1)):
            halo[:, 0:GROUP_CH] = x_last[:, group * GROUP_CH : (group + 1) * GROUP_CH]
            halo[:, GROUP_CH : GROUP_CH + STATE] = b_last[:, group * STATE : (group + 1) * STATE]
            halo[:, GROUP_CH + STATE : GROUP_CH + 512] = c_last[:, group * STATE : (group + 1) * STATE]
            halo[:, GROUP_CH + 512 :] = jnp.zeros((16, 512), BF16)
        lane = lax.broadcasted_iota(jnp.int32, (ROWS, LANES), 1)
        row = lax.broadcasted_iota(jnp.int32, (ROWS, LANES), 0)
        prompt = jnp.zeros((ROWS, LANES), F32)
        for r in range(ROWS):
            prompt = jnp.where(row == r, s_ref[1 + r].astype(F32), prompt)
        for out, group in ((d_own, core), (d_other, 1 - core)):
            low = group == 0
            rows_f32[...] = jnp.zeros_like(rows_f32)
            for step in range(STEPS):
                at = slice(ROWS * step, ROWS * step + ROWS)
                value = dx[step].astype(F32)
                rows_f32[at, 0:GROUP_CH] = jnp.where(low, value[:, 0:GROUP_CH], value[:, GROUP_CH:])
                for part in range(2):
                    value = dbc[step, :, part, :].astype(F32)
                    to = GROUP_CH + part * STATE
                    rows_f32[at, to : to + STATE] = jnp.where(low, value[:, 0:STATE], value[:, STATE:])
                steps = mm(ddt[step], head_copies(group))
                rows_f32[at, GROUP_CH + 512 : GROUP_CH + 640] = jnp.where(lane < 3 * REP, steps, prompt)
            out[...] = rows_f32[...].astype(BF16)


def run_pack(scalars, x, bc, dt_t, dx, dbc, ddt):
    rows = x.shape[0]
    tile = rows // 2
    last = rows // 16 - 1
    small = (16, WIDE)

    def fixed(shape):
        return pl.BlockSpec(shape, lambda i, s: (0,) * len(shape))

    return pl.pallas_call(
        kernel_pack,
        grid_spec=pltpu.PrefetchScalarGridSpec(
            num_scalar_prefetch=1,
            grid=(2,),
            in_specs=[
                pl.BlockSpec((tile, GROUP_CH), lambda i, s: (i, 1 - s[0])),
                pl.BlockSpec((tile, 2, 512), lambda i, s: (i, 0, 0)),
                fixed(dt_t.shape),
                pl.BlockSpec((16, CORES * GROUP_CH), lambda i, s: (last, 0)),
                pl.BlockSpec((16, 2, 512), lambda i, s: (last, 0, 0)),
                fixed(dx.shape),
                fixed(dbc.shape),
                fixed(ddt.shape),
            ],
            out_specs=[
                pl.BlockSpec((tile, WIDE), lambda i, s: (i, 0)),
                fixed(small),
                fixed(small),
                pl.BlockSpec((tile, 1024), lambda i, s: (i, 0)),
                fixed(small),
                fixed(small),
            ],
            scratch_shapes=[pltpu.VMEM(small, F32)],
        ),
        out_shape=[pltpu.HBM(shape, BF16) for shape in ((rows, WIDE), small, small, (rows, 1024), small, small)],
        compiler_params=pltpu.CompilerParams(vmem_limit_bytes=12 * MIB),
        cost_estimate=pl.CostEstimate(flops=10**6, bytes_accessed=4 * 10**6, transcendentals=0),
        name="pack",
    )(scalars, x, bc, dt_t, x, bc, dx, dbc, ddt)


def on_device(
    x_in, bc_in, dt_raw, conv_w_x, conv_b_x, conv_w_bc, conv_b_bc, dt_bias, a_log, d_skip,
    lengths, decode_prompt, dec_x, dec_bc, dec_dt,
):
    count = lax.axis_size("dp")
    place = lax.axis_index("dp")
    core = place % CORES
    z = (place // CORES) % RING
    upper = place // (CORES * RING)
    anchor = (place // CORES) * CHIP_TOKENS
    bounds = (lengths[0, 0], lengths[0, 0] + lengths[0, 1])
    zero = jnp.int32(0)
    scalars = jnp.stack([core, z, upper, anchor, bounds[0] - anchor, bounds[1] - anchor, zero, zero]).astype(jnp.int32)
    both = ("pool", "dp")

    x_rows, bc_rows = in_hbm(x_in[0]), in_hbm(bc_in[0])
    own = jnp.concatenate([core[None], decode_prompt[0, 0]]).astype(jnp.int32)
    packed, halo0, halo1, g_own, d_own, d_other = run_pack(
        own, x_rows, bc_rows, in_hbm(dt_raw[0].T), in_hbm(dec_x[0, 0]), in_hbm(dec_bc[0, 0]), in_hbm(dec_dt[0, 0])
    )
    recv = in_hbm(lax.ppermute(packed, "dp", [(i, i ^ 1) for i in range(count)]))
    g_own = in_hbm(g_own)
    halo = lax.ppermute(halo0, "dp", [(i, i + 1) for i in range(1, count - 1, 2)])
    halo = halo + lax.ppermute(halo1, "dp", [(i, i + 2) for i in range(1, count - 1, 2)])

    def after(value, other):
        return lax.optimization_barrier((value, other))[0]

    dec_rows = STEPS * ROWS
    total = 2 * count

    def hop(value, flip):
        return lax.ppermute(value, both, [(i, ((i + count) % total) ^ flip) for i in range(total)])

    def z_swap(value, m):
        if m == 0:
            return value
        return lax.ppermute(value, "dp", [(i, i ^ (CORES * m)) for i in range(count)])

    def z_swaps(values):
        order = (0, 2, 1, 3)
        moved = {m: z_swap(values[m], m) for m in order}
        return [moved[m] for m in range(RING)]

    dec_hops = [hop(d_own, 0), hop(d_other, 1), hop(d_own, CORES * RING), hop(d_other, CORES * RING + 1)]

    w_group = lax.dynamic_slice_in_dim(conv_w_bc, core * STATE, STATE, 2).reshape(CONV, 2 * STATE)
    b_group = lax.dynamic_slice_in_dim(conv_b_bc, core * STATE, STATE, 1).reshape(1, 2 * STATE)
    rates = -LOG2E * jnp.exp(a_log)
    heads = jnp.stack([dt_bias, rates])
    heads = lax.dynamic_slice_in_dim(heads, core * REP, REP, 1)
    vecs = jnp.pad(jnp.tile(heads, (1, 3)), ((0, 6), (0, LANES - 3 * REP)))
    skip = jnp.repeat(d_skip, HEAD_DIM)[None]
    b_x = conv_b_x[None]

    *ls, xc, bcc, dtc, wc3, cx, cg = run_a(scalars, x_rows, recv, halo, conv_w_x, b_x, g_own, w_group, b_group, vecs)
    sent_ls = z_swaps(ls)
    *fs, local = run_b(scalars, xc, bcc, dtc, skip, cx, cg, dec_hops, 1, 3)
    ls = after(tuple(sent_ls), fs[0])
    state_shape = jax.ShapeDtypeStruct((STATE, CHUNK), BF16)
    half_total = whole_call(kernel_total, state_shape, "half_total", 10**6)(scalars, *ls)
    own_end, local = run_b(scalars, xc, bcc, dtc, skip, cx, cg, after(tuple(dec_hops), half_total), 0, 1, in_hbm(local))
    fs = z_swaps([own_end, *fs])
    local = in_hbm(local)
    start = lax.ppermute(half_total, "dp", [(i, i + CORES * RING) for i in range(CORES * RING)])
    starts = whole_call(kernel_starts, [state_shape] * RING, "chip_starts", 10**6)(scalars, *ls, start)
    starts = z_swaps(starts)

    def own_columns(value):
        return lax.dynamic_slice_in_dim(value, core * GROUP_CH + z * CHUNK, CHUNK, 1)

    def decode(bounds_ref_args):
        shape = jax.ShapeDtypeStruct((RING, 32, CHUNK), BF16)
        args = [*ls, start, *fs, own_columns(conv_w_x), own_columns(b_x), w_group, b_group, vecs, own_columns(skip)]
        return pl.pallas_call(
            kernel_decode,
            in_specs=[pl.BlockSpec(memory_space=pltpu.SMEM)]
            + [pl.BlockSpec(memory_space=pltpu.VMEM)] * len(args)
            + [pl.BlockSpec(memory_space=pltpu.SMEM)],
            out_specs=[pl.BlockSpec(memory_space=pltpu.VMEM)] * 2,
            out_shape=[shape, shape],
            scratch_shapes=[
                pltpu.VMEM((PROMPTS, STATE, CHUNK), F32),
                pltpu.VMEM((RING, 64, 1152), F32),
                pltpu.VMEM((RING, 64, CHUNK), F32),
            ],
            compiler_params=pltpu.CompilerParams(vmem_limit_bytes=14 * MIB),
            cost_estimate=pl.CostEstimate(flops=20 * 10**9, bytes_accessed=6 * 10**6, transcendentals=0),
            name="decode_rows",
        )(scalars, *args, bounds_ref_args)

    kept, sent = after(tuple(decode(lengths.astype(jnp.int32))), starts[1])
    other_rows = run_d(scalars, local, bcc, wc3, starts, False)
    other_group = lax.ppermute(other_rows, "dp", [(i, i ^ 1) for i in range(count)])
    straight = lax.ppermute(kept, both, [(i, (i + count) % total) for i in range(total)])
    crossed = lax.ppermute(sent, both, [(i, ((i + count) % total) ^ (CORES * RING)) for i in range(total)])
    answers = after(straight + crossed, other_rows)
    answers = [z_swap(answers[m], m) for m in range(RING)]
    own_group = run_d(scalars, local, bcc, wc3, starts, True)
    answers = after(tuple(answers), own_group)
    columns = [
        functools.reduce(lambda a, m: jnp.where(z == j ^ m, answers[m], a), range(1, RING), answers[0])
        for j in range(RING)
    ]
    answers = jnp.concatenate(columns, axis=1).reshape(STEPS, CORES, ROWS, GROUP_CH)
    first, second = (answers[:, i].reshape(dec_rows, GROUP_CH) for i in range(CORES))
    mine = jnp.where(core == 0, first, second)
    theirs = lax.ppermute(jnp.where(core == 0, second, first), "dp", [(i, i ^ 1) for i in range(count)])
    out = put_group(scalars, own_group, other_group)
    theirs = after(theirs, out)
    decoded = jnp.where(core == 0, jnp.concatenate([mine, theirs], axis=1), jnp.concatenate([theirs, mine], axis=1))
    return out[None], decoded.reshape(dec_x.shape)


def solution(mesh):
    in_specs = (
        P("pool", "dp", "tp"),
        P("pool", "dp", None, "tp"),
        P("pool", "dp", "tp"),
        P(None, "tp"),
        P("tp"),
        P(None, None, "tp"),
        P(None, "tp"),
        P("tp"),
        P("tp"),
        P("tp"),
        P("pool", None),
        P("pool", "dp", None),
        P("pool", "dp", None, None, "tp"),
        P("pool", "dp", None, None, None, "tp"),
        P("pool", "dp", None, None, "tp"),
    )
    out_specs = (P("pool", "dp", "tp"), P("pool", "dp", None, None, "tp"))
    return jax.shard_map(on_device, mesh=mesh, in_specs=in_specs, out_specs=out_specs, check_vma=False)
```

```python
import functools

import jax
import jax.numpy as jnp
from jax import lax
from jax.experimental import pallas as pl
from jax.experimental.pallas import tpu as pltpu
from jax.sharding import PartitionSpec as P

HEAD_DIM = 64
STATE = 256
CONV = 4
BLOCK = 128
PROMPTS = 3
STEPS = 4
ROWS = 4
CORES = 2
RING = 4
LANES = 128
DEC = STATE + 32
MSG = DEC + 144
SCRATCH_B = 14
REP = 32
CHIP_TOKENS = 512
BLOCKS = CHIP_TOKENS // BLOCK
GROUP_CH = 2048
CHUNK = GROUP_CH // RING
WIDE = GROUP_CH + 1024
LOG2E = 1.4426950408889634
F32 = jnp.float32
BF16 = jnp.bfloat16
MIB = 1024 * 1024


def split3(value):
    high = value.astype(BF16).astype(F32)
    rest = value - high
    middle = rest.astype(BF16).astype(F32)
    return high, middle, rest - middle


def pack3(value):
    high, middle, low = split3(value)
    lane = lax.broadcasted_iota(jnp.int32, value.shape, 1)
    return jnp.where(lane < REP, high, jnp.where(lane < 2 * REP, middle, low)).astype(BF16)


def spread_matrix(chunk):
    lane = lax.broadcasted_iota(jnp.int32, (LANES, CHUNK), 0)
    head = (lax.broadcasted_iota(jnp.int32, (LANES, CHUNK), 1) >> 6) + chunk * (CHUNK // HEAD_DIM)
    hit = ((lane & (REP - 1)) == head) & (lane < 3 * REP)
    return jnp.where(hit, 1.0, 0.0).astype(BF16)


def in_hbm(value):
    return pltpu.with_memory_space_constraint(value, pltpu.HBM)


def mm(a, b):
    return jnp.dot(a, b, preferred_element_type=F32)


def silu(value):
    half = 0.5 * value
    return half + half * jnp.tanh(half)


def softplus(value):
    return jnp.maximum(value, 0.0) + jnp.log1p(jnp.exp(-jnp.abs(value)))


def seg_vec(s_ref, pos):
    anchor, lo0, lo1 = s_ref[3], s_ref[4], s_ref[5]
    seg = (pos >= lo0).astype(jnp.int32) + (pos >= lo1).astype(jnp.int32)
    return jnp.where(pos < -anchor, -1, seg)


def seg_at(s_ref, pos):
    anchor, lo0, lo1 = s_ref[3], s_ref[4], s_ref[5]
    seg = jnp.where(pos >= lo0, 1, 0) + jnp.where(pos >= lo1, 1, 0)
    return jnp.where(pos + anchor < 0, -1, seg)


def rows_of(parts, count, width):
    row = lax.broadcasted_iota(jnp.int32, (count, width), 0)
    out = jnp.zeros((count, width), F32)
    for index, part in enumerate(parts):
        out = jnp.where(row == index, part, out)
    return out


def conv_tile(src, start, lanes, weight, offset, mask):
    tile = src[pl.ds(start, BLOCK + 8), lanes]
    running = jnp.broadcast_to(offset[:, lanes], (BLOCK, LANES))
    for tap in range(CONV - 1):
        moved = pltpu.roll(tile, CONV - 1 - tap, 0)[8:]
        running = running + weight[tap : tap + 1, lanes] * (moved * mask[tap, pl.ds(start, BLOCK), :])
    return silu(running + weight[CONV - 1 : CONV, lanes] * tile[8:])


def cache_rows(s_ref, src, out):
    out[...] = jnp.zeros_like(out)
    for prompt in range(PROMPTS):
        last = (s_ref[4] - 1, s_ref[5] - 1, RING * CORES * CHIP_TOKENS - 1 - s_ref[3])[prompt]

        @pl.when((last >= 0) & (last < CHIP_TOKENS))
        def _():
            for tap in range(CONV - 1):
                row = last - (CONV - 2) + tap
                same = jnp.where(seg_at(s_ref, row) == seg_at(s_ref, last), 1.0, 0.0)
                value = src[pl.ds(row + 8, 1), :]
                out[pl.ds(prompt * 3 + tap, 1), :] = jnp.where(same > 0.5, value, 0.0)


def cut_of(s_ref):
    first, second = s_ref[4] - 1, s_ref[5] - 1
    limit = CHIP_TOKENS - 1
    one = jnp.where((second >= 0) & (second < limit), second, -1)
    return jnp.where((first >= 0) & (first < limit), first, one)


def kernel_a(
    s_ref, x_own, x_rec, halo_x, wx, bx, g_own, g_rec, halo_g, wg, bg, vecs,
    l0, l1, l2, l3, xc_out, bcc_out, dtc_out, wc3_out, cx_out, cg_out,
    xs, gs, mask, wp3, keep3, bt, cache, wide, scaled,
):
    m = pl.program_id(0)
    core = s_ref[0]
    chunk = s_ref[1] ^ m
    first = core == 0
    half = CHIP_TOKENS // 2

    @pl.when(m == 0)
    def _():
        pos = lax.broadcasted_iota(jnp.int32, (CHIP_TOKENS, LANES), 0)
        own_seg = seg_vec(s_ref, pos)
        for tap in range(CONV - 1):
            mask[tap] = jnp.where(seg_vec(s_ref, pos - 3 + tap) == own_seg, 1.0, 0.0)
        gs[0:8] = halo_g[:, 0:512].astype(F32)[8:]
        gs[8 : 8 + half] = jnp.where(first, g_own[:, 0:512], g_rec[:, 0:512]).astype(F32)
        gs[8 + half :] = jnp.where(first, g_rec[:, 0:512], g_own[:, 0:512]).astype(F32)
        weight = wg[...].astype(F32)
        for j in range(BLOCKS):
            for strip in range(4):
                lanes = slice(strip * LANES, (strip + 1) * LANES)
                tile = conv_tile(gs, j * BLOCK, lanes, weight, bg, mask).astype(BF16)
                bcc_out[pl.ds(j * BLOCK, BLOCK), lanes] = tile
                if strip < 2:
                    bt[j, lanes, :] = tile.astype(F32).T.astype(BF16)
        cache_rows(s_ref, gs, cache)
        cg_out[...] = cache[...].astype(BF16)
        raw_a = jnp.where(first, g_own[:, 512:640], g_rec[:, 512:640]).astype(F32)
        raw_b = jnp.where(first, g_rec[:, 512:640], g_own[:, 512:640]).astype(F32)
        dt = softplus(jnp.concatenate([raw_a, raw_b], axis=0) + vecs[0:1])
        decay = dt * vecs[1:2]
        row = lax.broadcasted_iota(jnp.int32, (BLOCK, BLOCK), 0)
        col = lax.broadcasted_iota(jnp.int32, (BLOCK, BLOCK), 1)
        lower = jnp.where(row >= col, 1.0, 0.0).astype(BF16)
        dtc_out[0:CHIP_TOKENS] = dt
        total = jnp.zeros((1, LANES), F32)
        before = seg_at(s_ref, -1)
        keeps = []
        for j in range(BLOCKS):
            rows = slice(j * BLOCK, (j + 1) * BLOCK)
            high, middle, low = split3(decay[rows])
            cum = mm(lower, high.astype(BF16)) + mm(lower, middle.astype(BF16)) + mm(lower, low.astype(BF16))
            dtc_out[CHIP_TOKENS + j * BLOCK : CHIP_TOKENS + (j + 1) * BLOCK] = cum
            end = cum[BLOCK - 1 :]
            end_seg = seg_at(s_ref, (j + 1) * BLOCK - 1)
            weight_p = jnp.where(own_seg[rows] == end_seg, jnp.exp2(end - cum) * dt[rows], 0.0)
            wp3[pl.ds(j * BLOCK, BLOCK), :] = pack3(weight_p)
            reach = jnp.where(own_seg[rows] == before, jnp.exp2(total + cum), 0.0)
            wc3_out[pl.ds(j * BLOCK, BLOCK), :] = pack3(reach)
            keeps.append(jnp.where(seg_at(s_ref, j * BLOCK - 1) == end_seg, jnp.exp2(end), 0.0))
            total = total + end
        keeps.append(jnp.where(before == seg_at(s_ref, CHIP_TOKENS - 1), jnp.exp2(total), 0.0))
        keep3[...] = pack3(rows_of(keeps, 16, LANES))

    xs[0:8] = halo_x[...].astype(F32)[8:]
    xs[8 : 8 + half] = jnp.where(first, x_own[...], x_rec[...]).astype(F32)
    xs[8 + half :] = jnp.where(first, x_rec[...], x_own[...]).astype(F32)
    weight = wx[...].astype(F32)
    spread = spread_matrix(chunk)
    keep = mm(keep3[...], spread)
    for j in range(BLOCKS):
        rows = pl.ds(j * BLOCK, BLOCK)
        wide[...] = mm(wp3[rows, :], spread)
        for strip in range(CHUNK // LANES):
            lanes = slice(strip * LANES, (strip + 1) * LANES)
            xc = conv_tile(xs, j * BLOCK, lanes, weight, bx, mask).astype(BF16)
            xc_out[rows, lanes] = xc
            scaled[rows, lanes] = (xc.astype(F32) * wide[:, lanes]).astype(BF16)
    state = mm(bt[0], scaled[0:BLOCK, :])
    for j in range(1, BLOCKS):
        state = keep[j : j + 1] * state + mm(bt[j], scaled[pl.ds(j * BLOCK, BLOCK), :])
    cache_rows(s_ref, xs, cache)
    cx_out[...] = cache[...].astype(BF16)
    tail = rows_of(split3(keep[BLOCKS : BLOCKS + 1]), 16, CHUNK).astype(BF16)
    for index, out in enumerate((l0, l1, l2, l3)):

        @pl.when(m == index)
        def _():
            out[0:STATE] = state.astype(BF16)
            out[STATE:] = tail


def run_a(scalars, x_in, recv, halo, wx, bx, g_own, wg, bg, vecs):
    def fixed(shape):
        return pl.BlockSpec(shape, lambda m, s: (0,) * len(shape))

    def chunked(rows, per_core=0):
        return pl.BlockSpec((rows, CHUNK), lambda m, s: (0, s[0] * per_core + (s[1] ^ m)))

    half = CHIP_TOKENS // 2
    side = pl.BlockSpec((half, 1024), lambda m, s: (0, 2))
    return pl.pallas_call(
        kernel_a,
        grid_spec=pltpu.PrefetchScalarGridSpec(
            num_scalar_prefetch=1,
            grid=(RING,),
            in_specs=[
                chunked(half, RING), chunked(half), chunked(16), chunked(CONV, RING), chunked(1, RING),
                fixed((half, 1024)), side, pl.BlockSpec((16, 1024), lambda m, s: (0, 2)),
                fixed((CONV, 512)), fixed((1, 512)), fixed((8, LANES)),
            ],
            out_specs=[fixed((STATE + 16, CHUNK))] * RING + [
                chunked(CHIP_TOKENS), fixed((CHIP_TOKENS, 512)), fixed((2 * CHIP_TOKENS, LANES)),
                fixed((CHIP_TOKENS, LANES)), chunked(16), fixed((16, 512)),
            ],
            scratch_shapes=[
                pltpu.VMEM((CHIP_TOKENS + 8, CHUNK), F32),
                pltpu.VMEM((CHIP_TOKENS + 8, 512), F32),
                pltpu.VMEM((CONV - 1, CHIP_TOKENS, LANES), F32),
                pltpu.VMEM((CHIP_TOKENS, LANES), BF16),
                pltpu.VMEM((16, LANES), BF16),
                pltpu.VMEM((BLOCKS, STATE, BLOCK), BF16),
                pltpu.VMEM((16, CHUNK), F32),
                pltpu.VMEM((BLOCK, CHUNK), F32),
                pltpu.VMEM((CHIP_TOKENS, CHUNK), BF16),
            ],
        ),
        out_shape=[jax.ShapeDtypeStruct((STATE + 16, CHUNK), BF16)] * RING + [
            jax.ShapeDtypeStruct((CHIP_TOKENS, GROUP_CH), BF16),
            jax.ShapeDtypeStruct((CHIP_TOKENS, 512), BF16),
            jax.ShapeDtypeStruct((2 * CHIP_TOKENS, LANES), F32),
            jax.ShapeDtypeStruct((CHIP_TOKENS, LANES), BF16),
            jax.ShapeDtypeStruct((16, GROUP_CH), BF16),
            jax.ShapeDtypeStruct((16, 512), BF16),
        ],
        compiler_params=pltpu.CompilerParams(vmem_limit_bytes=16 * MIB),
        cost_estimate=pl.CostEstimate(flops=6 * 10**9, bytes_accessed=8 * 10**6, transcendentals=10**6),
        name="conv_and_states",
    )(scalars, x_in, recv, halo, wx, bx, g_own, recv, halo, wg, bg, vecs)


def kernel_b(
    base, count, s_ref, xc_ref, bcc, dtc, skip, cx, cg, near_same, near_cross, far_same, far_cross, *rest
):
    *outs, local_out = rest[-SCRATCH_B - count - 1 : -SCRATCH_B]
    (wp3, wb3, keep3, bt, gm, cum_t, dt_t, wf3, wide, reach, carried, scaled, parts, dec_rows) = rest[-SCRATCH_B:]
    m = pl.program_id(0) + base
    chunk = s_ref[1] ^ m
    cut = cut_of(s_ref)
    cut_block = cut // BLOCK

    @pl.when(m == base)
    def _():
        pos = lax.broadcasted_iota(jnp.int32, (BLOCK, LANES), 0)
        row = lax.broadcasted_iota(jnp.int32, (BLOCK, BLOCK), 0)
        col = lax.broadcasted_iota(jnp.int32, (BLOCK, BLOCK), 1)
        total = jnp.zeros((1, LANES), F32)
        before = seg_at(s_ref, -1)
        keeps = []
        cut_keep = jnp.zeros((1, LANES), F32)
        cut_reach = jnp.zeros((1, LANES), F32)
        cut_row = dtc[pl.ds(CHIP_TOKENS + jnp.maximum(cut, 0), 1), :]
        cut_seg = seg_at(s_ref, cut)
        wf3[...] = jnp.zeros_like(wf3)
        for j in range(BLOCKS):
            dt = dtc[j * BLOCK : (j + 1) * BLOCK]
            cum = dtc[CHIP_TOKENS + j * BLOCK : CHIP_TOKENS + (j + 1) * BLOCK]
            end = cum[BLOCK - 1 :]
            seg = seg_vec(s_ref, pos + j * BLOCK)
            end_seg = seg_at(s_ref, (j + 1) * BLOCK - 1)
            prev_seg = seg_at(s_ref, j * BLOCK - 1)
            wp3[pl.ds(j * BLOCK, BLOCK), :] = pack3(jnp.where(seg == end_seg, jnp.exp2(end - cum) * dt, 0.0))
            wb3[pl.ds(j * BLOCK, BLOCK), :] = pack3(jnp.where(seg == prev_seg, jnp.exp2(cum), 0.0))
            keeps.append(jnp.where(prev_seg == end_seg, jnp.exp2(end), 0.0))
            b_rows = bcc[pl.ds(j * BLOCK, BLOCK), 0:STATE]
            c_rows = bcc[pl.ds(j * BLOCK, BLOCK), STATE : 2 * STATE]
            b_t = b_rows.astype(F32).T.astype(BF16)
            bt[j] = b_t
            scores = mm(c_rows, b_t)
            same = seg_vec(s_ref, row + j * BLOCK) == seg_vec(s_ref, col + j * BLOCK)
            gm[j] = jnp.where((row >= col) & same, scores, 0.0)
            cum_t[j] = cum.T
            dt_t[j] = dt.T
            here = cut_block == j
            cut_keep = jnp.where(here & (cut_seg == prev_seg), jnp.exp2(cut_row), cut_keep)
            cut_reach = jnp.where(here & (cut_seg == before), jnp.exp2(total + cut_row), cut_reach)

            @pl.when((cut >= 0) & here)
            def _():
                chosen = (seg == cut_seg) & (pos + j * BLOCK <= cut)
                wf3[...] = pack3(jnp.where(chosen, jnp.exp2(jnp.minimum(cut_row - cum, 0.0)) * dt, 0.0))

            total = total + end
        keep3[...] = pack3(rows_of(keeps + [cut_keep, cut_reach], 16, LANES))
        core, upper = s_ref[0], s_ref[2]
        for top in range(2):
            for source in range(CORES):
                near = jnp.where(core == source, near_same[...], near_cross[...])
                far = jnp.where(core == source, far_same[...], far_cross[...])
                value = jnp.where(upper == top, near, far).astype(F32)
                for step in range(STEPS):
                    at = 32 * top + 8 * step + ROWS * source
                    dec_rows[at : at + ROWS, :] = value[ROWS * step : ROWS * step + ROWS, :]

    spread = spread_matrix(chunk)
    keep = mm(keep3[...], spread)
    half_lane = lax.broadcasted_iota(jnp.int32, (BLOCK, LANES), 1) < HEAD_DIM
    for index, out in enumerate(outs):

        @pl.when(m == base + index)
        def _():
            out[0:STATE] = jnp.zeros((STATE, CHUNK), BF16)
            row = lax.broadcasted_iota(jnp.int32, (16, CHUNK), 0)
            tile = cx[...].astype(F32)
            for part, value in enumerate(split3(keep[BLOCKS + 1 : BLOCKS + 2])):
                tile = jnp.where(row == 9 + part, value, tile)
            out[STATE : STATE + 16] = tile.astype(BF16)
            out[STATE + 16 : STATE + 32] = cg[...]
            at = pl.multiple_of(chunk * CHUNK, CHUNK)
            out[DEC : DEC + 64] = dec_rows[:, pl.ds(at, CHUNK)].astype(BF16)
            out[DEC + 64 : DEC + 128] = dec_rows[:, GROUP_CH : GROUP_CH + 512].astype(BF16)
            for part in range(4):
                steps = dec_rows[16 * part : 16 * part + 16, GROUP_CH + 512 : GROUP_CH + 640]
                out[DEC + 128 : DEC + 144, part * LANES : (part + 1) * LANES] = steps.astype(BF16)

    state = None
    pairs = CHUNK // LANES
    heads = chunk * (CHUNK // HEAD_DIM)
    heads_tile = pl.ds(pl.multiple_of(heads, 8), 8)
    for j in range(BLOCKS):
        rows = slice(j * BLOCK, (j + 1) * BLOCK)
        if j > 0:
            high = state.astype(BF16)
            parts[0:STATE] = high
            parts[STATE:] = (state - high.astype(F32)).astype(BF16)
            c_rows = bcc[rows, STATE : 2 * STATE]
            carried[...] = mm(jnp.concatenate([c_rows, c_rows], axis=1), parts[...])
            reach[...] = mm(wb3[rows], spread)

        @pl.when((cut >= 0) & (cut_block == j))
        def _():
            wide[...] = mm(wf3[...], spread)
            fresh = mm(bt[j], (xc_ref[rows].astype(F32) * wide[...]).astype(BF16))
            if j > 0:
                fresh = keep[BLOCKS : BLOCKS + 1] * state + fresh
            for index, out in enumerate(outs):

                @pl.when(m == base + index)
                def _():
                    out[0:STATE] = fresh.astype(BF16)

        if j < BLOCKS - 1:
            wide[...] = mm(wp3[rows], spread)
            for pair in range(pairs):
                lanes = slice(pair * LANES, (pair + 1) * LANES)
                scaled[:, lanes] = (xc_ref[rows, lanes].astype(F32) * wide[:, lanes]).astype(BF16)
            fresh = mm(bt[j], scaled[...])
            state = fresh if j == 0 else keep[j : j + 1] * state + fresh
        cum = dtc[CHIP_TOKENS + j * BLOCK : CHIP_TOKENS + (j + 1) * BLOCK]
        turned = pltpu.roll(cum, LANES - heads, 1)
        cum_rows = cum_t[j, heads_tile, :]
        dt_rows = dt_t[j, heads_tile, :]
        for pair in range(pairs):
            weights = []
            for head in (2 * pair, 2 * pair + 1):
                gap = jnp.minimum(turned[:, head : head + 1] - cum_rows[head : head + 1], 0.0)
                weights.append((jnp.exp2(gap) * (gm[j] * dt_rows[head : head + 1])).astype(BF16))
            lanes = slice(pair * LANES, (pair + 1) * LANES)
            two = xc_ref[rows, lanes]
            zero = jnp.zeros_like(two)
            stacked = jnp.concatenate([jnp.where(half_lane, two, zero), jnp.where(half_lane, zero, two)], axis=0)
            value = mm(jnp.concatenate(weights, axis=1), stacked) + skip[:, lanes] * two.astype(F32)
            if j > 0:
                value = value + reach[:, lanes] * carried[:, lanes]
            local_out[rows, lanes] = value


def run_b(scalars, xc, bcc, dtc, skip, cx, cg, dec_hops, base, count, local=None):
    def fixed(shape):
        return pl.BlockSpec(shape, lambda m, s: (0,) * len(shape))

    def chunked(rows, per_core=0):
        return pl.BlockSpec((rows, CHUNK), lambda m, s: (0, s[0] * per_core + (s[1] ^ (m + base))))

    args = [scalars, xc, bcc, dtc, skip, cx, cg, *dec_hops]
    in_specs = [
        chunked(CHIP_TOKENS), fixed((CHIP_TOKENS, 512)), fixed((2 * CHIP_TOKENS, LANES)),
        chunked(1, RING), chunked(16), fixed((16, 512)),
    ] + [fixed((16, WIDE))] * 4
    aliases = {}
    if local is not None:
        aliases = {len(args): count}
        args.append(local)
        in_specs.append(pl.BlockSpec(memory_space=pl.ANY))
    scratch = [
        pltpu.VMEM((CHIP_TOKENS, LANES), BF16),
        pltpu.VMEM((CHIP_TOKENS, LANES), BF16),
        pltpu.VMEM((16, LANES), BF16),
        pltpu.VMEM((BLOCKS, STATE, BLOCK), BF16),
        pltpu.VMEM((BLOCKS, BLOCK, BLOCK), F32),
        pltpu.VMEM((BLOCKS, LANES, BLOCK), F32),
        pltpu.VMEM((BLOCKS, LANES, BLOCK), F32),
        pltpu.VMEM((BLOCK, LANES), BF16),
        pltpu.VMEM((BLOCK, CHUNK), F32),
        pltpu.VMEM((BLOCK, CHUNK), F32),
        pltpu.VMEM((BLOCK, CHUNK), F32),
        pltpu.VMEM((BLOCK, CHUNK), BF16),
        pltpu.VMEM((2 * STATE, CHUNK), BF16),
        pltpu.VMEM((64, WIDE), F32),
    ]
    assert len(scratch) == SCRATCH_B
    return pl.pallas_call(
        functools.partial(kernel_b, base, count),
        grid_spec=pltpu.PrefetchScalarGridSpec(
            num_scalar_prefetch=1,
            grid=(count,),
            in_specs=in_specs,
            out_specs=[fixed((MSG, CHUNK))] * count + [chunked(CHIP_TOKENS)],
            scratch_shapes=scratch,
        ),
        out_shape=[jax.ShapeDtypeStruct((MSG, CHUNK), BF16)] * count + [pltpu.HBM((CHIP_TOKENS, GROUP_CH), F32)],
        input_output_aliases=aliases,
        compiler_params=pltpu.CompilerParams(vmem_limit_bytes=14 * MIB),
        cost_estimate=pl.CostEstimate(
            flops=3 * count * 10**9, bytes_accessed=2 * count * 10**6, transcendentals=count * 10**5
        ),
        name=f"output_within_chip_{base}",
    )(*args)


def pick(refs, which, rows):
    out = refs[0][rows]
    for index in range(1, len(refs)):
        out = jnp.where(which == index, refs[index][rows], out)
    return out.astype(F32)


def decay_rows(tile):
    return tile[0:1] + tile[1:2] + tile[2:3]


def kernel_total(s_ref, l0, l1, l2, l3, total_out):
    state = jnp.zeros((STATE, CHUNK), F32)
    for chip in range(RING):
        which = s_ref[1] ^ chip
        part = pick((l0, l1, l2, l3), which, slice(0, STATE))
        factor = decay_rows(pick((l0, l1, l2, l3), which, slice(STATE, STATE + 16)))
        state = factor * state + part
    total_out[...] = state.astype(BF16)


def kernel_starts(s_ref, l0, l1, l2, l3, start, r0, r1, r2, r3):
    state = start[...].astype(F32)
    for chip in range(RING):
        which = s_ref[1] ^ chip
        for index, out in enumerate((r0, r1, r2, r3)):

            @pl.when(which == index)
            def _():
                out[...] = state.astype(BF16)

        if chip < RING - 1:
            part = pick((l0, l1, l2, l3), which, slice(0, STATE))
            factor = decay_rows(pick((l0, l1, l2, l3), which, slice(STATE, STATE + 16)))
            state = factor * state + part


def whole_call(kernel, out_shape, name, flops, scratch=()):
    def run(scalars, *args):
        return pl.pallas_call(
            kernel,
            in_specs=[pl.BlockSpec(memory_space=pltpu.SMEM)] + [pl.BlockSpec(memory_space=pltpu.VMEM)] * len(args),
            out_specs=jax.tree.map(lambda _: pl.BlockSpec(memory_space=pltpu.VMEM), out_shape),
            out_shape=out_shape,
            scratch_shapes=list(scratch),
            compiler_params=pltpu.CompilerParams(vmem_limit_bytes=8 * MIB),
            cost_estimate=pl.CostEstimate(flops=flops, bytes_accessed=3 * 10**6, transcendentals=0),
            name=name,
        )(scalars, *args)

    return run


def kernel_decode(
    s_ref, l0, l1, l2, l3, start, f0, f1, f2, f3,
    wx, bx, wg, bg, vecs, skip, bounds,
    keep_out, send_out,
    final, rows_f32, result,
):
    z, upper = s_ref[1], s_ref[2]
    ls, fs = (l0, l1, l2, l3), (f0, f1, f2, f3)
    first, second = bounds[0, 0], bounds[0, 0] + bounds[0, 1]
    lasts = [first - 1, second - 1, second + bounds[0, 2] - 1]
    final[...] = jnp.zeros_like(final)
    state = start[...].astype(F32)
    for chip in range(RING):
        which = z ^ chip
        origin = (upper * RING + chip) * CHIP_TOKENS
        part = pick(ls, which, slice(0, STATE))
        factor = decay_rows(pick(ls, which, slice(STATE, STATE + 16)))
        after = factor * state + part
        for q in range(PROMPTS):
            local = lasts[q] - origin

            @pl.when(local == CHIP_TOKENS - 1)
            def _():
                final[q] = after

            @pl.when((local >= 0) & (local < CHIP_TOKENS - 1))
            def _():
                fresh = pick(fs, which, slice(0, STATE))
                reach = decay_rows(pick(fs, which, slice(STATE, STATE + 16))[9:12])
                final[q] = fresh + reach * state

        state = after
    cache_x = sum(f[STATE : STATE + 16].astype(F32) for f in fs)
    cache_g = sum(f[STATE + 16 : STATE + 32].astype(F32) for f in fs)
    spread = spread_matrix(z)
    for index, f in enumerate(fs):
        rows_f32[index, :, 0:CHUNK] = f[DEC : DEC + 64].astype(F32)
        rows_f32[index, :, CHUNK : CHUNK + 512] = f[DEC + 64 : DEC + 128].astype(F32)
        for part in range(4):
            steps = f[DEC + 128 : DEC + 144, part * LANES : (part + 1) * LANES].astype(F32)
            rows_f32[index, 16 * part : 16 * part + 16, CHUNK + 512 :] = steps

    def step_rows(step, lanes):
        tiles = [
            rows_f32[index, 32 * side + 8 * step : 32 * side + 8 * step + 8, lanes]
            for index in range(RING)
            for side in range(2)
        ]
        return jnp.concatenate(tiles, axis=0)

    prompt = step_rows(0, slice(1024, 1152))[:, 96:97]
    chosen = [prompt == float(q) for q in range(PROMPTS)]
    mine = jnp.zeros_like(prompt)
    for q in range(PROMPTS):
        inside = jnp.where(lasts[q] // (RING * CHIP_TOKENS) == upper, 1.0, 0.0)
        mine = jnp.where(chosen[q], inside, mine)

    def window(cache, lanes):
        rows = []
        for tap in range(CONV - 1):
            row = jnp.zeros((STEPS * 16, CHUNK), F32)
            for q in range(PROMPTS):
                row = jnp.where(chosen[q], cache[3 * q + tap : 3 * q + tap + 1], row)
            rows.append(row)
        return rows + [step_rows(step, lanes) for step in range(STEPS)]

    def convolved(rows, weight, offset):
        out = []
        for step in range(STEPS):
            running = jnp.broadcast_to(offset, rows[0].shape)
            for tap in range(CONV):
                running = running + weight[tap : tap + 1] * rows[step + tap]
            out.append(silu(running).astype(BF16))
        return out

    mixed = convolved(window(cache_x, slice(0, 512)), wx[...].astype(F32), bx[...])
    both = convolved(window(cache_g, slice(512, 1024)), wg[...].astype(F32), bg[...])
    steps, fades = [], []
    fade = jnp.zeros((STEPS * 16, LANES), F32)
    for step in range(STEPS):
        dt = softplus(step_rows(step, slice(1024, 1152)) + vecs[0:1])
        fade = fade + dt * vecs[1:2]
        steps.append(dt)
        fades.append(fade)
    readers = jnp.concatenate([rows[:, STATE:] for rows in both], axis=0)
    readout = jnp.zeros((STEPS * STEPS * 16, CHUNK), F32)
    for q in range(PROMPTS):
        high = final[q].astype(BF16)
        low = (final[q] - high.astype(F32)).astype(BF16)
        value = mm(readers, high) + mm(readers, low)
        readout = jnp.where(jnp.concatenate([chosen[q]] * STEPS, axis=0), value, readout)
    for step in range(STEPS):
        mixed_now = mixed[step].astype(F32)
        total = readout[64 * step : 64 * step + 64] * mm(pack3(jnp.exp2(fades[step])), spread)
        total = total + skip[...] * mixed_now
        reader = both[step][:, STATE:].astype(F32)
        for past in range(step + 1):
            weight = steps[past]
            if past < step:
                weight = weight * jnp.exp2(fades[step] - fades[past])
            product = jnp.sum(reader * both[past][:, 0:STATE].astype(F32), axis=1, keepdims=True)
            total = total + mm(pack3(weight), spread) * (product * mixed[past].astype(F32))
        total = jnp.where(mine > 0.5, total, 0.0)
        for index in range(RING):
            for side in range(2):
                tile = total[8 * (2 * index + side) : 8 * (2 * index + side) + 8]
                result[index, 32 * side + 8 * step : 32 * side + 8 * step + 8, :] = tile
    for index in range(RING):
        keep_out[index] = result[index, pl.ds(pl.multiple_of(32 * upper, 32), 32), :].astype(BF16)
        send_out[index] = result[index, pl.ds(pl.multiple_of(32 * (1 - upper), 32), 32), :].astype(BF16)


def kernel_d(s_ref, local, c_rows, wc3, r0, r1, r2, r3, out):
    z = s_ref[1]
    block = (z >> 1) ^ pl.program_id(0)
    for side in range(2):
        chunk = 2 * block + side
        spread = spread_matrix(chunk)
        for index, r in enumerate((r0, r1, r2, r3)):

            @pl.when((chunk ^ z) == index)
            def _():
                for part in range(2):
                    lanes = slice(part * 256, (part + 1) * 256)
                    to = slice(side * CHUNK + part * 256, side * CHUNK + (part + 1) * 256)
                    factor = mm(wc3[...], spread[:, lanes])
                    out[:, to] = (local[:, to] + factor * mm(c_rows[...], r[:, lanes])).astype(BF16)


def run_d(scalars, local, bcc, wc3, starts, own):
    half = CHIP_TOKENS // 2

    def row(s):
        return s[0] if own else 1 - s[0]

    width = CORES * GROUP_CH if own else GROUP_CH
    return pl.pallas_call(
        kernel_d,
        grid_spec=pltpu.PrefetchScalarGridSpec(
            num_scalar_prefetch=1,
            grid=(2,),
            in_specs=[
                pl.BlockSpec((half, 2 * CHUNK), lambda m, s: (row(s), (s[1] >> 1) ^ m)),
                pl.BlockSpec((half, STATE), lambda m, s: (row(s), 1)),
                pl.BlockSpec((half, LANES), lambda m, s: (row(s), 0)),
            ] + [pl.BlockSpec((STATE, CHUNK), lambda m, s: (0, 0))] * RING,
            out_specs=pl.BlockSpec((half, 2 * CHUNK), lambda m, s: (0, (s[0] * 2 if own else 0) + ((s[1] >> 1) ^ m))),
        ),
        out_shape=jax.ShapeDtypeStruct((half, width), BF16),
        compiler_params=pltpu.CompilerParams(vmem_limit_bytes=12 * MIB),
        cost_estimate=pl.CostEstimate(flops=10**9, bytes_accessed=4 * 10**6, transcendentals=0),
        name="carried_own" if own else "carried_other",
    )(scalars, local, bcc, wc3, *starts)


def kernel_put(s_ref, part, whole, out):
    out[...] = part[...]


def put_group(scalars, whole, part):
    half = CHIP_TOKENS // 2
    return pl.pallas_call(
        kernel_put,
        grid_spec=pltpu.PrefetchScalarGridSpec(
            num_scalar_prefetch=1,
            grid=(2,),
            in_specs=[
                pl.BlockSpec((half, GROUP_CH // 2), lambda m, s: (0, m)),
                pl.BlockSpec(memory_space=pl.ANY),
            ],
            out_specs=pl.BlockSpec((half, GROUP_CH // 2), lambda m, s: (0, (1 - s[0]) * 2 + m)),
        ),
        out_shape=jax.ShapeDtypeStruct(whole.shape, BF16),
        input_output_aliases={2: 0},
        compiler_params=pltpu.CompilerParams(vmem_limit_bytes=4 * MIB),
        cost_estimate=pl.CostEstimate(flops=0, bytes_accessed=2 * 10**6, transcendentals=0),
        name="put_group",
    )(scalars, part, whole)


def head_copies(group):
    lane = lax.broadcasted_iota(jnp.int32, (64, LANES), 1)
    head = lax.broadcasted_iota(jnp.int32, (64, LANES), 0)
    hit = ((lane & (REP - 1)) + group * REP == head) & (lane < 3 * REP)
    return jnp.where(hit, 1.0, 0.0).astype(BF16)


def kernel_pack(s_ref, x, bc, dt_t, x_last, bc_last, dx, dbc, ddt, send, halo0, halo1, side, d_own, d_other, rows_f32):
    core = s_ref[0]
    first = core == 0
    rows = x.shape[0]
    start = pl.multiple_of(pl.program_id(0) * rows, rows)
    dt = dt_t[:, pl.ds(start, rows)].astype(F32).T.astype(BF16)
    b_rows, c_rows = bc[:, 0, :], bc[:, 1, :]
    send[:, 0:GROUP_CH] = x[...]
    for target, group, offset in ((send, 1 - core, GROUP_CH), (side, core, 0)):
        low = group == 0
        target[:, offset : offset + STATE] = jnp.where(low, b_rows[:, 0:STATE], b_rows[:, STATE:])
        target[:, offset + STATE : offset + 2 * STATE] = jnp.where(low, c_rows[:, 0:STATE], c_rows[:, STATE:])
        target[:, offset + 512 : offset + 640] = mm(dt, head_copies(group)).astype(BF16)
        target[:, offset + 640 : offset + 1024] = jnp.zeros((rows, 384), BF16)

    @pl.when(pl.program_id(0) == 0)
    def _():
        b_last, c_last = bc_last[:, 0, :], bc_last[:, 1, :]
        for group, halo in ((0, halo0), (1, halo1)):
            halo[:, 0:GROUP_CH] = x_last[:, group * GROUP_CH : (group + 1) * GROUP_CH]
            halo[:, GROUP_CH : GROUP_CH + STATE] = b_last[:, group * STATE : (group + 1) * STATE]
            halo[:, GROUP_CH + STATE : GROUP_CH + 512] = c_last[:, group * STATE : (group + 1) * STATE]
            halo[:, GROUP_CH + 512 :] = jnp.zeros((16, 512), BF16)
        lane = lax.broadcasted_iota(jnp.int32, (ROWS, LANES), 1)
        row = lax.broadcasted_iota(jnp.int32, (ROWS, LANES), 0)
        prompt = jnp.zeros((ROWS, LANES), F32)
        for r in range(ROWS):
            prompt = jnp.where(row == r, s_ref[1 + r].astype(F32), prompt)
        for out, group in ((d_own, core), (d_other, 1 - core)):
            low = group == 0
            rows_f32[...] = jnp.zeros_like(rows_f32)
            for step in range(STEPS):
                at = slice(ROWS * step, ROWS * step + ROWS)
                value = dx[step].astype(F32)
                rows_f32[at, 0:GROUP_CH] = jnp.where(low, value[:, 0:GROUP_CH], value[:, GROUP_CH:])
                for part in range(2):
                    value = dbc[step, :, part, :].astype(F32)
                    to = GROUP_CH + part * STATE
                    rows_f32[at, to : to + STATE] = jnp.where(low, value[:, 0:STATE], value[:, STATE:])
                steps = mm(ddt[step], head_copies(group))
                rows_f32[at, GROUP_CH + 512 : GROUP_CH + 640] = jnp.where(lane < 3 * REP, steps, prompt)
            out[...] = rows_f32[...].astype(BF16)


def run_pack(scalars, x, bc, dt_t, dx, dbc, ddt):
    rows = x.shape[0]
    tile = rows // 2
    last = rows // 16 - 1
    small = (16, WIDE)

    def fixed(shape):
        return pl.BlockSpec(shape, lambda i, s: (0,) * len(shape))

    return pl.pallas_call(
        kernel_pack,
        grid_spec=pltpu.PrefetchScalarGridSpec(
            num_scalar_prefetch=1,
            grid=(2,),
            in_specs=[
                pl.BlockSpec((tile, GROUP_CH), lambda i, s: (i, 1 - s[0])),
                pl.BlockSpec((tile, 2, 512), lambda i, s: (i, 0, 0)),
                fixed(dt_t.shape),
                pl.BlockSpec((16, CORES * GROUP_CH), lambda i, s: (last, 0)),
                pl.BlockSpec((16, 2, 512), lambda i, s: (last, 0, 0)),
                fixed(dx.shape),
                fixed(dbc.shape),
                fixed(ddt.shape),
            ],
            out_specs=[
                pl.BlockSpec((tile, WIDE), lambda i, s: (i, 0)),
                fixed(small),
                fixed(small),
                pl.BlockSpec((tile, 1024), lambda i, s: (i, 0)),
                fixed(small),
                fixed(small),
            ],
            scratch_shapes=[pltpu.VMEM(small, F32)],
        ),
        out_shape=[pltpu.HBM(shape, BF16) for shape in ((rows, WIDE), small, small, (rows, 1024), small, small)],
        compiler_params=pltpu.CompilerParams(vmem_limit_bytes=12 * MIB),
        cost_estimate=pl.CostEstimate(flops=10**6, bytes_accessed=4 * 10**6, transcendentals=0),
        name="pack",
    )(scalars, x, bc, dt_t, x, bc, dx, dbc, ddt)


def on_device(
    x_in, bc_in, dt_raw, conv_w_x, conv_b_x, conv_w_bc, conv_b_bc, dt_bias, a_log, d_skip,
    lengths, decode_prompt, dec_x, dec_bc, dec_dt,
):
    count = lax.axis_size("dp")
    place = lax.axis_index("dp")
    core = place % CORES
    z = (place // CORES) % RING
    upper = place // (CORES * RING)
    anchor = (place // CORES) * CHIP_TOKENS
    bounds = (lengths[0, 0], lengths[0, 0] + lengths[0, 1])
    zero = jnp.int32(0)
    scalars = jnp.stack([core, z, upper, anchor, bounds[0] - anchor, bounds[1] - anchor, zero, zero]).astype(jnp.int32)
    both = ("pool", "dp")

    x_rows, bc_rows = in_hbm(x_in[0]), in_hbm(bc_in[0])
    own = jnp.concatenate([core[None], decode_prompt[0, 0]]).astype(jnp.int32)
    packed, halo0, halo1, g_own, d_own, d_other = run_pack(
        own, x_rows, bc_rows, in_hbm(dt_raw[0].T), in_hbm(dec_x[0, 0]), in_hbm(dec_bc[0, 0]), in_hbm(dec_dt[0, 0])
    )
    recv = in_hbm(lax.ppermute(packed, "dp", [(i, i ^ 1) for i in range(count)]))
    g_own = in_hbm(g_own)
    halo = lax.ppermute(halo0, "dp", [(i, i + 1) for i in range(1, count - 1, 2)])
    halo = halo + lax.ppermute(halo1, "dp", [(i, i + 2) for i in range(1, count - 1, 2)])

    def after(value, other):
        return lax.optimization_barrier((value, other))[0]

    dec_rows = STEPS * ROWS
    total = 2 * count

    def hop(value, flip):
        return lax.ppermute(value, both, [(i, ((i + count) % total) ^ flip) for i in range(total)])

    def z_swap(value, m):
        if m == 0:
            return value
        return lax.ppermute(value, "dp", [(i, i ^ (CORES * m)) for i in range(count)])

    def z_swaps(values):
        order = (0, 2, 1, 3)
        moved = {m: z_swap(values[m], m) for m in order}
        return [moved[m] for m in range(RING)]

    dec_hops = [hop(d_own, 0), hop(d_other, 1), hop(d_own, CORES * RING), hop(d_other, CORES * RING + 1)]

    w_group = lax.dynamic_slice_in_dim(conv_w_bc, core * STATE, STATE, 2).reshape(CONV, 2 * STATE)
    b_group = lax.dynamic_slice_in_dim(conv_b_bc, core * STATE, STATE, 1).reshape(1, 2 * STATE)
    rates = -LOG2E * jnp.exp(a_log)
    heads = jnp.stack([dt_bias, rates])
    heads = lax.dynamic_slice_in_dim(heads, core * REP, REP, 1)
    vecs = jnp.pad(jnp.tile(heads, (1, 3)), ((0, 6), (0, LANES - 3 * REP)))
    skip = jnp.repeat(d_skip, HEAD_DIM)[None]
    b_x = conv_b_x[None]

    *ls, xc, bcc, dtc, wc3, cx, cg = run_a(scalars, x_rows, recv, halo, conv_w_x, b_x, g_own, w_group, b_group, vecs)
    sent_ls = z_swaps(ls)
    *fs, local = run_b(scalars, xc, bcc, dtc, skip, cx, cg, dec_hops, 1, 3)
    ls = after(tuple(sent_ls), fs[0])
    state_shape = jax.ShapeDtypeStruct((STATE, CHUNK), BF16)
    half_total = whole_call(kernel_total, state_shape, "half_total", 10**6)(scalars, *ls)
    own_end, local = run_b(scalars, xc, bcc, dtc, skip, cx, cg, after(tuple(dec_hops), half_total), 0, 1, in_hbm(local))
    fs = z_swaps([own_end, *fs])
    local = in_hbm(local)
    start = lax.ppermute(half_total, "dp", [(i, i + CORES * RING) for i in range(CORES * RING)])
    starts = whole_call(kernel_starts, [state_shape] * RING, "chip_starts", 10**6)(scalars, *ls, start)
    starts = z_swaps(starts)

    def own_columns(value):
        return lax.dynamic_slice_in_dim(value, core * GROUP_CH + z * CHUNK, CHUNK, 1)

    def decode(bounds_ref_args):
        shape = jax.ShapeDtypeStruct((RING, 32, CHUNK), BF16)
        args = [*ls, start, *fs, own_columns(conv_w_x), own_columns(b_x), w_group, b_group, vecs, own_columns(skip)]
        return pl.pallas_call(
            kernel_decode,
            in_specs=[pl.BlockSpec(memory_space=pltpu.SMEM)]
            + [pl.BlockSpec(memory_space=pltpu.VMEM)] * len(args)
            + [pl.BlockSpec(memory_space=pltpu.SMEM)],
            out_specs=[pl.BlockSpec(memory_space=pltpu.VMEM)] * 2,
            out_shape=[shape, shape],
            scratch_shapes=[
                pltpu.VMEM((PROMPTS, STATE, CHUNK), F32),
                pltpu.VMEM((RING, 64, 1152), F32),
                pltpu.VMEM((RING, 64, CHUNK), F32),
            ],
            compiler_params=pltpu.CompilerParams(vmem_limit_bytes=14 * MIB),
            cost_estimate=pl.CostEstimate(flops=20 * 10**9, bytes_accessed=6 * 10**6, transcendentals=0),
            name="decode_rows",
        )(scalars, *args, bounds_ref_args)

    kept, sent = after(tuple(decode(lengths.astype(jnp.int32))), starts[1])
    other_rows = run_d(scalars, local, bcc, wc3, starts, False)
    other_group = lax.ppermute(other_rows, "dp", [(i, i ^ 1) for i in range(count)])
    crossed = lax.ppermute(sent, both, [(i, ((i + count) % total) ^ (CORES * RING)) for i in range(total)])
    straight = lax.ppermute(kept, both, [(i, (i + count) % total) for i in range(total)])
    answers = after(straight + crossed, other_rows)
    answers = z_swaps([answers[m] for m in range(RING)])
    own_group = run_d(scalars, local, bcc, wc3, starts, True)
    answers = after(tuple(answers), own_group)
    columns = [
        functools.reduce(lambda a, m: jnp.where(z == j ^ m, answers[m], a), range(1, RING), answers[0])
        for j in range(RING)
    ]
    answers = jnp.concatenate(columns, axis=1).reshape(STEPS, CORES, ROWS, GROUP_CH)
    first, second = (answers[:, i].reshape(dec_rows, GROUP_CH) for i in range(CORES))
    mine = jnp.where(core == 0, first, second)
    theirs = lax.ppermute(jnp.where(core == 0, second, first), "dp", [(i, i ^ 1) for i in range(count)])
    out = put_group(scalars, own_group, other_group)
    theirs = after(theirs, out)
    decoded = jnp.where(core == 0, jnp.concatenate([mine, theirs], axis=1), jnp.concatenate([theirs, mine], axis=1))
    return out[None], decoded.reshape(dec_x.shape)


def solution(mesh):
    in_specs = (
        P("pool", "dp", "tp"),
        P("pool", "dp", None, "tp"),
        P("pool", "dp", "tp"),
        P(None, "tp"),
        P("tp"),
        P(None, None, "tp"),
        P(None, "tp"),
        P("tp"),
        P("tp"),
        P("tp"),
        P("pool", None),
        P("pool", "dp", None),
        P("pool", "dp", None, None, "tp"),
        P("pool", "dp", None, None, None, "tp"),
        P("pool", "dp", None, None, "tp"),
    )
    out_specs = (P("pool", "dp", "tp"), P("pool", "dp", None, None, "tp"))
    return jax.shard_map(on_device, mesh=mesh, in_specs=in_specs, out_specs=out_specs, check_vma=False)
```
